32 devices in a mesh: dp: 8 (over z, x), tensor: 4 (over y, core).
Axes of the slice: x: 2, y: 2, z: 4, core: 2. Of those that a mesh axis runs over, the one named last changes fastest.
Arguments:
- gate_pre: bfloat16 [2048, 12800], P('dp', 'tensor'), may hold values from -6 to 6
- up_pre: bfloat16 [2048, 12800], P('dp', 'tensor'), may hold values from -6 to 6
- down_codes: bfloat16 [12800, 2560], P(('tensor', 'dp')), may hold values from -127 to 127
- down_scales: float32 [12800, 10], P(('tensor', 'dp')), may hold values from 4e-05 to 0.00024
- cotangent: bfloat16 [2048, 2560], P(('dp', 'tensor')), may hold values from -6 to 6
Outputs:
- layer_out: bfloat16 [2048, 2560], P(('dp', 'tensor'))
- gate_grad: bfloat16 [2048, 12800], P('dp', 'tensor')
- up_grad: bfloat16 [2048, 12800], P('dp', 'tensor')
- weight_grad: float32 [12800, 2560], P(('tensor', 'dp'))
The draws below stay inside these ranges and needn't reach their ends.
All inputs are finite; a program needn't handle non-finite values.
Results may differ from the reference program's by a relative error of at most 0.022.
Values may be sent and summed in bfloat16 or wider, within the bound.
No kernel may reach another device: no remote copies, remote signals or barrier semaphores. Data moves between devices by JAX's collectives and lax.ppermute only.
A program may use at most 192 MiB of HBM per device.

```python
import math
import jax
import jax.numpy as jnp
from jax import lax

D = 2560
FF = 12800
BLOCK = 256
TOKENS = 2048
N_DP = 8


def block_levels(key, dims, split, smallest, high):
    factor_of, own = 1.0, jax.random.fold_in(key, 6)
    for dim, blocks in split:
        heights = jnp.exp(jax.random.uniform(jax.random.fold_in(own, dim), (blocks,), jnp.float32, smallest / len(split), high / len(split)))
        factor_of = factor_of * jnp.repeat(heights, dims[dim] // blocks).reshape([-1 if axis == dim else 1 for axis in range(len(dims))])
    return factor_of


def scatter_about(key, shape, scale, limit, shards=(), kind=jnp.bfloat16):
    loudness = block_levels(key, shape, shards, -0.22, 0.18) if shards else 1.0
    values = jax.random.normal(key, shape, jnp.float32) * scale * loudness
    return jnp.minimum(jnp.maximum(values, -limit), limit).astype(kind)


def setup_inputs(seed: int = 0) -> dict:
    seeds = jax.random.split(jax.random.key(seed), 6)
    return {
        "gate_pre": scatter_about(seeds[0], (TOKENS, FF), 1.5, 6.0, ((0, 8), (1, 4))),
        "up_pre": scatter_about(seeds[1], (TOKENS, FF), 1.0, 6.0, ((0, 8), (1, 4))),
        "down_codes": jnp.clip(jax.random.uniform(seeds[2], (FF, D), jnp.float32, -127.0, 127.0) * block_levels(seeds[2], (FF, D), ((0, 32),), -0.4, 0.0), -127.0, 127.0).astype(jnp.bfloat16),
        "down_scales": jnp.clip(jnp.exp(math.log(0.00024) - 1.7917595 * jax.random.uniform(seeds[3], (FF, D // BLOCK), jnp.float32) ** block_levels(seeds[3], (FF, D // BLOCK), ((0, 32),), -0.2, 0.2)), 3.9999998989515007e-05, 0.00024),
        "cotangent": scatter_about(seeds[4], (TOKENS, D), 1.0, 6.0, ((0, 32),)),
    }


def silu_parts(gate_value):
    sigmoid_gate = jax.nn.sigmoid(gate_value)
    return gate_value * sigmoid_gate, sigmoid_gate


def dequantize(code_block, scales):
    row_count, full_width = code_block.shape
    nblocks = scales.shape[1]
    blocks = code_block.astype(jnp.float32).reshape(row_count, nblocks, full_width // nblocks) * scales[:, :, None]
    return blocks.reshape(row_count, full_width).astype(jnp.bfloat16)


def reference(gate_pre, up_pre, down_codes, down_scales, cotangent):
    weight = dequantize(down_codes, down_scales)
    hidden_rows, full_width = weight.shape
    nblocks = down_scales.shape[1]
    group_rows = gate_pre.shape[0] // N_DP

    def group_step(running, pieces):
        gate_piece, up_piece, back_piece = pieces
        gate_value = gate_piece.astype(jnp.float32)
        up_value = up_piece.astype(jnp.float32)
        activated, sigmoid_gate = silu_parts(gate_value)
        hidden = (activated * up_value).astype(jnp.bfloat16)
        layer_rows = jnp.dot(hidden, weight, preferred_element_type=jnp.float32).astype(jnp.bfloat16)
        dhidden = jnp.dot(back_piece, weight.T, preferred_element_type=jnp.float32)
        gate_rows = (dhidden * up_value * sigmoid_gate * (1.0 + gate_value * (1.0 - sigmoid_gate))).astype(jnp.bfloat16)
        up_rows = (dhidden * activated).astype(jnp.bfloat16)
        partial_value = jnp.dot(hidden.T, back_piece, preferred_element_type=jnp.float32)
        blocks = partial_value.reshape(hidden_rows, nblocks, full_width // nblocks)
        scale_rows = (jnp.max(jnp.abs(blocks), axis=2) + 1e-6) / 127.0
        grad_codes = (blocks / scale_rows[:, :, None]).astype(jnp.bfloat16)
        running = running + grad_codes.astype(jnp.float32) * scale_rows[:, :, None]
        return running, (layer_rows, gate_rows, up_rows)

    pieces = (gate_pre.reshape(N_DP, group_rows, hidden_rows),
              up_pre.reshape(N_DP, group_rows, hidden_rows),
              cotangent.reshape(N_DP, group_rows, full_width))
    start_sum = jnp.zeros((hidden_rows, nblocks, full_width // nblocks), jnp.float32)
    running, (layer_rows, gate_rows, up_rows) = lax.scan(group_step, start_sum, pieces)
    weight_grad = running.reshape(hidden_rows, full_width) * (TOKENS ** -0.5)
    layer_out = layer_rows.reshape(-1, full_width)
    gate_grad = gate_rows.reshape(-1, hidden_rows)
    up_grad = up_rows.reshape(-1, hidden_rows)
    return layer_out, gate_grad, up_grad, weight_grad
```

```python
import jax
import jax.numpy as jnp
from jax import lax
from jax.sharding import Mesh, PartitionSpec as P


def dequantize(codes, scales):
    rows, width = codes.shape
    nblocks = scales.shape[1]
    blocks = codes.astype(jnp.float32).reshape(rows, nblocks, width // nblocks) * scales[:, :, None]
    return blocks.reshape(rows, width).astype(jnp.bfloat16)


def swap(value, axis):
    return lax.ppermute(value, axis, [(0, 1), (1, 0)])


def gather_pair(value, axis):
    if lax.axis_size(axis) != 2:
        return lax.all_gather(value, axis, axis=0)
    other = swap(value, axis)
    first = lax.axis_index(axis) == 0
    return jnp.stack([jnp.where(first, value, other), jnp.where(first, other, value)])


def scatter_sum(parts, axis):
    size = lax.axis_size(axis)
    if size == 1:
        return parts[0].astype(jnp.float32)
    if size != 2:
        received = lax.all_to_all(parts.astype(jnp.bfloat16), axis, 0, 0, tiled=True)
        return jnp.sum(received.astype(jnp.float32), axis=0)
    me = lax.axis_index(axis)
    theirs = lax.dynamic_index_in_dim(parts, 1 - me, 0, keepdims=False).astype(jnp.bfloat16)
    mine = lax.dynamic_index_in_dim(parts, me, 0, keepdims=False)
    return mine.astype(jnp.float32) + swap(theirs, axis).astype(jnp.float32)


def body(gate_pre, up_pre, down_codes, down_scales, cotangent):
    group_rows, local_hidden = gate_pre.shape
    owned, width = down_codes.shape
    nz, nx, ny, nc = (lax.axis_size(name) for name in ("z", "x", "y", "c"))
    rows = cotangent.shape[0]
    units = nx * owned
    total_tokens = group_rows * nz * nx

    gate_value = gate_pre.astype(jnp.float32)
    up_value = up_pre.astype(jnp.float32)
    sigmoid_gate = jax.nn.sigmoid(gate_value)
    activated = gate_value * sigmoid_gate
    hidden = (activated * up_value).astype(jnp.bfloat16)

    sent = hidden.T.reshape(nz, units, group_rows)
    columns = lax.all_to_all(sent, "z", 0, 0, tiled=True) if nz > 1 else sent

    line = lax.all_gather(cotangent, ("z", "y"), axis=0)
    both = gather_pair(line, "c")
    received = jnp.moveaxis(both, 0, 1).reshape(nz, group_rows, width)

    weight = gather_pair(dequantize(down_codes, down_scales), "x").reshape(units, width)

    partial_out = lax.dot_general(
        columns, weight, (((1,), (0,)), ((), ())), preferred_element_type=jnp.float32
    ).astype(jnp.bfloat16)
    partial_out = partial_out.reshape(nz, ny, nc, rows, width)
    over_c = scatter_sum(jnp.moveaxis(partial_out, 2, 0), "c")
    over_y = scatter_sum(jnp.moveaxis(over_c.astype(jnp.bfloat16), 1, 0), "y")
    layer_out = scatter_sum(over_y.astype(jnp.bfloat16), "z").astype(jnp.bfloat16)

    dcolumns = lax.dot_general(
        weight, received, (((1,), (2,)), ((), ())), preferred_element_type=jnp.float32
    ).astype(jnp.bfloat16)
    dcolumns = jnp.moveaxis(dcolumns, 1, 0)
    back = lax.all_to_all(dcolumns, "z", 0, 0, tiled=True) if nz > 1 else dcolumns
    dhidden = back.reshape(local_hidden, group_rows).T.astype(jnp.float32)
    gate_grad = (
        dhidden * up_value * sigmoid_gate * (1.0 + gate_value * (1.0 - sigmoid_gate))
    ).astype(jnp.bfloat16)
    up_grad = (dhidden * activated).astype(jnp.bfloat16)

    partial_grad = lax.dot_general(
        columns, received, (((0, 2), (0, 1)), ((), ())), preferred_element_type=jnp.float32
    )
    weight_grad = scatter_sum(partial_grad.reshape(nx, owned, width), "x") * float(total_tokens) ** (-0.5)
    return layer_out, gate_grad, up_grad, weight_grad


def outer_split(mesh, tokens, hidden, width):
    dp, tensor = mesh.shape["dp"], mesh.shape["tensor"]

    def rows_sent(nz):
        moved = 2 * (tokens // dp) * (hidden // tensor) / width if nz > 1 else 0
        return 2 * hidden // (tensor * nz) + 2 * tokens * nz // dp + moved

    return min((nz for nz in range(1, dp + 1) if dp % nz == 0), key=rows_sent)


def solution(mesh):
    def call(gate_pre, up_pre, down_codes, down_scales, cotangent):
        tokens, hidden = gate_pre.shape
        nz = outer_split(mesh, tokens, hidden, cotangent.shape[1])
        dp, tensor = mesh.shape["dp"], mesh.shape["tensor"]
        fine = Mesh(mesh.devices.reshape(nz, dp // nz, tensor // 2, 2), ("z", "x", "y", "c"))
        act = P(("z", "x"), ("y", "c"))
        weight = P(("y", "c", "z", "x"), None)
        layer = P(("z", "x", "y", "c"), None)
        return jax.shard_map(
            body,
            mesh=fine,
            in_specs=(act, act, weight, weight, layer),
            out_specs=(layer, act, act, weight),
            check_vma=False,
        )(gate_pre, up_pre, down_codes, down_scales, cotangent)

    return call
```

```python
import functools

import jax
import jax.numpy as jnp
from jax import lax
from jax.experimental import pallas as pl
from jax.experimental.pallas import tpu as pltpu
from jax.sharding import Mesh, PartitionSpec as P

VMEM_BYTES = 48 * 2**20


def dequantize(codes, scales):
    rows, width = codes.shape
    nblocks = scales.shape[1]
    blocks = codes.astype(jnp.float32).reshape(rows, nblocks, width // nblocks) * scales[:, :, None]
    return blocks.reshape(rows, width).astype(jnp.bfloat16)


def swap(value, axis):
    return lax.ppermute(value, axis, [(0, 1), (1, 0)])


def gather_pair(value, axis):
    if lax.axis_size(axis) != 2:
        return lax.all_gather(value, axis, axis=0)
    other = swap(value, axis)
    first = lax.axis_index(axis) == 0
    return jnp.stack([jnp.where(first, value, other), jnp.where(first, other, value)])


def scatter_sum(parts, axis):
    size = lax.axis_size(axis)
    if size == 1:
        return parts[0].astype(jnp.float32)
    if size != 2:
        received = lax.all_to_all(parts.astype(jnp.bfloat16), axis, 0, 0, tiled=True)
        return jnp.sum(received.astype(jnp.float32), axis=0)
    me = lax.axis_index(axis)
    theirs = lax.dynamic_index_in_dim(parts, 1 - me, 0, keepdims=False).astype(jnp.bfloat16)
    mine = lax.dynamic_index_in_dim(parts, me, 0, keepdims=False)
    return mine.astype(jnp.float32) + swap(theirs, axis).astype(jnp.float32)


def exchange(value, axis, offset):
    size = lax.axis_size(axis)
    return lax.ppermute(value, axis, [(i, i ^ offset) for i in range(size)])


def call_kernel(kernel, place, inputs, in_specs, out_shapes, out_specs, grid, scratch, cost):
    flops, nbytes, transcendentals = cost
    return pl.pallas_call(
        kernel,
        out_shape=out_shapes,
        grid_spec=pltpu.PrefetchScalarGridSpec(
            num_scalar_prefetch=1,
            grid=grid,
            in_specs=in_specs,
            out_specs=out_specs,
            scratch_shapes=scratch,
        ),
        compiler_params=pltpu.CompilerParams(vmem_limit_bytes=VMEM_BYTES),
        cost_estimate=pl.CostEstimate(
            flops=flops, bytes_accessed=nbytes, transcendentals=transcendentals
        ),
    )(place, *inputs)


def whole(shape):
    return pl.BlockSpec(shape, lambda i, place: (0,) * len(shape))


def dequantize_kernel(place, codes, scales, weight):
    span = codes.shape[1] // scales.shape[1]
    for block in range(scales.shape[1]):
        cols = slice(block * span, (block + 1) * span)
        value = codes[:, cols].astype(jnp.float32) * scales[:, block : block + 1]
        weight[:, cols] = value.astype(jnp.bfloat16)


def hidden_kernel(nz, units, place, gate, up, *refs):
    outs, rows = refs[:nz], refs[nz]
    step = pl.program_id(0)
    span = gate.shape[1]
    value = gate[...].astype(jnp.float32)
    hidden = value * jax.nn.sigmoid(value) * up[...].astype(jnp.float32)
    rows[pl.ds(pl.multiple_of(step * span, 128), span), :] = hidden.astype(jnp.bfloat16).T

    @pl.when(step == pl.num_programs(0) - 1)
    def _():
        half = units // 2
        for k in range(nz):
            for r in range(2):
                start = (place[0] ^ k) * units + (place[1] ^ r) * half
                outs[k][r * half : (r + 1) * half, :] = rows[
                    pl.ds(pl.multiple_of(start, 16), half), :
                ]


def layer_rows(place, r, s, rows):
    return pl.multiple_of(((place[2] ^ r) * 2 + (place[3] ^ s)) * rows, 16)


def dhidden_kernel(nz, place, own, other, c00, c10, c01, c11, *refs):
    outs, tokens = refs[:nz], refs[nz]
    step = pl.program_id(0)
    rows = c00.shape[1]
    for (r, s), piece in (((0, 0), c00), ((1, 0), c10), ((0, 1), c01), ((1, 1), c11)):
        tokens[pl.ds(layer_rows(place, r, s, rows), rows), :] = piece[0]
    half = own.shape[0]
    for r, weight in enumerate((own, other)):
        value = lax.dot_general(
            weight[...], tokens[...], (((1,), (1,)), ((), ())), preferred_element_type=jnp.float32
        ).astype(jnp.bfloat16)
        for k in range(nz):
            @pl.when(step == k)
            def _():
                outs[k][r * half : (r + 1) * half, :] = value


def out_kernel(nz, place, own, other, *refs):
    columns, (keep, send, total) = refs[:nz], refs[nz:]
    step = pl.program_id(0)
    rows = keep.shape[2]
    half = own.shape[0]
    for k in range(nz):
        @pl.when(step == k)
        def _():
            lhs = columns[k][...].T
            value = jnp.dot(lhs[:, :half], own[...], preferred_element_type=jnp.float32)
            value += jnp.dot(lhs[:, half:], other[...], preferred_element_type=jnp.float32)
            total[...] = value.astype(jnp.bfloat16)
    for r in range(2):
        keep[0, r] = total[pl.ds(layer_rows(place, r, 0, rows), rows), :]
        send[0, r] = total[pl.ds(layer_rows(place, r, 1, rows), rows), :]


def weight_grad_kernel(nz, factor, place, c00, c10, c01, c11, *refs):
    columns, (mine, theirs, lhs, tokens) = refs[:nz], refs[nz:]
    rows = c00.shape[1]
    group = 4 * rows
    half = mine.shape[0]

    @pl.when(pl.program_id(0) == 0)
    def _():
        for k in range(nz):
            lhs[:, k * group : (k + 1) * group] = columns[k][...]

    for (r, s), piece in (((0, 0), c00), ((1, 0), c10), ((0, 1), c01), ((1, 1), c11)):
        for k in range(nz):
            start = pl.multiple_of(k * group + layer_rows(place, r, s, rows), 16)
            tokens[pl.ds(start, rows), :] = piece[k]
    value = jnp.dot(lhs[...], tokens[...], preferred_element_type=jnp.float32) * factor
    mine[...] = value[:half]
    theirs[...] = value[half:].astype(jnp.bfloat16)


def grads_kernel(nz, units, place, gate, up, *refs):
    pieces, (gate_grad, up_grad, rows) = refs[:nz], refs[nz:]
    step = pl.program_id(0)
    span = gate.shape[1]

    @pl.when(step == 0)
    def _():
        half = units // 2
        for k in range(nz):
            for r in range(2):
                start = (place[0] ^ k) * units + (place[1] ^ r) * half
                rows[pl.ds(pl.multiple_of(start, 16), half), :] = pieces[k][
                    r * half : (r + 1) * half, :
                ]

    dhidden = rows[pl.ds(pl.multiple_of(step * span, 128), span), :].T.astype(jnp.float32)
    value = gate[...].astype(jnp.float32)
    up_value = up[...].astype(jnp.float32)
    sigmoid_gate = jax.nn.sigmoid(value)
    gate_grad[...] = (
        dhidden * up_value * sigmoid_gate * (1.0 + value * (1.0 - sigmoid_gate))
    ).astype(jnp.bfloat16)
    up_grad[...] = (dhidden * (value * sigmoid_gate)).astype(jnp.bfloat16)


def paired_body(gate_pre, up_pre, down_codes, down_scales, cotangent):
    group_rows, local_hidden = gate_pre.shape
    owned, width = down_codes.shape
    nz = lax.axis_size("z")
    rows = cotangent.shape[0]
    units = 2 * owned
    total_tokens = group_rows * nz * 2
    bf16, f32 = jnp.bfloat16, jnp.float32
    place = jnp.stack([lax.axis_index(name) for name in ("z", "x", "y", "c")]).astype(jnp.int32)
    struct = jax.ShapeDtypeStruct

    line = jnp.stack([cotangent] + [exchange(cotangent, "z", k) for k in range(1, nz)])
    over_y = exchange(line, "y", 1)
    received = (line, over_y, exchange(line, "c", 1), exchange(over_y, "c", 1))

    own = call_kernel(
        dequantize_kernel, place, (down_codes, down_scales),
        [whole(down_codes.shape), whole(down_scales.shape)],
        struct((owned, width), bf16), whole((owned, width)), (1,), [],
        (owned * width, owned * width * 4, 0),
    )
    other = exchange(own, "x", 1)

    span = column_span(local_hidden)
    steps = local_hidden // span
    piece = struct((units, group_rows), bf16)
    wide = pl.BlockSpec((group_rows, span), lambda i, place: (0, i))
    act_bytes = group_rows * local_hidden * 2
    sent = call_kernel(
        functools.partial(hidden_kernel, nz, units), place, (gate_pre, up_pre), [wide] * 2,
        [piece] * nz, [whole(piece.shape)] * nz, (steps,),
        [pltpu.VMEM((local_hidden, group_rows), bf16)],
        (4 * act_bytes, 3 * act_bytes, act_bytes // 2),
    )
    columns = [sent[0]] + [exchange(sent[k], "z", k) for k in range(1, nz)]

    weight_specs = [whole((owned, width))] * 2
    token_block = pl.BlockSpec((1, rows, width), lambda i, place: (i, 0, 0))
    flops = 2 * group_rows * nz * units * width
    dsent = call_kernel(
        functools.partial(dhidden_kernel, nz), place, (own, other) + received,
        weight_specs + [token_block] * 4,
        [piece] * nz, [whole(piece.shape)] * nz, (nz,),
        [pltpu.VMEM((group_rows, width), bf16)],
        (flops, 2 * units * width + 2 * nz * group_rows * width, 0),
    )
    back = [dsent[0]] + [exchange(dsent[k], "z", k) for k in range(1, nz)]

    halves = struct((nz, 2, rows, width), bf16)
    half_spec = pl.BlockSpec((1, 2, rows, width), lambda i, place: (i, 0, 0, 0))
    keep, send = call_kernel(
        functools.partial(out_kernel, nz), place, (own, other, *columns),
        weight_specs + [whole(piece.shape)] * nz,
        [halves] * 2, [half_spec] * 2, (nz,),
        [pltpu.VMEM((group_rows, width), bf16)],
        (flops, 2 * units * width + 2 * nz * group_rows * width, 0),
    )
    over_c = keep.astype(f32) + exchange(send, "c", 1).astype(f32)
    over_y = over_c[:, 0] + exchange(over_c[:, 1].astype(bf16), "y", 1).astype(f32)
    layer_out = over_y[0]
    for k in range(1, nz):
        layer_out = layer_out + exchange(over_y[k].astype(bf16), "z", k).astype(f32)
    layer_out = layer_out.astype(bf16)

    tile = column_span(width)
    token_tile = pl.BlockSpec((nz, rows, tile), lambda i, place: (0, 0, i))
    grad_tile = pl.BlockSpec((owned, tile), lambda i, place: (0, i))
    factor = float(total_tokens) ** (-0.5)
    mine, theirs = call_kernel(
        functools.partial(weight_grad_kernel, nz, factor), place, received + tuple(columns),
        [token_tile] * 4 + [whole(piece.shape)] * nz,
        [struct((owned, width), f32), struct((owned, width), bf16)], [grad_tile] * 2,
        (width // tile,),
        [pltpu.VMEM((units, nz * group_rows), bf16), pltpu.VMEM((nz * group_rows, tile), bf16)],
        (flops, 3 * units * width + 2 * nz * group_rows * width, 0),
    )
    weight_grad = mine + exchange(theirs, "x", 1).astype(f32)

    gate_grad, up_grad = call_kernel(
        functools.partial(grads_kernel, nz, units), place, (gate_pre, up_pre, *back),
        [wide] * 2 + [whole(piece.shape)] * nz,
        [struct((group_rows, local_hidden), bf16)] * 2, [wide] * 2, (steps,),
        [pltpu.VMEM((local_hidden, group_rows), bf16)],
        (12 * act_bytes, 5 * act_bytes, act_bytes // 2),
    )
    return layer_out, gate_grad, up_grad, weight_grad


def column_span(width):
    return max((s for s in range(128, 641, 128) if width % s == 0), default=0)


def body(gate_pre, up_pre, down_codes, down_scales, cotangent):
    group_rows, local_hidden = gate_pre.shape
    owned, width = down_codes.shape
    nz, nx, ny, nc = (lax.axis_size(name) for name in ("z", "x", "y", "c"))
    rows = cotangent.shape[0]
    units = nx * owned
    total_tokens = group_rows * nz * nx

    gate_value = gate_pre.astype(jnp.float32)
    up_value = up_pre.astype(jnp.float32)
    sigmoid_gate = jax.nn.sigmoid(gate_value)
    activated = gate_value * sigmoid_gate
    hidden = (activated * up_value).astype(jnp.bfloat16)

    sent = hidden.T.reshape(nz, units, group_rows)
    columns = lax.all_to_all(sent, "z", 0, 0, tiled=True) if nz > 1 else sent

    line = lax.all_gather(cotangent, ("z", "y"), axis=0)
    both = gather_pair(line, "c")
    received = jnp.moveaxis(both, 0, 1).reshape(nz, group_rows, width)

    weight = gather_pair(dequantize(down_codes, down_scales), "x").reshape(units, width)

    partial_out = lax.dot_general(
        columns, weight, (((1,), (0,)), ((), ())), preferred_element_type=jnp.float32
    ).astype(jnp.bfloat16)
    partial_out = partial_out.reshape(nz, ny, nc, rows, width)
    over_c = scatter_sum(jnp.moveaxis(partial_out, 2, 0), "c")
    over_y = scatter_sum(jnp.moveaxis(over_c.astype(jnp.bfloat16), 1, 0), "y")
    layer_out = scatter_sum(over_y.astype(jnp.bfloat16), "z").astype(jnp.bfloat16)

    dcolumns = lax.dot_general(
        weight, received, (((1,), (2,)), ((), ())), preferred_element_type=jnp.float32
    ).astype(jnp.bfloat16)
    dcolumns = jnp.moveaxis(dcolumns, 1, 0)
    back = lax.all_to_all(dcolumns, "z", 0, 0, tiled=True) if nz > 1 else dcolumns
    dhidden = back.reshape(local_hidden, group_rows).T.astype(jnp.float32)
    gate_grad = (
        dhidden * up_value * sigmoid_gate * (1.0 + gate_value * (1.0 - sigmoid_gate))
    ).astype(jnp.bfloat16)
    up_grad = (dhidden * activated).astype(jnp.bfloat16)

    partial_grad = lax.dot_general(
        columns, received, (((0, 2), (0, 1)), ((), ())), preferred_element_type=jnp.float32
    )
    weight_grad = scatter_sum(partial_grad.reshape(nx, owned, width), "x") * float(total_tokens) ** (-0.5)
    return layer_out, gate_grad, up_grad, weight_grad


def outer_split(mesh, tokens, hidden, width):
    dp, tensor = mesh.shape["dp"], mesh.shape["tensor"]

    def rows_sent(nz):
        moved = 2 * (tokens // dp) * (hidden // tensor) / width if nz > 1 else 0
        return 2 * hidden // (tensor * nz) + 2 * tokens * nz // dp + moved

    return min((nz for nz in range(1, dp + 1) if dp % nz == 0), key=rows_sent)


def solution(mesh):
    def call(gate_pre, up_pre, down_codes, down_scales, cotangent):
        tokens, hidden = gate_pre.shape
        nz = outer_split(mesh, tokens, hidden, cotangent.shape[1])
        dp, tensor = mesh.shape["dp"], mesh.shape["tensor"]
        fine = Mesh(mesh.devices.reshape(nz, dp // nz, tensor // 2, 2), ("z", "x", "y", "c"))
        act = P(("z", "x"), ("y", "c"))
        weight = P(("y", "c", "z", "x"), None)
        layer = P(("z", "x", "y", "c"), None)
        owned = hidden // (dp * tensor)
        rows = tokens // (dp * tensor)
        pairs = fine.shape["x"] == 2 and fine.shape["y"] == 2 and nz & (nz - 1) == 0
        aligned = owned % 16 == 0 and rows % 16 == 0 and column_span(hidden // tensor)
        return jax.shard_map(
            paired_body if pairs and aligned and column_span(cotangent.shape[1]) else body,
            mesh=fine,
            in_specs=(act, act, weight, weight, layer),
            out_specs=(layer, act, act, weight),
            check_vma=False,
        )(gate_pre, up_pre, down_codes, down_scales, cotangent)

    return call
```

```python
import functools

import jax
import jax.numpy as jnp
from jax import lax
from jax.experimental import pallas as pl
from jax.experimental.pallas import tpu as pltpu
from jax.sharding import Mesh, PartitionSpec as P

VMEM_BYTES = 48 * 2**20


def dequantize(codes, scales):
    rows, width = codes.shape
    nblocks = scales.shape[1]
    blocks = codes.astype(jnp.float32).reshape(rows, nblocks, width // nblocks) * scales[:, :, None]
    return blocks.reshape(rows, width).astype(jnp.bfloat16)


def swap(value, axis):
    return lax.ppermute(value, axis, [(0, 1), (1, 0)])


def gather_pair(value, axis):
    if lax.axis_size(axis) != 2:
        return lax.all_gather(value, axis, axis=0)
    other = swap(value, axis)
    first = lax.axis_index(axis) == 0
    return jnp.stack([jnp.where(first, value, other), jnp.where(first, other, value)])


def scatter_sum(parts, axis):
    size = lax.axis_size(axis)
    if size == 1:
        return parts[0].astype(jnp.float32)
    if size != 2:
        received = lax.all_to_all(parts.astype(jnp.bfloat16), axis, 0, 0, tiled=True)
        return jnp.sum(received.astype(jnp.float32), axis=0)
    me = lax.axis_index(axis)
    theirs = lax.dynamic_index_in_dim(parts, 1 - me, 0, keepdims=False).astype(jnp.bfloat16)
    mine = lax.dynamic_index_in_dim(parts, me, 0, keepdims=False)
    return mine.astype(jnp.float32) + swap(theirs, axis).astype(jnp.float32)


def exchange(value, axis, offset):
    size = lax.axis_size(axis)
    return lax.ppermute(value, axis, [(i, i ^ offset) for i in range(size)])


def call_kernel(kernel, place, inputs, in_specs, out_shapes, out_specs, grid, scratch, cost):
    flops, nbytes, transcendentals = cost
    return pl.pallas_call(
        kernel,
        out_shape=out_shapes,
        grid_spec=pltpu.PrefetchScalarGridSpec(
            num_scalar_prefetch=1,
            grid=grid,
            in_specs=in_specs,
            out_specs=out_specs,
            scratch_shapes=scratch,
        ),
        compiler_params=pltpu.CompilerParams(vmem_limit_bytes=VMEM_BYTES),
        cost_estimate=pl.CostEstimate(
            flops=flops, bytes_accessed=nbytes, transcendentals=transcendentals
        ),
    )(place, *inputs)


def whole(shape):
    return pl.BlockSpec(shape, lambda i, place: (0,) * len(shape))


def hidden_kernel(nz, units, place, gate, up, *refs):
    outs, rows = refs[:nz], refs[nz]
    step = pl.program_id(0)
    span = gate.shape[1]
    value = gate[...].astype(jnp.float32)
    hidden = value * jax.nn.sigmoid(value) * up[...].astype(jnp.float32)
    rows[pl.ds(pl.multiple_of(step * span, 128), span), :] = hidden.astype(jnp.bfloat16).T

    @pl.when(step == pl.num_programs(0) - 1)
    def _():
        half = units // 2
        for k in range(nz):
            for r in range(2):
                start = (place[0] ^ k) * units + (place[1] ^ r) * half
                outs[k][r * half : (r + 1) * half, :] = rows[
                    pl.ds(pl.multiple_of(start, 16), half), :
                ]


def layer_rows(place, r, s, rows):
    return pl.multiple_of(((place[2] ^ r) * 2 + (place[3] ^ s)) * rows, 16)


def weight_kernel(first, place, codes, scales, other_codes, other_scales, weight, turned):
    span = codes.shape[1]
    lane = lax.broadcasted_iota(jnp.int32, scales.shape, 1)
    pair = []
    for code, scale in ((codes, scales), (other_codes, other_scales)):
        mine = jnp.where(lane == first + pl.program_id(0), scale[...], 0.0)
        column = jnp.sum(mine, axis=1, keepdims=True)
        pair.append((code[...].astype(jnp.float32) * column).astype(jnp.bfloat16))
    value = jnp.concatenate(pair, axis=0)
    weight[...] = value
    turned[...] = value.T


def dhidden_kernel(place, upper, lower, c00, c10, c01, c11, rows_out, tokens):
    rows = c00.shape[1]
    for (r, s), piece in (((0, 0), c00), ((1, 0), c10), ((0, 1), c01), ((1, 1), c11)):
        tokens[pl.ds(layer_rows(place, r, s, rows), rows), :] = piece[0]
    middle = upper.shape[0]
    value = jnp.dot(tokens[:, :middle], upper[...], preferred_element_type=jnp.float32)
    value += jnp.dot(tokens[:, middle:], lower[...], preferred_element_type=jnp.float32)
    rows_out[...] = value.astype(jnp.bfloat16).T


def out_kernel(count, place, left, right, *refs):
    columns, (_, keep, send, lhs, total) = refs[:count], refs[count:]
    rows = keep.shape[2]
    group = 4 * rows

    @pl.when(pl.program_id(0) == 0)
    def _():
        for k in range(count):
            lhs[k * group : (k + 1) * group, :] = columns[k][...].T

    weight = jnp.where(pl.program_id(0) * 2 < pl.num_programs(0), left[...], right[...])
    value = jnp.dot(lhs[...], weight, preferred_element_type=jnp.float32)
    total[...] = value.astype(jnp.bfloat16)
    for k in range(count):
        for r in range(2):
            for s, target in ((0, keep), (1, send)):
                start = pl.multiple_of(k * group + layer_rows(place, r, s, rows), 16)
                target[k, r] = total[pl.ds(start, rows), :]


def weight_grad_kernel(nz, first, factor, place, *refs):
    columns, tokens, (_, grad) = refs[:nz], refs[nz : 2 * nz], refs[2 * nz :]
    half = grad.shape[0]
    lhs = jnp.concatenate([c[first : first + half, :] for c in columns], axis=1)
    rhs = jnp.concatenate([t[...] for t in tokens], axis=0)
    value = jnp.dot(lhs, rhs, preferred_element_type=jnp.float32) * factor
    grad[...] = value.astype(grad.dtype)


def grads_kernel(nz, units, place, gate, up, *refs):
    pieces, (gate_grad, up_grad, rows) = refs[:nz], refs[nz:]
    step = pl.program_id(0)
    span = gate.shape[1]

    @pl.when(step == 0)
    def _():
        half = units // 2
        for k in range(nz):
            for r in range(2):
                start = (place[0] ^ k) * units + (place[1] ^ r) * half
                rows[pl.ds(pl.multiple_of(start, 16), half), :] = pieces[k][
                    r * half : (r + 1) * half, :
                ]

    dhidden = rows[pl.ds(pl.multiple_of(step * span, 128), span), :].T.astype(jnp.float32)
    value = gate[...].astype(jnp.float32)
    up_value = up[...].astype(jnp.float32)
    sigmoid_gate = jax.nn.sigmoid(value)
    gate_grad[...] = (
        dhidden * up_value * sigmoid_gate * (1.0 + value * (1.0 - sigmoid_gate))
    ).astype(jnp.bfloat16)
    up_grad[...] = (dhidden * (value * sigmoid_gate)).astype(jnp.bfloat16)


def paired_body(gate_pre, up_pre, down_codes, down_scales, cotangent):
    group_rows, local_hidden = gate_pre.shape
    owned, width = down_codes.shape
    nz = lax.axis_size("z")
    rows = cotangent.shape[0]
    units = 2 * owned
    total_tokens = group_rows * nz * 2
    bf16, f32 = jnp.bfloat16, jnp.float32
    place = jnp.stack([lax.axis_index(name) for name in ("z", "x", "y", "c")]).astype(jnp.int32)
    struct = jax.ShapeDtypeStruct

    middle = width // 2
    codes = [down_codes[:, :middle], down_codes[:, middle:]]
    partner_scales = exchange(down_scales, "x", 1)
    partner_codes = [exchange(codes[0], "x", 1)]

    span = column_span(local_hidden)
    steps = local_hidden // span
    piece = struct((units, group_rows), bf16)
    wide = pl.BlockSpec((group_rows, span), lambda i, place: (0, i))
    act_bytes = group_rows * local_hidden * 2
    sent = call_kernel(
        functools.partial(hidden_kernel, nz, units), place, (gate_pre, up_pre), [wide] * 2,
        [piece] * nz, [whole(piece.shape)] * nz, (steps,),
        [pltpu.VMEM((local_hidden, group_rows), bf16)],
        (4 * act_bytes, 3 * act_bytes, act_bytes // 2),
    )
    line = [exchange(cotangent, "z", k) for k in range(1, nz)]
    line, sent, partner_codes, partner_scales = lax.optimization_barrier(
        (line, sent, partner_codes, partner_scales)
    )
    partner_codes.append(exchange(codes[1], "x", 1))
    line = jnp.stack([cotangent] + line)
    columns = [sent[0]] + [exchange(sent[k], "z", k) for k in range(1, nz)]
    over_y = exchange(line, "y", 1)
    other_core = exchange(line, "c", 1)
    over_y, columns, partner_codes = lax.optimization_barrier((over_y, columns, partner_codes))
    received = (line, over_y, other_core, exchange(over_y, "c", 1))

    tile = column_span(middle)
    steps_out = width // tile
    tall = pl.BlockSpec((owned, tile), lambda i, place: (0, i))
    nblocks = down_scales.shape[1]
    block = width // nblocks
    code_block = pl.BlockSpec((owned, block), lambda i, place: (0, i))
    weight, turned = [], []
    for side in range(2):
        half_weight, half_turned = call_kernel(
            functools.partial(weight_kernel, side * nblocks // 2), place,
            (codes[side], down_scales, partner_codes[side], partner_scales),
            [code_block, whole(down_scales.shape)] * 2,
            [struct((units, middle), bf16), struct((middle, units), bf16)],
            [pl.BlockSpec((units, block), lambda i, place: (0, i)),
             pl.BlockSpec((block, units), lambda i, place: (i, 0))], (nblocks // 2,), [],
            (0, 3 * units * width, 0),
        )
        weight.append(half_weight)
        turned.append(half_turned)

    flops = 2 * group_rows * units * width
    dsent, tokens = [], []

    def layer_group(k):
        return pl.BlockSpec((1, rows, width), lambda i, place: (k, 0, 0))

    for k in range(nz):
        value, group = call_kernel(
            dhidden_kernel, place, (*turned, *received),
            [whole((middle, units))] * 2 + [layer_group(k)] * 4,
            [piece, struct((group_rows, width), bf16)],
            [whole(piece.shape), whole((group_rows, width))], (1,), [],
            (flops, 2 * units * width + 4 * group_rows * width, 0),
        )
        dsent.append(value)
        tokens.append(group)
    back = [dsent[0]] + [exchange(dsent[k], "z", k) for k in range(1, nz)]

    token_tile = pl.BlockSpec((group_rows, tile), lambda i, place: (0, i))
    factor = float(total_tokens) ** (-0.5)
    anywhere = pl.BlockSpec(memory_space=pl.ANY)

    def grad_half(first, dtype, after):
        return call_kernel(
            functools.partial(weight_grad_kernel, nz, first, factor), place,
            (*columns, *tokens, after),
            [whole(piece.shape)] * nz + [token_tile] * nz + [anywhere],
            struct((owned, width), dtype), tall, (steps_out,), [],
            (nz * flops // 2, 4 * owned * width + 2 * nz * group_rows * (width + units), 0),
        )

    theirs = grad_half(owned, bf16, dsent[0])
    x_sum = exchange(theirs, "x", 1)

    over_z = []
    after = theirs
    order = list(range(nz))[::-1]
    for chunk in (order[: nz // 2], order[nz // 2 :]):
        count = len(chunk)
        if not count:
            continue
        halves = struct((count, 2, rows, width), bf16)
        half_spec = pl.BlockSpec((count, 2, rows, tile), lambda i, place: (0, 0, 0, i))
        keep, send = call_kernel(
            functools.partial(out_kernel, count), place,
            (*weight, *(columns[k] for k in chunk), after),
            [pl.BlockSpec((units, tile), lambda i, place: (0, jnp.minimum(i, steps_out // 2 - 1))),
             pl.BlockSpec((units, tile), lambda i, place: (0, jnp.maximum(i - steps_out // 2, 0)))] + [whole(piece.shape)] * count + [anywhere],
            [halves] * 2, [half_spec] * 2, (steps_out,),
            [pltpu.VMEM((count * group_rows, units), bf16), pltpu.VMEM((count * group_rows, tile), bf16)],
            (count * flops, 2 * units * width + 2 * count * group_rows * width, 0),
        )
        after = keep
        over_c = keep.astype(f32) + exchange(send, "c", 1).astype(f32)
        over_y = over_c[:, 0] + exchange(over_c[:, 1].astype(bf16), "y", 1).astype(f32)
        for at, k in enumerate(chunk):
            over_z.append(exchange(over_y[at].astype(bf16), "z", k).astype(f32) if k else over_y[at])
    layer_out = sum(over_z[::-1][1:], over_z[-1]).astype(bf16)

    mine = grad_half(0, f32, after)
    weight_grad = mine + x_sum.astype(f32)

    gate_grad, up_grad = call_kernel(
        functools.partial(grads_kernel, nz, units), place, (gate_pre, up_pre, *back),
        [wide] * 2 + [whole(piece.shape)] * nz,
        [struct((group_rows, local_hidden), bf16)] * 2, [wide] * 2, (steps,),
        [pltpu.VMEM((local_hidden, group_rows), bf16)],
        (12 * act_bytes, 5 * act_bytes, act_bytes // 2),
    )
    return layer_out, gate_grad, up_grad, weight_grad


def column_span(width):
    return max((s for s in range(128, 641, 128) if width % s == 0), default=0)


def body(gate_pre, up_pre, down_codes, down_scales, cotangent):
    group_rows, local_hidden = gate_pre.shape
    owned, width = down_codes.shape
    nz, nx, ny, nc = (lax.axis_size(name) for name in ("z", "x", "y", "c"))
    rows = cotangent.shape[0]
    units = nx * owned
    total_tokens = group_rows * nz * nx

    gate_value = gate_pre.astype(jnp.float32)
    up_value = up_pre.astype(jnp.float32)
    sigmoid_gate = jax.nn.sigmoid(gate_value)
    activated = gate_value * sigmoid_gate
    hidden = (activated * up_value).astype(jnp.bfloat16)

    sent = hidden.T.reshape(nz, units, group_rows)
    columns = lax.all_to_all(sent, "z", 0, 0, tiled=True) if nz > 1 else sent

    line = lax.all_gather(cotangent, ("z", "y"), axis=0)
    both = gather_pair(line, "c")
    received = jnp.moveaxis(both, 0, 1).reshape(nz, group_rows, width)

    weight = gather_pair(dequantize(down_codes, down_scales), "x").reshape(units, width)

    partial_out = lax.dot_general(
        columns, weight, (((1,), (0,)), ((), ())), preferred_element_type=jnp.float32
    ).astype(jnp.bfloat16)
    partial_out = partial_out.reshape(nz, ny, nc, rows, width)
    over_c = scatter_sum(jnp.moveaxis(partial_out, 2, 0), "c")
    over_y = scatter_sum(jnp.moveaxis(over_c.astype(jnp.bfloat16), 1, 0), "y")
    layer_out = scatter_sum(over_y.astype(jnp.bfloat16), "z").astype(jnp.bfloat16)

    dcolumns = lax.dot_general(
        weight, received, (((1,), (2,)), ((), ())), preferred_element_type=jnp.float32
    ).astype(jnp.bfloat16)
    dcolumns = jnp.moveaxis(dcolumns, 1, 0)
    back = lax.all_to_all(dcolumns, "z", 0, 0, tiled=True) if nz > 1 else dcolumns
    dhidden = back.reshape(local_hidden, group_rows).T.astype(jnp.float32)
    gate_grad = (
        dhidden * up_value * sigmoid_gate * (1.0 + gate_value * (1.0 - sigmoid_gate))
    ).astype(jnp.bfloat16)
    up_grad = (dhidden * activated).astype(jnp.bfloat16)

    partial_grad = lax.dot_general(
        columns, received, (((0, 2), (0, 1)), ((), ())), preferred_element_type=jnp.float32
    )
    weight_grad = scatter_sum(partial_grad.reshape(nx, owned, width), "x") * float(total_tokens) ** (-0.5)
    return layer_out, gate_grad, up_grad, weight_grad


def outer_split(mesh, tokens, hidden, width):
    dp, tensor = mesh.shape["dp"], mesh.shape["tensor"]

    def rows_sent(nz):
        moved = 2 * (tokens // dp) * (hidden // tensor) / width if nz > 1 else 0
        return 2 * hidden // (tensor * nz) + 2 * tokens * nz // dp + moved

    return min((nz for nz in range(1, dp + 1) if dp % nz == 0), key=rows_sent)


def solution(mesh):
    def call(gate_pre, up_pre, down_codes, down_scales, cotangent):
        tokens, hidden = gate_pre.shape
        nz = outer_split(mesh, tokens, hidden, cotangent.shape[1])
        dp, tensor = mesh.shape["dp"], mesh.shape["tensor"]
        fine = Mesh(mesh.devices.reshape(nz, dp // nz, tensor // 2, 2), ("z", "x", "y", "c"))
        act = P(("z", "x"), ("y", "c"))
        weight = P(("y", "c", "z", "x"), None)
        layer = P(("z", "x", "y", "c"), None)
        owned = hidden // (dp * tensor)
        rows = tokens // (dp * tensor)
        pairs = fine.shape["x"] == 2 and fine.shape["y"] == 2 and nz & (nz - 1) == 0
        nblocks = down_scales.shape[1]
        blocks = nblocks % 2 == 0 and cotangent.shape[1] // nblocks % 128 == 0
        aligned = owned % 16 == 0 and rows % 16 == 0 and column_span(hidden // tensor)
        return jax.shard_map(
            paired_body if pairs and aligned and blocks else body,
            mesh=fine,
            in_specs=(act, act, weight, weight, layer),
            out_specs=(layer, act, act, weight),
            check_vma=False,
        )(gate_pre, up_pre, down_codes, down_scales, cotangent)

    return call
```

```python
import functools

import jax
import jax.numpy as jnp
from jax import lax
from jax.experimental import pallas as pl
from jax.experimental.pallas import tpu as pltpu
from jax.sharding import Mesh, PartitionSpec as P

VMEM_BYTES = 32 * 2**20
WEIGHT_COST = 6


def dequantize(codes, scales):
    rows, width = codes.shape
    nblocks = scales.shape[1]
    blocks = codes.astype(jnp.float32).reshape(rows, nblocks, width // nblocks) * scales[:, :, None]
    return blocks.reshape(rows, width).astype(jnp.bfloat16)


def swap(value, axis):
    return lax.ppermute(value, axis, [(0, 1), (1, 0)])


def gather_pair(value, axis):
    if lax.axis_size(axis) != 2:
        return lax.all_gather(value, axis, axis=0)
    other = swap(value, axis)
    first = lax.axis_index(axis) == 0
    return jnp.stack([jnp.where(first, value, other), jnp.where(first, other, value)])


def scatter_sum(parts, axis):
    size = lax.axis_size(axis)
    if size == 1:
        return parts[0].astype(jnp.float32)
    if size != 2:
        received = lax.all_to_all(parts.astype(jnp.bfloat16), axis, 0, 0, tiled=True)
        return jnp.sum(received.astype(jnp.float32), axis=0)
    me = lax.axis_index(axis)
    theirs = lax.dynamic_index_in_dim(parts, 1 - me, 0, keepdims=False).astype(jnp.bfloat16)
    mine = lax.dynamic_index_in_dim(parts, me, 0, keepdims=False)
    return mine.astype(jnp.float32) + swap(theirs, axis).astype(jnp.float32)


def exchange(value, axis, offset):
    size = lax.axis_size(axis)
    return lax.ppermute(value, axis, [(i, i ^ offset) for i in range(size)])


def call_kernel(kernel, place, inputs, in_specs, out_shapes, out_specs, grid, scratch, cost):
    flops, nbytes, transcendentals = cost
    return pl.pallas_call(
        kernel,
        out_shape=out_shapes,
        grid_spec=pltpu.PrefetchScalarGridSpec(
            num_scalar_prefetch=1,
            grid=grid,
            in_specs=in_specs,
            out_specs=out_specs,
            scratch_shapes=scratch,
        ),
        compiler_params=pltpu.CompilerParams(vmem_limit_bytes=VMEM_BYTES),
        cost_estimate=pl.CostEstimate(
            flops=flops, bytes_accessed=nbytes, transcendentals=transcendentals
        ),
    )(place, *inputs)


def whole(shape):
    return pl.BlockSpec(shape, lambda i, place: (0,) * len(shape))


def token_start(place, block, rows):
    return pl.multiple_of(((place[2] ^ (block % 2)) * 2 + (place[3] ^ (block // 2))) * rows, 16)


def hidden_kernel(nz, units, place, gate, up, *refs):
    outs, (natural, columns) = refs[:nz], refs[nz:]
    step = pl.program_id(0)
    group, span = gate.shape
    rows = group // 4
    value = gate[...].astype(jnp.float32)
    hidden = value * jax.nn.sigmoid(value) * up[...].astype(jnp.float32)
    natural[...] = hidden.astype(jnp.bfloat16)
    ordered = [natural[pl.ds(token_start(place, b, rows), rows), :] for b in range(4)]
    columns[pl.ds(pl.multiple_of(step * span, 128), span), :] = jnp.concatenate(ordered, axis=0).T

    @pl.when(step == pl.num_programs(0) - 1)
    def _():
        half = units // 2
        for k in range(nz):
            for r in range(2):
                start = (place[0] ^ k) * units + (place[1] ^ r) * half
                outs[k][r * half : (r + 1) * half, :] = columns[
                    pl.ds(pl.multiple_of(start, 16), half), :
                ]


def weight_kernel(place, codes, scales, other_codes, other_scales, weight):
    lane = lax.broadcasted_iota(jnp.int32, scales.shape, 1)
    half = codes.shape[0]
    for r, (code, scale) in enumerate(((codes, scales), (other_codes, other_scales))):
        mine = jnp.where(lane == pl.program_id(0), scale[...], 0.0)
        value = code[...].astype(jnp.float32) * jnp.sum(mine, axis=1, keepdims=True)
        weight[r * half : (r + 1) * half, :] = value.astype(jnp.bfloat16)


def columns_kernel(nz, place, *refs):
    pieces, (keep, send, mine, theirs) = refs[:nz], refs[nz:]
    half, group = mine.shape[0], pieces[0].shape[1]
    rows = group // 4
    for k in range(nz):
        turned = pieces[k][...].T
        for b in range(4):
            target = send if b >= 2 else keep
            start = ((b % 2) * nz + k) * rows
            target[start : start + rows, :] = turned[b * rows : (b + 1) * rows, :]
        mine[:, k * group : (k + 1) * group] = pieces[k][:half, :]
        theirs[:, k * group : (k + 1) * group] = pieces[k][half:, :]


def grads_kernel(nz, units, place, gate, up, *refs):
    pieces, (gate_grad, up_grad, columns, natural) = refs[:nz], refs[nz:]
    step = pl.program_id(0)
    group, span = gate.shape
    rows = group // 4

    @pl.when(step == 0)
    def _():
        half = units // 2
        for k in range(nz):
            for r in range(2):
                start = (place[0] ^ k) * units + (place[1] ^ r) * half
                columns[pl.ds(pl.multiple_of(start, 16), half), :] = pieces[k][
                    r * half : (r + 1) * half, :
                ]

    ordered = columns[pl.ds(pl.multiple_of(step * span, 128), span), :].T
    for b in range(4):
        natural[pl.ds(token_start(place, b, rows), rows), :] = ordered[b * rows : (b + 1) * rows]
    dhidden = natural[...].astype(jnp.float32)
    value = gate[...].astype(jnp.float32)
    up_value = up[...].astype(jnp.float32)
    sigmoid_gate = jax.nn.sigmoid(value)
    gate_grad[...] = (
        dhidden * up_value * sigmoid_gate * (1.0 + value * (1.0 - sigmoid_gate))
    ).astype(jnp.bfloat16)
    up_grad[...] = (dhidden * (value * sigmoid_gate)).astype(jnp.bfloat16)


def matmul(lhs, rhs, lhs_dim=1, rhs_dim=0, dtype=jnp.float32):
    dims = (((lhs_dim,), (rhs_dim,)), ((), ()))
    return lax.dot_general(lhs, rhs, dims, preferred_element_type=jnp.float32).astype(dtype)


def paired_body(gate_pre, up_pre, down_codes, down_scales, cotangent):
    group_rows, local_hidden = gate_pre.shape
    owned, width = down_codes.shape
    nz = lax.axis_size("z")
    rows = cotangent.shape[0]
    units = 2 * owned
    total_tokens = group_rows * nz * 2
    bf16, f32 = jnp.bfloat16, jnp.float32
    place = jnp.stack([lax.axis_index(name) for name in ("z", "x", "y", "c")]).astype(jnp.int32)
    struct = jax.ShapeDtypeStruct

    other_codes, other_scales = exchange(down_codes, "x", 1), exchange(down_scales, "x", 1)

    span = column_span(local_hidden)
    steps = local_hidden // span
    piece = struct((units, group_rows), bf16)
    wide = pl.BlockSpec((group_rows, span), lambda i, place: (0, i))
    act_bytes = group_rows * local_hidden * 2
    act_scratch = [pltpu.VMEM((group_rows, span), bf16), pltpu.VMEM((local_hidden, group_rows), bf16)]
    sent = call_kernel(
        functools.partial(hidden_kernel, nz, units), place, (gate_pre, up_pre), [wide] * 2,
        [piece] * nz, [whole(piece.shape)] * nz, (steps,), act_scratch,
        (4 * act_bytes, 3 * act_bytes, act_bytes // 2),
    )

    line = [exchange(cotangent, "z", k) for k in range(1, nz)]
    line, sent = lax.optimization_barrier((line, sent))
    line = jnp.stack([cotangent] + line)
    columns = [sent[0]] + [exchange(sent[k], "z", k) for k in range(1, nz)]
    over_y = exchange(line, "y", 1)
    other_core = exchange(line, "c", 1)

    nblocks = down_scales.shape[1]
    block = width // nblocks
    code_block = pl.BlockSpec((owned, block), lambda i, place: (0, i))
    weight = call_kernel(
        weight_kernel, place, (down_codes, down_scales, other_codes, other_scales),
        [code_block, whole(down_scales.shape)] * 2, struct((units, width), bf16),
        pl.BlockSpec((units, block), lambda i, place: (0, i)), (nblocks,), [],
        (2 * units * width, WEIGHT_COST * units * width, 0),
    )
    over_y, columns, weight = lax.optimization_barrier((over_y, columns, weight))
    received = (line, over_y, other_core, exchange(over_y, "c", 1))
    half_tokens = nz * group_rows // 2
    keep, send, mine, theirs = call_kernel(
        functools.partial(columns_kernel, nz), place, tuple(columns),
        [whole(piece.shape)] * nz,
        [struct((half_tokens, units), bf16)] * 2 + [struct((owned, 2 * half_tokens), bf16)] * 2,
        [whole((half_tokens, units))] * 2 + [whole((owned, 2 * half_tokens))] * 2, (1,), [],
        (0, 12 * units * half_tokens, 0),
    )

    tokens = jnp.stack(received, axis=1).reshape(nz, group_rows, width)
    back = [matmul(weight, tokens[k], 1, 1, bf16) for k in range(nz)]
    back = [back[0]] + [exchange(back[k], "z", k) for k in range(1, nz)]

    tokens = tokens.reshape(-1, width)
    factor = float(total_tokens) ** (-0.5)
    over_x = exchange((matmul(theirs, tokens) * factor).astype(bf16), "x", 1)
    weight_grad = matmul(mine, tokens) * factor + over_x.astype(f32)

    over_c = exchange(matmul(send, weight, dtype=bf16), "c", 1)
    own_c = matmul(keep, weight, dtype=bf16)
    sums = (own_c.astype(f32) + over_c.astype(f32)).reshape(2, nz, rows, width)
    over_y = sums[0] + exchange(sums[1].astype(bf16), "y", 1).astype(f32)
    layer_out = over_y[0]
    for k in range(1, nz):
        layer_out = layer_out + exchange(over_y[k].astype(bf16), "z", k).astype(f32)
    layer_out = layer_out.astype(bf16)

    gate_grad, up_grad = call_kernel(
        functools.partial(grads_kernel, nz, units), place, (gate_pre, up_pre, *back),
        [wide] * 2 + [whole(piece.shape)] * nz,
        [struct((group_rows, local_hidden), bf16)] * 2, [wide] * 2, (steps,), act_scratch[::-1],
        (12 * act_bytes, 5 * act_bytes, act_bytes // 2),
    )
    return layer_out, gate_grad, up_grad, weight_grad


def column_span(width):
    return max((s for s in range(128, 641, 128) if width % s == 0), default=0)


def body(gate_pre, up_pre, down_codes, down_scales, cotangent):
    group_rows, local_hidden = gate_pre.shape
    owned, width = down_codes.shape
    nz, nx, ny, nc = (lax.axis_size(name) for name in ("z", "x", "y", "c"))
    rows = cotangent.shape[0]
    units = nx * owned
    total_tokens = group_rows * nz * nx

    gate_value = gate_pre.astype(jnp.float32)
    up_value = up_pre.astype(jnp.float32)
    sigmoid_gate = jax.nn.sigmoid(gate_value)
    activated = gate_value * sigmoid_gate
    hidden = (activated * up_value).astype(jnp.bfloat16)

    sent = hidden.T.reshape(nz, units, group_rows)
    columns = lax.all_to_all(sent, "z", 0, 0, tiled=True) if nz > 1 else sent

    line = lax.all_gather(cotangent, ("z", "y"), axis=0)
    both = gather_pair(line, "c")
    received = jnp.moveaxis(both, 0, 1).reshape(nz, group_rows, width)

    weight = gather_pair(dequantize(down_codes, down_scales), "x").reshape(units, width)

    partial_out = lax.dot_general(
        columns, weight, (((1,), (0,)), ((), ())), preferred_element_type=jnp.float32
    ).astype(jnp.bfloat16)
    partial_out = partial_out.reshape(nz, ny, nc, rows, width)
    over_c = scatter_sum(jnp.moveaxis(partial_out, 2, 0), "c")
    over_y = scatter_sum(jnp.moveaxis(over_c.astype(jnp.bfloat16), 1, 0), "y")
    layer_out = scatter_sum(over_y.astype(jnp.bfloat16), "z").astype(jnp.bfloat16)

    dcolumns = lax.dot_general(
        weight, received, (((1,), (2,)), ((), ())), preferred_element_type=jnp.float32
    ).astype(jnp.bfloat16)
    dcolumns = jnp.moveaxis(dcolumns, 1, 0)
    back = lax.all_to_all(dcolumns, "z", 0, 0, tiled=True) if nz > 1 else dcolumns
    dhidden = back.reshape(local_hidden, group_rows).T.astype(jnp.float32)
    gate_grad = (
        dhidden * up_value * sigmoid_gate * (1.0 + gate_value * (1.0 - sigmoid_gate))
    ).astype(jnp.bfloat16)
    up_grad = (dhidden * activated).astype(jnp.bfloat16)

    partial_grad = lax.dot_general(
        columns, received, (((0, 2), (0, 1)), ((), ())), preferred_element_type=jnp.float32
    )
    weight_grad = scatter_sum(partial_grad.reshape(nx, owned, width), "x") * float(total_tokens) ** (-0.5)
    return layer_out, gate_grad, up_grad, weight_grad


def outer_split(mesh, tokens, hidden, width):
    dp, tensor = mesh.shape["dp"], mesh.shape["tensor"]

    def rows_sent(nz):
        moved = 2 * (tokens // dp) * (hidden // tensor) / width if nz > 1 else 0
        return 2 * hidden // (tensor * nz) + 2 * tokens * nz // dp + moved

    return min((nz for nz in range(1, dp + 1) if dp % nz == 0), key=rows_sent)


def solution(mesh):
    def call(gate_pre, up_pre, down_codes, down_scales, cotangent):
        tokens, hidden = gate_pre.shape
        nz = outer_split(mesh, tokens, hidden, cotangent.shape[1])
        dp, tensor = mesh.shape["dp"], mesh.shape["tensor"]
        fine = Mesh(mesh.devices.reshape(nz, dp // nz, tensor // 2, 2), ("z", "x", "y", "c"))
        act = P(("z", "x"), ("y", "c"))
        weight = P(("y", "c", "z", "x"), None)
        layer = P(("z", "x", "y", "c"), None)
        owned = hidden // (dp * tensor)
        rows = tokens // (dp * tensor)
        pairs = fine.shape["x"] == 2 and fine.shape["y"] == 2 and nz & (nz - 1) == 0
        aligned = owned % 16 == 0 and rows % 16 == 0 and column_span(hidden // tensor)
        block = cotangent.shape[1] // down_scales.shape[1]
        return jax.shard_map(
            paired_body if pairs and aligned and block % 128 == 0 else body,
            mesh=fine,
            in_specs=(act, act, weight, weight, layer),
            out_specs=(layer, act, act, weight),
            check_vma=False,
        )(gate_pre, up_pre, down_codes, down_scales, cotangent)

    return call
```

```python
import functools

import jax
import jax.numpy as jnp
from jax import lax
from jax.experimental import pallas as pl
from jax.experimental.pallas import tpu as pltpu
from jax.sharding import Mesh, PartitionSpec as P

VMEM_BYTES = 32 * 2**20


def dequantize(codes, scales):
    rows, width = codes.shape
    nblocks = scales.shape[1]
    blocks = codes.astype(jnp.float32).reshape(rows, nblocks, width // nblocks) * scales[:, :, None]
    return blocks.reshape(rows, width).astype(jnp.bfloat16)


def swap(value, axis):
    return lax.ppermute(value, axis, [(0, 1), (1, 0)])


def gather_pair(value, axis):
    if lax.axis_size(axis) != 2:
        return lax.all_gather(value, axis, axis=0)
    other = swap(value, axis)
    first = lax.axis_index(axis) == 0
    return jnp.stack([jnp.where(first, value, other), jnp.where(first, other, value)])


def scatter_sum(parts, axis):
    size = lax.axis_size(axis)
    if size == 1:
        return parts[0].astype(jnp.float32)
    if size != 2:
        received = lax.all_to_all(parts.astype(jnp.bfloat16), axis, 0, 0, tiled=True)
        return jnp.sum(received.astype(jnp.float32), axis=0)
    me = lax.axis_index(axis)
    theirs = lax.dynamic_index_in_dim(parts, 1 - me, 0, keepdims=False).astype(jnp.bfloat16)
    mine = lax.dynamic_index_in_dim(parts, me, 0, keepdims=False)
    return mine.astype(jnp.float32) + swap(theirs, axis).astype(jnp.float32)


def exchange(value, axis, offset):
    size = lax.axis_size(axis)
    return lax.ppermute(value, axis, [(i, i ^ offset) for i in range(size)])


def call_kernel(kernel, place, inputs, in_specs, out_shapes, out_specs, grid, scratch, cost):
    flops, nbytes, transcendentals = cost
    return pl.pallas_call(
        kernel,
        out_shape=out_shapes,
        grid_spec=pltpu.PrefetchScalarGridSpec(
            num_scalar_prefetch=1,
            grid=grid,
            in_specs=in_specs,
            out_specs=out_specs,
            scratch_shapes=scratch,
        ),
        compiler_params=pltpu.CompilerParams(vmem_limit_bytes=VMEM_BYTES),
        cost_estimate=pl.CostEstimate(
            flops=flops, bytes_accessed=nbytes, transcendentals=transcendentals
        ),
    )(place, *inputs)


def whole(shape):
    return pl.BlockSpec(shape, lambda i, place: (0,) * len(shape))


def token_start(place, block, rows):
    return pl.multiple_of(((place[2] ^ (block % 2)) * 2 + (place[3] ^ (block // 2))) * rows, 16)


def hidden_kernel(parts, units, place, gate, up, *refs):
    outs, (natural, columns) = refs[: len(parts)], refs[len(parts) :]
    step = pl.program_id(0)
    group, span = gate.shape
    rows = group // 4
    value = gate[...].astype(jnp.float32)
    hidden = value * jax.nn.sigmoid(value) * up[...].astype(jnp.float32)
    natural[...] = hidden.astype(jnp.bfloat16)
    ordered = [natural[pl.ds(token_start(place, b, rows), rows), :] for b in range(4)]
    columns[pl.ds(pl.multiple_of(step * span, 128), span), :] = jnp.concatenate(ordered, axis=0).T

    @pl.when(step == pl.num_programs(0) - 1)
    def _():
        half = units // 2
        for out, (k, first, count) in zip(outs, parts):
            for r in range(count):
                start = (place[0] ^ k) * units + (place[1] ^ (first + r)) * half
                out[r * half : (r + 1) * half, :] = columns[
                    pl.ds(pl.multiple_of(start, 16), half), :
                ]


def weight_kernel(place, codes, scales, *halves):
    span = codes.shape[1] // scales.shape[1]
    per_half = scales.shape[1] // 2
    for block in range(scales.shape[1]):
        value = codes[:, block * span : (block + 1) * span].astype(jnp.float32)
        value = (value * scales[:, block : block + 1]).astype(jnp.bfloat16)
        at = block % per_half * span
        halves[block // per_half][:, at : at + span] = value


def join_kernel(place, own_a, own_b, other_a, other_b, weight):
    half, middle = own_a.shape
    weight[:half, :middle] = own_a[...]
    weight[:half, middle:] = own_b[...]
    weight[half:, :middle] = other_a[...]
    weight[half:, middle:] = other_b[...]


def columns_kernel(parts, by_rows, by_lanes, place, *refs):
    pieces, (keep, send, *rest) = refs[: len(parts)], refs[len(parts) :]
    half, group = rest[0].shape[0], pieces[0].shape[1]
    rows = group // 4
    for piece, (k, first, count) in zip(pieces, parts):
        turned = piece[...].T
        row, lane = by_rows.index(k), by_lanes.index(k)
        lanes = slice(lane % 2 * group, (lane % 2 + 1) * group)
        for b in range(4):
            target = send if b >= 2 else keep
            start = ((b % 2) * len(by_rows) + row) * rows
            target[start : start + rows, first * half : (first + count) * half] = turned[
                b * rows : (b + 1) * rows, :
            ]
        for r in range(count):
            rest[lane // 2 * 2 + first + r][:, lanes] = piece[r * half : (r + 1) * half, :]


def grads_kernel(nz, units, place, gate, up, *refs):
    pieces, (gate_grad, up_grad, columns, natural) = refs[:nz], refs[nz:]
    step = pl.program_id(0)
    group, span = gate.shape
    rows = group // 4

    @pl.when(step == 0)
    def _():
        half = units // 2
        for k in range(nz):
            for r in range(2):
                start = (place[0] ^ k) * units + (place[1] ^ r) * half
                columns[pl.ds(pl.multiple_of(start, 16), half), :] = pieces[k][
                    r * half : (r + 1) * half, :
                ]

    ordered = columns[pl.ds(pl.multiple_of(step * span, 128), span), :].T
    for b in range(4):
        natural[pl.ds(token_start(place, b, rows), rows), :] = ordered[b * rows : (b + 1) * rows]
    dhidden = natural[...].astype(jnp.float32)
    value = gate[...].astype(jnp.float32)
    up_value = up[...].astype(jnp.float32)
    sigmoid_gate = jax.nn.sigmoid(value)
    gate_grad[...] = (
        dhidden * up_value * sigmoid_gate * (1.0 + value * (1.0 - sigmoid_gate))
    ).astype(jnp.bfloat16)
    up_grad[...] = (dhidden * (value * sigmoid_gate)).astype(jnp.bfloat16)


def matmul(lhs, rhs, lhs_dim=1, rhs_dim=0, dtype=jnp.float32):
    dims = (((lhs_dim,), (rhs_dim,)), ((), ()))
    return lax.dot_general(lhs, rhs, dims, preferred_element_type=jnp.float32).astype(dtype)


def paired_body(gate_pre, up_pre, down_codes, down_scales, cotangent):
    group_rows, local_hidden = gate_pre.shape
    owned, width = down_codes.shape
    rows = cotangent.shape[0]
    nz, units, middle = 4, 2 * owned, width // 2
    total_tokens = group_rows * nz * 2
    bf16, f32 = jnp.bfloat16, jnp.float32
    place = jnp.stack([lax.axis_index(name) for name in ("z", "x", "y", "c")]).astype(jnp.int32)
    struct = jax.ShapeDtypeStruct
    barrier = lax.optimization_barrier

    far = exchange(cotangent, "z", 2)

    own_a, own_b = call_kernel(
        weight_kernel, place, (down_codes, down_scales),
        [whole(down_codes.shape), whole(down_scales.shape)],
        [struct((owned, middle), bf16)] * 2, [whole((owned, middle))] * 2, (1,), [],
        (2 * owned * width, 4 * owned * width, 0),
    )
    other_a = exchange(own_a, "x", 1)

    parts = ((0, 0, 2), (1, 0, 2), (2, 0, 1), (3, 0, 1), (2, 1, 1), (3, 1, 1))
    pieces = [struct((count * owned, group_rows), bf16) for _, _, count in parts]
    piece_specs = [whole(piece.shape) for piece in pieces]
    span = column_span(local_hidden)
    steps = local_hidden // span
    wide = pl.BlockSpec((group_rows, span), lambda i, place: (0, i))
    act_bytes = group_rows * local_hidden * 2
    act_scratch = [pltpu.VMEM((group_rows, span), bf16), pltpu.VMEM((local_hidden, group_rows), bf16)]
    sent = call_kernel(
        functools.partial(hidden_kernel, parts, units), place, (gate_pre, up_pre), [wide] * 2,
        pieces, piece_specs, (steps,), act_scratch,
        (4 * act_bytes, 3 * act_bytes, act_bytes // 2),
    )

    far, sent = barrier((far, sent))
    even = jnp.stack([cotangent, far])
    odd = exchange(even, "z", 1)
    even_y = exchange(even, "y", 1)
    columns = [sent[0], None] + [exchange(sent[i], "z", parts[i][0]) for i in (2, 3)]
    odd, even_y, columns, other_a, sent, own_b = barrier((odd, even_y, columns, other_a, sent, own_b))

    odd_y = exchange(odd, "y", 1)
    other_b = exchange(own_b, "x", 1)
    columns[1] = exchange(sent[1], "z", 1)
    columns += [exchange(sent[i], "z", parts[i][0]) for i in (4, 5)]
    even_c = [even, even_y, exchange(even, "c", 1), exchange(even_y, "c", 1)]
    odd_c = exchange(odd, "c", 1)
    odd_y, columns, other_b = barrier((odd_y, columns, other_b))
    tile = column_span(middle)
    weight = call_kernel(
        join_kernel, place, (own_a, own_b, other_a, other_b), [whole((owned, middle))] * 4,
        struct((units, width), bf16), whole((units, width)), (1,), [],
        (0, 4 * units * width, 0),
    )

    half_tokens = nz * group_rows // 2
    by_rows, by_lanes = (1, 3, 0, 2), (0, 2, 1, 3)
    keep, send, *by_units = call_kernel(
        functools.partial(columns_kernel, parts, by_rows, by_lanes), place, columns, piece_specs,
        [struct((half_tokens, units), bf16)] * 2 + [struct((owned, half_tokens), bf16)] * 4,
        [whole((half_tokens, units))] * 2 + [whole((owned, half_tokens))] * 4, (1,), [],
        (0, 12 * units * half_tokens, 0),
    )

    odd_c = [odd, odd_y, odd_c, exchange(odd_y, "c", 1)]
    even_c, odd_c, send, keep = barrier((even_c, odd_c, send, keep))
    tokens = [jnp.stack(c, axis=1).reshape(2, group_rows, width) for c in (even_c, odd_c)]

    factor = float(total_tokens) ** (-0.5)
    flat = [t.reshape(half_tokens, width) for t in tokens]

    first_units, first_rows = units // 48 * 16, owned // 48 * 16

    def grad_half(r, low, high):
        near, far = by_units[r][low:high], by_units[2 + r][low:high]
        return (matmul(near, flat[0]) + matmul(far, flat[1])) * factor

    def back_of(k, low, high):
        return matmul(weight[low:high], tokens[k % 2][k // 2], 1, 1, bf16)

    far_first = [back_of(k, 0, first_units) for k in (2, 3)]
    far_last = [back_of(k, first_units, units) for k in (2, 3)]
    far_first, far_last, flat = barrier((far_first, far_last, flat))
    theirs = grad_half(1, 0, first_rows).astype(bf16), grad_half(1, first_rows, owned).astype(bf16)
    theirs, send, keep = barrier((theirs, send, keep))
    far_first = [exchange(value, "z", 2 + i) for i, value in enumerate(far_first)]
    over_x = [exchange(theirs[0], "x", 1)]
    over_c = exchange(matmul(send, weight, dtype=bf16), "c", 1)
    own_c = matmul(keep, weight, dtype=bf16)
    own_c, over_c, tokens = barrier((own_c, over_c, tokens))
    near_back = [back_of(0, 0, units), back_of(1, 0, units)]
    far_first, over_x, far_last, theirs, own_c, over_c = barrier(
        (far_first, over_x, far_last, theirs, own_c, over_c)
    )
    back = [near_back[0], exchange(near_back[1], "z", 1)]
    back += [
        jnp.concatenate([value, exchange(far_last[i], "z", 2 + i)])
        for i, value in enumerate(far_first)
    ]
    over_x.append(exchange(theirs[1], "x", 1))

    sums = (own_c.astype(f32) + over_c.astype(f32)).reshape(2, nz, rows, width)
    odd_sum = sums[0, :2] + exchange(sums[1, :2].astype(bf16), "y", 1).astype(f32)
    even_sum = sums[0, 2:] + exchange(sums[1, 2:].astype(bf16), "y", 1).astype(f32)
    near = exchange(odd_sum.astype(bf16), "z", 1).astype(f32)
    ours, across = even_sum[0] + near[0], (even_sum[1] + near[1]).astype(bf16)
    layer_out = (ours + exchange(across, "z", 2).astype(f32)).astype(bf16)

    weight_grad = grad_half(0, 0, owned) + jnp.concatenate(over_x).astype(f32)
    back, _ = barrier((back, across))
    gate_grad, up_grad = call_kernel(
        functools.partial(grads_kernel, nz, units), place, (gate_pre, up_pre, *back),
        [wide] * 2 + [whole((units, group_rows))] * nz,
        [struct((group_rows, local_hidden), bf16)] * 2, [wide] * 2, (steps,), act_scratch[::-1],
        (12 * act_bytes, 5 * act_bytes, act_bytes // 2),
    )
    return layer_out, gate_grad, up_grad, weight_grad


def column_span(width):
    return max((s for s in range(128, 641, 128) if width % s == 0), default=0)


def body(gate_pre, up_pre, down_codes, down_scales, cotangent):
    group_rows, local_hidden = gate_pre.shape
    owned, width = down_codes.shape
    nz, nx, ny, nc = (lax.axis_size(name) for name in ("z", "x", "y", "c"))
    rows = cotangent.shape[0]
    units = nx * owned
    total_tokens = group_rows * nz * nx

    gate_value = gate_pre.astype(jnp.float32)
    up_value = up_pre.astype(jnp.float32)
    sigmoid_gate = jax.nn.sigmoid(gate_value)
    activated = gate_value * sigmoid_gate
    hidden = (activated * up_value).astype(jnp.bfloat16)

    sent = hidden.T.reshape(nz, units, group_rows)
    columns = lax.all_to_all(sent, "z", 0, 0, tiled=True) if nz > 1 else sent

    line = lax.all_gather(cotangent, ("z", "y"), axis=0)
    both = gather_pair(line, "c")
    received = jnp.moveaxis(both, 0, 1).reshape(nz, group_rows, width)

    weight = gather_pair(dequantize(down_codes, down_scales), "x").reshape(units, width)

    partial_out = lax.dot_general(
        columns, weight, (((1,), (0,)), ((), ())), preferred_element_type=jnp.float32
    ).astype(jnp.bfloat16)
    partial_out = partial_out.reshape(nz, ny, nc, rows, width)
    over_c = scatter_sum(jnp.moveaxis(partial_out, 2, 0), "c")
    over_y = scatter_sum(jnp.moveaxis(over_c.astype(jnp.bfloat16), 1, 0), "y")
    layer_out = scatter_sum(over_y.astype(jnp.bfloat16), "z").astype(jnp.bfloat16)

    dcolumns = lax.dot_general(
        weight, received, (((1,), (2,)), ((), ())), preferred_element_type=jnp.float32
    ).astype(jnp.bfloat16)
    dcolumns = jnp.moveaxis(dcolumns, 1, 0)
    back = lax.all_to_all(dcolumns, "z", 0, 0, tiled=True) if nz > 1 else dcolumns
    dhidden = back.reshape(local_hidden, group_rows).T.astype(jnp.float32)
    gate_grad = (
        dhidden * up_value * sigmoid_gate * (1.0 + gate_value * (1.0 - sigmoid_gate))
    ).astype(jnp.bfloat16)
    up_grad = (dhidden * activated).astype(jnp.bfloat16)

    partial_grad = lax.dot_general(
        columns, received, (((0, 2), (0, 1)), ((), ())), preferred_element_type=jnp.float32
    )
    weight_grad = scatter_sum(partial_grad.reshape(nx, owned, width), "x") * float(total_tokens) ** (-0.5)
    return layer_out, gate_grad, up_grad, weight_grad


def outer_split(mesh, tokens, hidden, width):
    dp, tensor = mesh.shape["dp"], mesh.shape["tensor"]

    def rows_sent(nz):
        moved = 2 * (tokens // dp) * (hidden // tensor) / width if nz > 1 else 0
        return 2 * hidden // (tensor * nz) + 2 * tokens * nz // dp + moved

    return min((nz for nz in range(1, dp + 1) if dp % nz == 0), key=rows_sent)


def solution(mesh):
    def call(gate_pre, up_pre, down_codes, down_scales, cotangent):
        tokens, hidden = gate_pre.shape
        nz = outer_split(mesh, tokens, hidden, cotangent.shape[1])
        dp, tensor = mesh.shape["dp"], mesh.shape["tensor"]
        fine = Mesh(mesh.devices.reshape(nz, dp // nz, tensor // 2, 2), ("z", "x", "y", "c"))
        act = P(("z", "x"), ("y", "c"))
        weight = P(("y", "c", "z", "x"), None)
        layer = P(("z", "x", "y", "c"), None)
        owned = hidden // (dp * tensor)
        rows = tokens // (dp * tensor)
        pairs = fine.shape["x"] == 2 and fine.shape["y"] == 2 and nz == 4
        aligned = owned % 16 == 0 and rows % 16 == 0 and column_span(hidden // tensor)
        nblocks = down_scales.shape[1]
        blocks = nblocks % 2 == 0 and cotangent.shape[1] // nblocks % 128 == 0
        return jax.shard_map(
            paired_body if pairs and aligned and blocks else body,
            mesh=fine,
            in_specs=(act, act, weight, weight, layer),
            out_specs=(layer, act, act, weight),
            check_vma=False,
        )(gate_pre, up_pre, down_codes, down_scales, cotangent)

    return call
```

```python
import functools

import jax
import jax.numpy as jnp
from jax import lax
from jax.experimental import pallas as pl
from jax.experimental.pallas import tpu as pltpu
from jax.sharding import Mesh, PartitionSpec as P

VMEM_BYTES = 32 * 2**20


def dequantize(codes, scales):
    rows, width = codes.shape
    nblocks = scales.shape[1]
    blocks = codes.astype(jnp.float32).reshape(rows, nblocks, width // nblocks) * scales[:, :, None]
    return blocks.reshape(rows, width).astype(jnp.bfloat16)


def swap(value, axis):
    return lax.ppermute(value, axis, [(0, 1), (1, 0)])


def gather_pair(value, axis):
    if lax.axis_size(axis) != 2:
        return lax.all_gather(value, axis, axis=0)
    other = swap(value, axis)
    first = lax.axis_index(axis) == 0
    return jnp.stack([jnp.where(first, value, other), jnp.where(first, other, value)])


def scatter_sum(parts, axis):
    size = lax.axis_size(axis)
    if size == 1:
        return parts[0].astype(jnp.float32)
    if size != 2:
        received = lax.all_to_all(parts.astype(jnp.bfloat16), axis, 0, 0, tiled=True)
        return jnp.sum(received.astype(jnp.float32), axis=0)
    me = lax.axis_index(axis)
    theirs = lax.dynamic_index_in_dim(parts, 1 - me, 0, keepdims=False).astype(jnp.bfloat16)
    mine = lax.dynamic_index_in_dim(parts, me, 0, keepdims=False)
    return mine.astype(jnp.float32) + swap(theirs, axis).astype(jnp.float32)


def exchange(value, axis, offset):
    size = lax.axis_size(axis)
    return lax.ppermute(value, axis, [(i, i ^ offset) for i in range(size)])


def call_kernel(kernel, place, inputs, in_specs, out_shapes, out_specs, grid, scratch, cost):
    flops, nbytes, transcendentals = cost
    return pl.pallas_call(
        kernel,
        out_shape=out_shapes,
        grid_spec=pltpu.PrefetchScalarGridSpec(
            num_scalar_prefetch=1,
            grid=grid,
            in_specs=in_specs,
            out_specs=out_specs,
            scratch_shapes=scratch,
        ),
        compiler_params=pltpu.CompilerParams(vmem_limit_bytes=VMEM_BYTES),
        cost_estimate=pl.CostEstimate(
            flops=flops, bytes_accessed=nbytes, transcendentals=transcendentals
        ),
    )(place, *inputs)


def whole(shape):
    return pl.BlockSpec(shape, lambda i, place: (0,) * len(shape))


def token_start(place, block, rows):
    return pl.multiple_of(((place[2] ^ (block % 2)) * 2 + (place[3] ^ (block // 2))) * rows, 16)


def hidden_kernel(parts, units, place, gate, up, *refs):
    outs, (natural, columns) = refs[: len(parts)], refs[len(parts) :]
    step = pl.program_id(0)
    group, span = gate.shape
    rows = group // 4
    value = gate[...].astype(jnp.float32)
    hidden = value * jax.nn.sigmoid(value) * up[...].astype(jnp.float32)
    natural[...] = hidden.astype(jnp.bfloat16)
    ordered = [natural[pl.ds(token_start(place, b, rows), rows), :] for b in range(4)]
    columns[pl.ds(pl.multiple_of(step * span, 128), span), :] = jnp.concatenate(ordered, axis=0).T

    @pl.when(step == pl.num_programs(0) - 1)
    def _():
        half = units // 2
        for out, (k, first, count) in zip(outs, parts):
            for r in range(count):
                start = (place[0] ^ k) * units + (place[1] ^ (first + r)) * half
                out[r * half : (r + 1) * half, :] = columns[
                    pl.ds(pl.multiple_of(start, 16), half), :
                ]


def weight_kernel(place, codes, scales, *halves):
    span = codes.shape[1] // scales.shape[1]
    per_half = scales.shape[1] // 2
    for block in range(scales.shape[1]):
        value = codes[:, block * span : (block + 1) * span].astype(jnp.float32)
        value = (value * scales[:, block : block + 1]).astype(jnp.bfloat16)
        at = block % per_half * span
        halves[block // per_half][:, at : at + span] = value


def join_kernel(place, own_a, own_b, other_a, other_b, weight):
    half, middle = own_a.shape
    weight[:half, :middle] = own_a[...]
    weight[:half, middle:] = own_b[...]
    weight[half:, :middle] = other_a[...]
    weight[half:, middle:] = other_b[...]


def columns_kernel(parts, by_rows, by_lanes, place, *refs):
    pieces, (keep, send, *rest) = refs[: len(parts)], refs[len(parts) :]
    half, group = rest[0].shape[0], pieces[0].shape[1]
    rows = group // 4
    for piece, (k, first, count) in zip(pieces, parts):
        turned = piece[...].T
        row, lane = by_rows.index(k), by_lanes.index(k)
        lanes = slice(lane % 2 * group, (lane % 2 + 1) * group)
        for b in range(4):
            target = send if b >= 2 else keep
            start = ((b % 2) * len(by_rows) + row) * rows
            target[start : start + rows, first * half : (first + count) * half] = turned[
                b * rows : (b + 1) * rows, :
            ]
        for r in range(count):
            rest[lane // 2 * 2 + first + r][:, lanes] = piece[r * half : (r + 1) * half, :]


def grads_kernel(nz, units, place, gate, up, *refs):
    pieces, (gate_grad, up_grad, columns, natural) = refs[:nz], refs[nz:]
    step = pl.program_id(0)
    group, span = gate.shape
    rows = group // 4

    @pl.when(step == 0)
    def _():
        half = units // 2
        for k in range(nz):
            for r in range(2):
                start = (place[0] ^ k) * units + (place[1] ^ r) * half
                columns[pl.ds(pl.multiple_of(start, 16), half), :] = pieces[k][
                    r * half : (r + 1) * half, :
                ]

    ordered = columns[pl.ds(pl.multiple_of(step * span, 128), span), :].T
    for b in range(4):
        natural[pl.ds(token_start(place, b, rows), rows), :] = ordered[b * rows : (b + 1) * rows]
    dhidden = natural[...].astype(jnp.float32)
    value = gate[...].astype(jnp.float32)
    up_value = up[...].astype(jnp.float32)
    sigmoid_gate = jax.nn.sigmoid(value)
    gate_grad[...] = (
        dhidden * up_value * sigmoid_gate * (1.0 + value * (1.0 - sigmoid_gate))
    ).astype(jnp.bfloat16)
    up_grad[...] = (dhidden * (value * sigmoid_gate)).astype(jnp.bfloat16)


def matmul(lhs, rhs, lhs_dim=1, rhs_dim=0, dtype=jnp.float32):
    dims = (((lhs_dim,), (rhs_dim,)), ((), ()))
    return lax.dot_general(lhs, rhs, dims, preferred_element_type=jnp.float32).astype(dtype)


def paired_body(gate_pre, up_pre, down_codes, down_scales, cotangent):
    group_rows, local_hidden = gate_pre.shape
    owned, width = down_codes.shape
    rows = cotangent.shape[0]
    nz, units, middle = 4, 2 * owned, width // 2
    total_tokens = group_rows * nz * 2
    bf16, f32 = jnp.bfloat16, jnp.float32
    place = jnp.stack([lax.axis_index(name) for name in ("z", "x", "y", "c")]).astype(jnp.int32)
    struct = jax.ShapeDtypeStruct
    barrier = lax.optimization_barrier

    far = exchange(cotangent, "z", 2)

    own_a, own_b = call_kernel(
        weight_kernel, place, (down_codes, down_scales),
        [whole(down_codes.shape), whole(down_scales.shape)],
        [struct((owned, middle), bf16)] * 2, [whole((owned, middle))] * 2, (1,), [],
        (2 * owned * width, 4 * owned * width, 0),
    )
    other_a = exchange(own_a, "x", 1)

    parts = ((0, 0, 2), (2, 0, 2), (3, 0, 2), (1, 0, 1), (1, 1, 1))
    pieces = [struct((count * owned, group_rows), bf16) for _, _, count in parts]
    piece_specs = [whole(piece.shape) for piece in pieces]
    span = column_span(local_hidden)
    steps = local_hidden // span
    wide = pl.BlockSpec((group_rows, span), lambda i, place: (0, i))
    act_bytes = group_rows * local_hidden * 2
    act_scratch = [pltpu.VMEM((group_rows, span), bf16), pltpu.VMEM((local_hidden, group_rows), bf16)]
    sent = call_kernel(
        functools.partial(hidden_kernel, parts, units), place, (gate_pre, up_pre), [wide] * 2,
        pieces, piece_specs, (steps,), act_scratch,
        (4 * act_bytes, 3 * act_bytes, act_bytes // 2),
    )

    far, sent = barrier((far, sent))
    even = jnp.stack([cotangent, far])
    odd = exchange(even, "z", 1)
    even_y = exchange(even, "y", 1)
    columns = [sent[0], exchange(sent[1], "z", 2)]
    odd, even_y, columns, other_a, sent, own_b = barrier((odd, even_y, columns, other_a, sent, own_b))

    odd_y = exchange(odd, "y", 1)
    other_b = exchange(own_b, "x", 1)
    columns += [exchange(sent[i], "z", parts[i][0]) for i in range(2, len(parts))]
    even_c = [even, even_y, exchange(even, "c", 1), exchange(even_y, "c", 1)]
    odd_c = exchange(odd, "c", 1)
    odd_y, columns, other_b = barrier((odd_y, columns, other_b))
    tile = column_span(middle)
    weight = call_kernel(
        join_kernel, place, (own_a, own_b, other_a, other_b), [whole((owned, middle))] * 4,
        struct((units, width), bf16), whole((units, width)), (1,), [],
        (0, 4 * units * width, 0),
    )

    half_tokens = nz * group_rows // 2
    by_rows, by_lanes = (1, 3, 0, 2), (0, 2, 1, 3)
    keep, send, *by_units = call_kernel(
        functools.partial(columns_kernel, parts, by_rows, by_lanes), place, columns, piece_specs,
        [struct((half_tokens, units), bf16)] * 2 + [struct((owned, half_tokens), bf16)] * 4,
        [whole((half_tokens, units))] * 2 + [whole((owned, half_tokens))] * 4, (1,), [],
        (0, 12 * units * half_tokens, 0),
    )

    odd_c = [odd, odd_y, odd_c, exchange(odd_y, "c", 1)]
    tokens = [jnp.stack(c, axis=1).reshape(2, group_rows, width) for c in (even_c, odd_c)]

    factor = float(total_tokens) ** (-0.5)
    flat = [t.reshape(half_tokens, width) for t in tokens]


    def grad_half(r):
        return (matmul(by_units[r], flat[0]) + matmul(by_units[2 + r], flat[1])) * factor

    def back_of(k):
        value = matmul(weight, tokens[k % 2][k // 2], 1, 1, bf16)
        return exchange(value, "z", k) if k else value

    over_c = exchange(matmul(send, weight, dtype=bf16), "c", 1)
    own_c = matmul(keep, weight, dtype=bf16)
    sums = (own_c.astype(f32) + over_c.astype(f32)).reshape(2, nz, rows, width)
    odd_y = exchange(sums[1, :2].astype(bf16), "y", 1)
    even_y = exchange(sums[1, 2:].astype(bf16), "y", 1)
    over_x = exchange(grad_half(1).astype(bf16), "x", 1)
    back = [back_of(k) for k in range(nz)]
    odd_sum = (sums[0, :2] + odd_y.astype(f32)).astype(bf16)
    odd_sum, back[2] = barrier((odd_sum, back[2]))
    even_y, _ = barrier((even_y, odd_sum))
    near = exchange(odd_sum, "z", 1).astype(f32)
    even_sum = sums[0, 2:] + even_y.astype(f32)
    ours, across = even_sum[0] + near[0], (even_sum[1] + near[1]).astype(bf16)
    across, back[3] = barrier((across, back[3]))
    layer_out = (ours + exchange(across, "z", 2).astype(f32)).astype(bf16)

    weight_grad = grad_half(0) + over_x.astype(f32)
    back, _ = barrier((back, across))
    gate_grad, up_grad = call_kernel(
        functools.partial(grads_kernel, nz, units), place, (gate_pre, up_pre, *back),
        [wide] * 2 + [whole((units, group_rows))] * nz,
        [struct((group_rows, local_hidden), bf16)] * 2, [wide] * 2, (steps,), act_scratch[::-1],
        (12 * act_bytes, 5 * act_bytes, act_bytes // 2),
    )
    return layer_out, gate_grad, up_grad, weight_grad


def column_span(width):
    return max((s for s in range(128, 641, 128) if width % s == 0), default=0)


def body(gate_pre, up_pre, down_codes, down_scales, cotangent):
    group_rows, local_hidden = gate_pre.shape
    owned, width = down_codes.shape
    nz, nx, ny, nc = (lax.axis_size(name) for name in ("z", "x", "y", "c"))
    rows = cotangent.shape[0]
    units = nx * owned
    total_tokens = group_rows * nz * nx

    gate_value = gate_pre.astype(jnp.float32)
    up_value = up_pre.astype(jnp.float32)
    sigmoid_gate = jax.nn.sigmoid(gate_value)
    activated = gate_value * sigmoid_gate
    hidden = (activated * up_value).astype(jnp.bfloat16)

    sent = hidden.T.reshape(nz, units, group_rows)
    columns = lax.all_to_all(sent, "z", 0, 0, tiled=True) if nz > 1 else sent

    line = lax.all_gather(cotangent, ("z", "y"), axis=0)
    both = gather_pair(line, "c")
    received = jnp.moveaxis(both, 0, 1).reshape(nz, group_rows, width)

    weight = gather_pair(dequantize(down_codes, down_scales), "x").reshape(units, width)

    partial_out = lax.dot_general(
        columns, weight, (((1,), (0,)), ((), ())), preferred_element_type=jnp.float32
    ).astype(jnp.bfloat16)
    partial_out = partial_out.reshape(nz, ny, nc, rows, width)
    over_c = scatter_sum(jnp.moveaxis(partial_out, 2, 0), "c")
    over_y = scatter_sum(jnp.moveaxis(over_c.astype(jnp.bfloat16), 1, 0), "y")
    layer_out = scatter_sum(over_y.astype(jnp.bfloat16), "z").astype(jnp.bfloat16)

    dcolumns = lax.dot_general(
        weight, received, (((1,), (2,)), ((), ())), preferred_element_type=jnp.float32
    ).astype(jnp.bfloat16)
    dcolumns = jnp.moveaxis(dcolumns, 1, 0)
    back = lax.all_to_all(dcolumns, "z", 0, 0, tiled=True) if nz > 1 else dcolumns
    dhidden = back.reshape(local_hidden, group_rows).T.astype(jnp.float32)
    gate_grad = (
        dhidden * up_value * sigmoid_gate * (1.0 + gate_value * (1.0 - sigmoid_gate))
    ).astype(jnp.bfloat16)
    up_grad = (dhidden * activated).astype(jnp.bfloat16)

    partial_grad = lax.dot_general(
        columns, received, (((0, 2), (0, 1)), ((), ())), preferred_element_type=jnp.float32
    )
    weight_grad = scatter_sum(partial_grad.reshape(nx, owned, width), "x") * float(total_tokens) ** (-0.5)
    return layer_out, gate_grad, up_grad, weight_grad


def outer_split(mesh, tokens, hidden, width):
    dp, tensor = mesh.shape["dp"], mesh.shape["tensor"]

    def rows_sent(nz):
        moved = 2 * (tokens // dp) * (hidden // tensor) / width if nz > 1 else 0
        return 2 * hidden // (tensor * nz) + 2 * tokens * nz // dp + moved

    return min((nz for nz in range(1, dp + 1) if dp % nz == 0), key=rows_sent)


def solution(mesh):
    def call(gate_pre, up_pre, down_codes, down_scales, cotangent):
        tokens, hidden = gate_pre.shape
        nz = outer_split(mesh, tokens, hidden, cotangent.shape[1])
        dp, tensor = mesh.shape["dp"], mesh.shape["tensor"]
        fine = Mesh(mesh.devices.reshape(nz, dp // nz, tensor // 2, 2), ("z", "x", "y", "c"))
        act = P(("z", "x"), ("y", "c"))
        weight = P(("y", "c", "z", "x"), None)
        layer = P(("z", "x", "y", "c"), None)
        owned = hidden // (dp * tensor)
        rows = tokens // (dp * tensor)
        pairs = fine.shape["x"] == 2 and fine.shape["y"] == 2 and nz == 4
        aligned = owned % 16 == 0 and rows % 16 == 0 and column_span(hidden // tensor)
        nblocks = down_scales.shape[1]
        blocks = nblocks % 2 == 0 and cotangent.shape[1] // nblocks % 128 == 0
        return jax.shard_map(
            paired_body if pairs and aligned and blocks else body,
            mesh=fine,
            in_specs=(act, act, weight, weight, layer),
            out_specs=(layer, act, act, weight),
            check_vma=False,
        )(gate_pre, up_pre, down_codes, down_scales, cotangent)

    return call
```

```python
import functools

import jax
import jax.numpy as jnp
from jax import lax
from jax.experimental import pallas as pl
from jax.experimental.pallas import tpu as pltpu
from jax.sharding import Mesh, PartitionSpec as P

VMEM_BYTES = 32 * 2**20


def dequantize(codes, scales):
    rows, width = codes.shape
    nblocks = scales.shape[1]
    blocks = codes.astype(jnp.float32).reshape(rows, nblocks, width // nblocks) * scales[:, :, None]
    return blocks.reshape(rows, width).astype(jnp.bfloat16)


def swap(value, axis):
    return lax.ppermute(value, axis, [(0, 1), (1, 0)])


def gather_pair(value, axis):
    if lax.axis_size(axis) != 2:
        return lax.all_gather(value, axis, axis=0)
    other = swap(value, axis)
    first = lax.axis_index(axis) == 0
    return jnp.stack([jnp.where(first, value, other), jnp.where(first, other, value)])


def scatter_sum(parts, axis):
    size = lax.axis_size(axis)
    if size == 1:
        return parts[0].astype(jnp.float32)
    if size != 2:
        received = lax.all_to_all(parts.astype(jnp.bfloat16), axis, 0, 0, tiled=True)
        return jnp.sum(received.astype(jnp.float32), axis=0)
    me = lax.axis_index(axis)
    theirs = lax.dynamic_index_in_dim(parts, 1 - me, 0, keepdims=False).astype(jnp.bfloat16)
    mine = lax.dynamic_index_in_dim(parts, me, 0, keepdims=False)
    return mine.astype(jnp.float32) + swap(theirs, axis).astype(jnp.float32)


def exchange(value, axis, offset):
    size = lax.axis_size(axis)
    return lax.ppermute(value, axis, [(i, i ^ offset) for i in range(size)])


def call_kernel(kernel, place, inputs, in_specs, out_shapes, out_specs, grid, scratch, cost):
    flops, nbytes, transcendentals = cost
    return pl.pallas_call(
        kernel,
        out_shape=out_shapes,
        grid_spec=pltpu.PrefetchScalarGridSpec(
            num_scalar_prefetch=1,
            grid=grid,
            in_specs=in_specs,
            out_specs=out_specs,
            scratch_shapes=scratch,
        ),
        compiler_params=pltpu.CompilerParams(vmem_limit_bytes=VMEM_BYTES),
        cost_estimate=pl.CostEstimate(
            flops=flops, bytes_accessed=nbytes, transcendentals=transcendentals
        ),
    )(place, *inputs)


def whole(shape):
    return pl.BlockSpec(shape, lambda i, place: (0,) * len(shape))


def token_start(place, block, rows):
    return pl.multiple_of(((place[2] ^ (block % 2)) * 2 + (place[3] ^ (block // 2))) * rows, 16)


def hidden_kernel(parts, units, place, gate, up, *refs):
    outs, (natural, columns) = refs[: len(parts)], refs[len(parts) :]
    step = pl.program_id(0)
    group, span = gate.shape
    rows = group // 4
    value = gate[...].astype(jnp.float32)
    hidden = value * jax.nn.sigmoid(value) * up[...].astype(jnp.float32)
    natural[...] = hidden.astype(jnp.bfloat16)
    ordered = [natural[pl.ds(token_start(place, b, rows), rows), :] for b in range(4)]
    columns[pl.ds(pl.multiple_of(step * span, 128), span), :] = jnp.concatenate(ordered, axis=0).T

    @pl.when(step == pl.num_programs(0) - 1)
    def _():
        half = units // 2
        for out, (k, first, count) in zip(outs, parts):
            for r in range(count):
                start = (place[0] ^ k) * units + (place[1] ^ (first + r)) * half
                out[r * half : (r + 1) * half, :] = columns[
                    pl.ds(pl.multiple_of(start, 16), half), :
                ]


def weight_kernel(place, codes, scales, *halves):
    span = codes.shape[1] // scales.shape[1]
    for block in range(scales.shape[1]):
        value = codes[:, block * span : (block + 1) * span].astype(jnp.float32)
        value = (value * scales[:, block : block + 1]).astype(jnp.bfloat16)
        at = block * span
        half, at = (0, at) if at < halves[0].shape[1] else (1, at - halves[0].shape[1])
        halves[half][:, at : at + span] = value


def join_kernel(place, own_a, own_b, other_a, other_b, weight):
    half, middle = own_a.shape
    weight[:half, :middle] = own_a[...]
    weight[:half, middle:] = own_b[...]
    weight[half:, :middle] = other_a[...]
    weight[half:, middle:] = other_b[...]


def tokens_kernel(picks, place, *refs):
    tokens = refs[-1]
    rows = refs[0].shape[-2]
    for at, (array, block) in enumerate(picks):
        source = refs[array]
        tokens[at * rows : (at + 1) * rows, :] = source[block] if len(source.shape) == 3 else source[...]


def columns_kernel(parts, by_rows, by_lanes, place, *refs):
    pieces, (keep, send, *rest) = refs[: len(parts)], refs[len(parts) :]
    half, group = rest[0].shape[0], pieces[0].shape[1]
    rows = group // 4
    for piece, (k, first, count) in zip(pieces, parts):
        turned = piece[...].T
        row, lane = by_rows.index(k), by_lanes.index(k)
        lanes = slice(lane % 2 * group, (lane % 2 + 1) * group)
        for b in range(4):
            target = send if b >= 2 else keep
            start = ((b % 2) * len(by_rows) + row) * rows
            target[start : start + rows, first * half : (first + count) * half] = turned[
                b * rows : (b + 1) * rows, :
            ]
        for r in range(count):
            rest[lane // 2 * 2 + first + r][:, lanes] = piece[r * half : (r + 1) * half, :]


def grads_kernel(nz, units, place, gate, up, *refs):
    pieces, (gate_grad, up_grad, columns, natural) = refs[:nz], refs[nz:]
    step = pl.program_id(0)
    group, span = gate.shape
    rows = group // 4

    @pl.when(step == 0)
    def _():
        half = units // 2
        for k in range(nz):
            for r in range(2):
                start = (place[0] ^ k) * units + (place[1] ^ r) * half
                columns[pl.ds(pl.multiple_of(start, 16), half), :] = pieces[k][
                    r * half : (r + 1) * half, :
                ]

    ordered = columns[pl.ds(pl.multiple_of(step * span, 128), span), :].T
    for b in range(4):
        natural[pl.ds(token_start(place, b, rows), rows), :] = ordered[b * rows : (b + 1) * rows]
    dhidden = natural[...].astype(jnp.float32)
    value = gate[...].astype(jnp.float32)
    up_value = up[...].astype(jnp.float32)
    sigmoid_gate = jax.nn.sigmoid(value)
    gate_grad[...] = (
        dhidden * up_value * sigmoid_gate * (1.0 + value * (1.0 - sigmoid_gate))
    ).astype(jnp.bfloat16)
    up_grad[...] = (dhidden * (value * sigmoid_gate)).astype(jnp.bfloat16)


def matmul(lhs, rhs, lhs_dim=1, rhs_dim=0, dtype=jnp.float32):
    dims = (((lhs_dim,), (rhs_dim,)), ((), ()))
    return lax.dot_general(lhs, rhs, dims, preferred_element_type=jnp.float32).astype(dtype)


def paired_body(gate_pre, up_pre, down_codes, down_scales, cotangent):
    group_rows, local_hidden = gate_pre.shape
    owned, width = down_codes.shape
    rows = cotangent.shape[0]
    nz, units, nblocks = 4, 2 * owned, down_scales.shape[1]
    middle = 3 * nblocks // 5 * (width // nblocks)
    total_tokens = group_rows * nz * 2
    bf16, f32 = jnp.bfloat16, jnp.float32
    place = jnp.stack([lax.axis_index(name) for name in ("z", "x", "y", "c")]).astype(jnp.int32)
    struct = jax.ShapeDtypeStruct
    barrier = lax.optimization_barrier

    far, near = exchange(cotangent, "z", 2), exchange(cotangent, "z", 1)
    own_y, own_c = exchange(cotangent, "y", 1), exchange(cotangent, "c", 1)

    sides = ((owned, middle), (owned, width - middle))
    own_a, own_b = call_kernel(
        weight_kernel, place, (down_codes, down_scales),
        [whole(down_codes.shape), whole(down_scales.shape)],
        [struct(shape, bf16) for shape in sides], [whole(shape) for shape in sides], (1,), [],
        (2 * owned * width, 4 * owned * width, 0),
    )
    other_a = exchange(own_a, "x", 1)

    parts = tuple((k, 0, 2) for k in (0, 2, 3, 1))
    pieces = [struct((count * owned, group_rows), bf16) for _, _, count in parts]
    piece_specs = [whole(piece.shape) for piece in pieces]
    span = column_span(local_hidden)
    steps = local_hidden // span
    wide = pl.BlockSpec((group_rows, span), lambda i, place: (0, i))
    act_bytes = group_rows * local_hidden * 2
    act_scratch = [pltpu.VMEM((group_rows, span), bf16), pltpu.VMEM((local_hidden, group_rows), bf16)]
    sent = call_kernel(
        functools.partial(hidden_kernel, parts, units), place, (gate_pre, up_pre), [wide] * 2,
        pieces, piece_specs, (steps,), act_scratch,
        (4 * act_bytes, 3 * act_bytes, act_bytes // 2),
    )

    far, near, own_y, own_c, sent = barrier((far, near, own_y, own_c, sent))
    last = exchange(far, "z", 1)
    other_y = exchange(jnp.stack([far, near]), "y", 1)
    other_b = exchange(own_b, "x", 1)
    columns = [sent[0], exchange(sent[1], "z", 2)]
    first_c = exchange(jnp.stack([own_y, far, near]), "c", 1)
    last, other_y, columns, other_a, sent, first_c = barrier(
        (last, other_y, columns, other_a, sent, first_c)
    )

    last_y = exchange(last, "y", 1)
    columns += [exchange(sent[i], "z", parts[i][0]) for i in range(2, len(parts))]
    other_c = exchange(jnp.stack([other_y[0], other_y[1], last]), "c", 1)
    last_y, columns, other_b = barrier((last_y, columns, other_b))
    last_c = exchange(last_y, "c", 1)

    weight = call_kernel(
        join_kernel, place, (own_a, own_b, other_a, other_b),
        [whole(shape) for shape in sides] * 2,
        struct((units, width), bf16), whole((units, width)), (1,), [],
        (0, 4 * units * width, 0),
    )

    half_tokens = nz * group_rows // 2
    by_rows, by_lanes = (1, 3, 0, 2), (0, 2, 1, 3)
    keep, send, *by_units = call_kernel(
        functools.partial(columns_kernel, parts, by_rows, by_lanes), place, columns, piece_specs,
        [struct((half_tokens, units), bf16)] * 2 + [struct((owned, half_tokens), bf16)] * 4,
        [whole((half_tokens, units))] * 2 + [whole((owned, half_tokens))] * 4, (1,), [],
        (0, 12 * units * half_tokens, 0),
    )

    def gather_tokens(arrays, picks):
        return call_kernel(
            functools.partial(tokens_kernel, picks), place, arrays,
            [whole(array.shape) for array in arrays], struct((half_tokens, width), bf16),
            whole((half_tokens, width)), (1,), [], (0, 4 * half_tokens * width, 0),
        )

    even = gather_tokens(
        (cotangent, own_y, own_c, far, other_y, first_c, other_c),
        ((0, 0), (1, 0), (2, 0), (5, 0), (3, 0), (4, 0), (5, 1), (6, 0)),
    )
    odd = gather_tokens(
        (near, last, last_y, other_y, first_c, other_c, last_c),
        ((0, 0), (3, 1), (4, 2), (5, 1), (1, 0), (2, 0), (5, 2), (6, 0)),
    )
    even, odd, send, keep = barrier((even, odd, send, keep))
    flat = [even, odd]

    factor = float(total_tokens) ** (-0.5)


    def grad_half(r):
        return (matmul(by_units[r], flat[0]) + matmul(by_units[2 + r], flat[1])) * factor

    def back_of(k):
        rows_of_k = flat[k % 2][k // 2 * group_rows : (k // 2 + 1) * group_rows]
        return matmul(weight, rows_of_k, 1, 1, bf16)

    over_c = exchange(matmul(send, weight, dtype=bf16), "c", 1)
    back = [None, None, back_of(2), None]
    back[2], flat = barrier((back[2], flat))
    theirs = grad_half(1).astype(bf16)
    theirs, keep, flat = barrier((theirs, keep, flat))
    over_x = exchange(theirs, "x", 1)
    kept = matmul(keep, weight, dtype=bf16)
    back = [back_of(0), back_of(1), back[2], back_of(3)]
    back = [back[0]] + [exchange(back[k], "z", k) for k in range(1, nz)]
    sums = (kept.astype(f32) + over_c.astype(f32)).reshape(2, nz, rows, width)
    odd_y = exchange(sums[1, :2].astype(bf16), "y", 1)
    even_y = exchange(sums[1, 2:].astype(bf16), "y", 1)
    odd_sum = (sums[0, :2] + odd_y.astype(f32)).astype(bf16)
    odd_sum, back[2] = barrier((odd_sum, back[2]))
    even_y, _ = barrier((even_y, odd_sum))
    near_sum = exchange(odd_sum, "z", 1).astype(f32)
    even_sum = sums[0, 2:] + even_y.astype(f32)
    ours, across = even_sum[0] + near_sum[0], (even_sum[1] + near_sum[1]).astype(bf16)
    across, back[3] = barrier((across, back[3]))
    layer_out = (ours + exchange(across, "z", 2).astype(f32)).astype(bf16)

    back, _ = barrier((back, across))
    gate_grad, up_grad = call_kernel(
        functools.partial(grads_kernel, nz, units), place, (gate_pre, up_pre, *back),
        [wide] * 2 + [whole((units, group_rows))] * nz,
        [struct((group_rows, local_hidden), bf16)] * 2, [wide] * 2, (steps,), act_scratch[::-1],
        (12 * act_bytes, 5 * act_bytes, act_bytes // 2),
    )
    over_x, _ = barrier((over_x, gate_grad))
    weight_grad = grad_half(0) + over_x.astype(f32)
    return layer_out, gate_grad, up_grad, weight_grad


def column_span(width):
    return max((s for s in range(128, 641, 128) if width % s == 0), default=0)


def body(gate_pre, up_pre, down_codes, down_scales, cotangent):
    group_rows, local_hidden = gate_pre.shape
    owned, width = down_codes.shape
    nz, nx, ny, nc = (lax.axis_size(name) for name in ("z", "x", "y", "c"))
    rows = cotangent.shape[0]
    units = nx * owned
    total_tokens = group_rows * nz * nx

    gate_value = gate_pre.astype(jnp.float32)
    up_value = up_pre.astype(jnp.float32)
    sigmoid_gate = jax.nn.sigmoid(gate_value)
    activated = gate_value * sigmoid_gate
    hidden = (activated * up_value).astype(jnp.bfloat16)

    sent = hidden.T.reshape(nz, units, group_rows)
    columns = lax.all_to_all(sent, "z", 0, 0, tiled=True) if nz > 1 else sent

    line = lax.all_gather(cotangent, ("z", "y"), axis=0)
    both = gather_pair(line, "c")
    received = jnp.moveaxis(both, 0, 1).reshape(nz, group_rows, width)

    weight = gather_pair(dequantize(down_codes, down_scales), "x").reshape(units, width)

    partial_out = lax.dot_general(
        columns, weight, (((1,), (0,)), ((), ())), preferred_element_type=jnp.float32
    ).astype(jnp.bfloat16)
    partial_out = partial_out.reshape(nz, ny, nc, rows, width)
    over_c = scatter_sum(jnp.moveaxis(partial_out, 2, 0), "c")
    over_y = scatter_sum(jnp.moveaxis(over_c.astype(jnp.bfloat16), 1, 0), "y")
    layer_out = scatter_sum(over_y.astype(jnp.bfloat16), "z").astype(jnp.bfloat16)

    dcolumns = lax.dot_general(
        weight, received, (((1,), (2,)), ((), ())), preferred_element_type=jnp.float32
    ).astype(jnp.bfloat16)
    dcolumns = jnp.moveaxis(dcolumns, 1, 0)
    back = lax.all_to_all(dcolumns, "z", 0, 0, tiled=True) if nz > 1 else dcolumns
    dhidden = back.reshape(local_hidden, group_rows).T.astype(jnp.float32)
    gate_grad = (
        dhidden * up_value * sigmoid_gate * (1.0 + gate_value * (1.0 - sigmoid_gate))
    ).astype(jnp.bfloat16)
    up_grad = (dhidden * activated).astype(jnp.bfloat16)

    partial_grad = lax.dot_general(
        columns, received, (((0, 2), (0, 1)), ((), ())), preferred_element_type=jnp.float32
    )
    weight_grad = scatter_sum(partial_grad.reshape(nx, owned, width), "x") * float(total_tokens) ** (-0.5)
    return layer_out, gate_grad, up_grad, weight_grad


def outer_split(mesh, tokens, hidden, width):
    dp, tensor = mesh.shape["dp"], mesh.shape["tensor"]

    def rows_sent(nz):
        moved = 2 * (tokens // dp) * (hidden // tensor) / width if nz > 1 else 0
        return 2 * hidden // (tensor * nz) + 2 * tokens * nz // dp + moved

    return min((nz for nz in range(1, dp + 1) if dp % nz == 0), key=rows_sent)


def solution(mesh):
    def call(gate_pre, up_pre, down_codes, down_scales, cotangent):
        tokens, hidden = gate_pre.shape
        nz = outer_split(mesh, tokens, hidden, cotangent.shape[1])
        dp, tensor = mesh.shape["dp"], mesh.shape["tensor"]
        fine = Mesh(mesh.devices.reshape(nz, dp // nz, tensor // 2, 2), ("z", "x", "y", "c"))
        act = P(("z", "x"), ("y", "c"))
        weight = P(("y", "c", "z", "x"), None)
        layer = P(("z", "x", "y", "c"), None)
        owned = hidden // (dp * tensor)
        rows = tokens // (dp * tensor)
        pairs = fine.shape["x"] == 2 and fine.shape["y"] == 2 and nz == 4
        aligned = owned % 16 == 0 and rows % 16 == 0 and column_span(hidden // tensor)
        nblocks = down_scales.shape[1]
        blocks = nblocks > 2 and cotangent.shape[1] // nblocks % 128 == 0
        return jax.shard_map(
            paired_body if pairs and aligned and blocks else body,
            mesh=fine,
            in_specs=(act, act, weight, weight, layer),
            out_specs=(layer, act, act, weight),
            check_vma=False,
        )(gate_pre, up_pre, down_codes, down_scales, cotangent)

    return call
```

```python
import functools

import jax
import jax.numpy as jnp
from jax import lax
from jax.experimental import pallas as pl
from jax.experimental.pallas import tpu as pltpu
from jax.sharding import Mesh, PartitionSpec as P

VMEM_BYTES = 32 * 2**20


def dequantize(codes, scales):
    rows, width = codes.shape
    nblocks = scales.shape[1]
    blocks = codes.astype(jnp.float32).reshape(rows, nblocks, width // nblocks) * scales[:, :, None]
    return blocks.reshape(rows, width).astype(jnp.bfloat16)


def swap(value, axis):
    return lax.ppermute(value, axis, [(0, 1), (1, 0)])


def gather_pair(value, axis):
    if lax.axis_size(axis) != 2:
        return lax.all_gather(value, axis, axis=0)
    other = swap(value, axis)
    first = lax.axis_index(axis) == 0
    return jnp.stack([jnp.where(first, value, other), jnp.where(first, other, value)])


def scatter_sum(parts, axis):
    size = lax.axis_size(axis)
    if size == 1:
        return parts[0].astype(jnp.float32)
    if size != 2:
        received = lax.all_to_all(parts.astype(jnp.bfloat16), axis, 0, 0, tiled=True)
        return jnp.sum(received.astype(jnp.float32), axis=0)
    me = lax.axis_index(axis)
    theirs = lax.dynamic_index_in_dim(parts, 1 - me, 0, keepdims=False).astype(jnp.bfloat16)
    mine = lax.dynamic_index_in_dim(parts, me, 0, keepdims=False)
    return mine.astype(jnp.float32) + swap(theirs, axis).astype(jnp.float32)


def exchange(value, axis, offset):
    size = lax.axis_size(axis)
    return lax.ppermute(value, axis, [(i, i ^ offset) for i in range(size)])


def call_kernel(kernel, place, inputs, in_specs, out_shapes, out_specs, grid, scratch, cost):
    flops, nbytes, transcendentals = cost
    return pl.pallas_call(
        kernel,
        out_shape=out_shapes,
        grid_spec=pltpu.PrefetchScalarGridSpec(
            num_scalar_prefetch=1,
            grid=grid,
            in_specs=in_specs,
            out_specs=out_specs,
            scratch_shapes=scratch,
        ),
        compiler_params=pltpu.CompilerParams(vmem_limit_bytes=VMEM_BYTES),
        cost_estimate=pl.CostEstimate(
            flops=flops, bytes_accessed=nbytes, transcendentals=transcendentals
        ),
    )(place, *inputs)


def whole(shape):
    return pl.BlockSpec(shape, lambda i, place: (0,) * len(shape))


def token_start(place, block, rows):
    return pl.multiple_of(((place[2] ^ (block % 2)) * 2 + (place[3] ^ (block // 2))) * rows, 16)


def hidden_kernel(parts, units, place, gate, up, *refs):
    outs, (natural, columns) = refs[: len(parts)], refs[len(parts) :]
    step = pl.program_id(0)
    group, span = gate.shape
    rows = group // 4
    value = gate[...].astype(jnp.float32)
    hidden = value * jax.nn.sigmoid(value) * up[...].astype(jnp.float32)
    natural[...] = hidden.astype(jnp.bfloat16)
    ordered = [natural[pl.ds(token_start(place, b, rows), rows), :] for b in range(4)]
    columns[pl.ds(pl.multiple_of(step * span, 128), span), :] = jnp.concatenate(ordered, axis=0).T

    @pl.when(step == pl.num_programs(0) - 1)
    def _():
        half = units // 2
        for out, (k, first, count) in zip(outs, parts):
            for r in range(count):
                start = (place[0] ^ k) * units + (place[1] ^ (first + r)) * half
                out[r * half : (r + 1) * half, :] = columns[
                    pl.ds(pl.multiple_of(start, 16), half), :
                ]


def weight_kernel(place, codes, scales, *halves):
    span = codes.shape[1] // scales.shape[1]
    for block in range(scales.shape[1]):
        value = codes[:, block * span : (block + 1) * span].astype(jnp.float32)
        value = (value * scales[:, block : block + 1]).astype(jnp.bfloat16)
        at = block * span
        half, at = (0, at) if at < halves[0].shape[1] else (1, at - halves[0].shape[1])
        halves[half][:, at : at + span] = value


def join_kernel(place, own_a, own_b, other_a, other_b, weight):
    half, middle = own_a.shape
    weight[:half, :middle] = own_a[...]
    weight[:half, middle:] = own_b[...]
    weight[half:, :middle] = other_a[...]
    weight[half:, middle:] = other_b[...]


def tokens_kernel(picks, place, *refs):
    tokens = refs[-1]
    rows = refs[0].shape[-2]
    for at, (array, block) in enumerate(picks):
        source = refs[array]
        tokens[at * rows : (at + 1) * rows, :] = source[block] if len(source.shape) == 3 else source[...]


def columns_kernel(parts, by_rows, by_lanes, place, *refs):
    pieces, (keep, send, *rest) = refs[: len(parts)], refs[len(parts) :]
    half, group = rest[0].shape[0], pieces[0].shape[1]
    rows = group // 4
    for piece, (k, first, count) in zip(pieces, parts):
        turned = piece[...].T
        row, lane = by_rows.index(k), by_lanes.index(k)
        lanes = slice(lane % 2 * group, (lane % 2 + 1) * group)
        for b in range(4):
            target = send if b >= 2 else keep
            start = ((b % 2) * len(by_rows) + row) * rows
            target[start : start + rows, first * half : (first + count) * half] = turned[
                b * rows : (b + 1) * rows, :
            ]
        for r in range(count):
            rest[lane // 2 * 2 + first + r][:, lanes] = piece[r * half : (r + 1) * half, :]


def grads_kernel(nz, units, place, gate, up, *refs):
    pieces, (gate_grad, up_grad, columns, natural) = refs[:nz], refs[nz:]
    step = pl.program_id(0)
    group, span = gate.shape
    rows = group // 4

    @pl.when(step == 0)
    def _():
        half = units // 2
        for k in range(nz):
            for r in range(2):
                start = (place[0] ^ k) * units + (place[1] ^ r) * half
                columns[pl.ds(pl.multiple_of(start, 16), half), :] = pieces[k][
                    r * half : (r + 1) * half, :
                ]

    ordered = columns[pl.ds(pl.multiple_of(step * span, 128), span), :].T
    for b in range(4):
        natural[pl.ds(token_start(place, b, rows), rows), :] = ordered[b * rows : (b + 1) * rows]
    dhidden = natural[...].astype(jnp.float32)
    value = gate[...].astype(jnp.float32)
    up_value = up[...].astype(jnp.float32)
    sigmoid_gate = jax.nn.sigmoid(value)
    gate_grad[...] = (
        dhidden * up_value * sigmoid_gate * (1.0 + value * (1.0 - sigmoid_gate))
    ).astype(jnp.bfloat16)
    up_grad[...] = (dhidden * (value * sigmoid_gate)).astype(jnp.bfloat16)


def matmul(lhs, rhs, lhs_dim=1, rhs_dim=0, dtype=jnp.float32):
    dims = (((lhs_dim,), (rhs_dim,)), ((), ()))
    return lax.dot_general(lhs, rhs, dims, preferred_element_type=jnp.float32).astype(dtype)


def paired_body(gate_pre, up_pre, down_codes, down_scales, cotangent):
    group_rows, local_hidden = gate_pre.shape
    owned, width = down_codes.shape
    rows = cotangent.shape[0]
    nz, units, nblocks = 4, 2 * owned, down_scales.shape[1]
    middle = 3 * nblocks // 5 * (width // nblocks)
    total_tokens = group_rows * nz * 2
    bf16, f32 = jnp.bfloat16, jnp.float32
    place = jnp.stack([lax.axis_index(name) for name in ("z", "x", "y", "c")]).astype(jnp.int32)
    struct = jax.ShapeDtypeStruct
    barrier = lax.optimization_barrier

    far, near = exchange(cotangent, "z", 2), exchange(cotangent, "z", 1)
    own_y, own_c = exchange(cotangent, "y", 1), exchange(cotangent, "c", 1)

    sides = ((owned, middle), (owned, width - middle))
    own_a, own_b = call_kernel(
        weight_kernel, place, (down_codes, down_scales),
        [whole(down_codes.shape), whole(down_scales.shape)],
        [struct(shape, bf16) for shape in sides], [whole(shape) for shape in sides], (1,), [],
        (2 * owned * width, 4 * owned * width, 0),
    )
    other_a = exchange(own_a, "x", 1)

    parts = tuple((k, 0, 2) for k in (0, 2, 3, 1))
    pieces = [struct((count * owned, group_rows), bf16) for _, _, count in parts]
    piece_specs = [whole(piece.shape) for piece in pieces]
    span = column_span(local_hidden)
    steps = local_hidden // span
    wide = pl.BlockSpec((group_rows, span), lambda i, place: (0, i))
    act_bytes = group_rows * local_hidden * 2
    act_scratch = [pltpu.VMEM((group_rows, span), bf16), pltpu.VMEM((local_hidden, group_rows), bf16)]
    sent = call_kernel(
        functools.partial(hidden_kernel, parts, units), place, (gate_pre, up_pre), [wide] * 2,
        pieces, piece_specs, (steps,), act_scratch,
        (4 * act_bytes, 3 * act_bytes, act_bytes // 2),
    )

    far, near, own_y, own_c, sent = barrier((far, near, own_y, own_c, sent))
    last = exchange(far, "z", 1)
    other_y = exchange(jnp.stack([far, near]), "y", 1)
    other_b = exchange(own_b, "x", 1)
    columns = [sent[0], exchange(sent[1], "z", 2)]
    first_c = exchange(jnp.stack([own_y, far, near]), "c", 1)
    last, other_y, columns, other_a, sent, first_c = barrier(
        (last, other_y, columns, other_a, sent, first_c)
    )

    last_y = exchange(last, "y", 1)
    columns += [exchange(sent[i], "z", parts[i][0]) for i in range(2, len(parts))]
    other_c = exchange(jnp.stack([other_y[0], other_y[1], last]), "c", 1)
    last_y, columns, other_b = barrier((last_y, columns, other_b))
    last_c = exchange(last_y, "c", 1)

    weight = call_kernel(
        join_kernel, place, (own_a, own_b, other_a, other_b),
        [whole(shape) for shape in sides] * 2,
        struct((units, width), bf16), whole((units, width)), (1,), [],
        (0, 4 * units * width, 0),
    )

    half_tokens = nz * group_rows // 2
    by_rows, by_lanes = (1, 3, 0, 2), (0, 2, 1, 3)
    keep, send, *by_units = call_kernel(
        functools.partial(columns_kernel, parts, by_rows, by_lanes), place, columns, piece_specs,
        [struct((half_tokens, units), bf16)] * 2 + [struct((owned, half_tokens), bf16)] * 4,
        [whole((half_tokens, units))] * 2 + [whole((owned, half_tokens))] * 4, (1,), [],
        (0, 12 * units * half_tokens, 0),
    )

    def gather_tokens(arrays, picks):
        return call_kernel(
            functools.partial(tokens_kernel, picks), place, arrays,
            [whole(array.shape) for array in arrays], struct((half_tokens, width), bf16),
            whole((half_tokens, width)), (1,), [], (0, 4 * half_tokens * width, 0),
        )

    even = gather_tokens(
        (cotangent, own_y, own_c, far, other_y, first_c, other_c),
        ((0, 0), (1, 0), (2, 0), (5, 0), (3, 0), (4, 0), (5, 1), (6, 0)),
    )
    odd = gather_tokens(
        (near, last, last_y, other_y, first_c, other_c, last_c),
        ((0, 0), (3, 1), (4, 2), (5, 1), (1, 0), (2, 0), (5, 2), (6, 0)),
    )
    even, odd, send, keep = barrier((even, odd, send, keep))
    flat = [even, odd]

    factor = float(total_tokens) ** (-0.5)


    def grad_half(r, low=0, high=owned):
        first, second = by_units[r][low:high], by_units[2 + r][low:high]
        return (matmul(first, flat[0]) + matmul(second, flat[1])) * factor

    def back_of(k):
        rows_of_k = flat[k % 2][k // 2 * group_rows : (k // 2 + 1) * group_rows]
        return matmul(weight, rows_of_k, 1, 1, bf16)

    far_back = back_of(2)
    far_back, send = barrier((far_back, send))
    given = matmul(send, weight, dtype=bf16)
    given, flat = barrier((given, flat))
    over_c = exchange(given, "c", 1)
    early = owned // 96 * 16
    theirs = [grad_half(1, 0, early).astype(bf16), grad_half(1, early, owned).astype(bf16)]
    theirs, keep, flat = barrier((theirs, keep, flat))
    over_x = [exchange(part, "x", 1) for part in theirs]
    kept = matmul(keep, weight, dtype=bf16)
    kept, flat = barrier((kept, flat))
    back = [back_of(0), exchange(back_of(1), "z", 1), exchange(far_back, "z", 2)]
    last_back, _ = barrier((back_of(3), back[2]))
    back.append(exchange(last_back, "z", 3))
    sums = (kept.astype(f32) + over_c.astype(f32)).reshape(2, nz, rows, width)
    sums, over_x[0] = barrier((sums, over_x[0]))
    odd_y = exchange(sums[1, :2].astype(bf16), "y", 1)
    even_y = exchange(sums[1, 2:].astype(bf16), "y", 1)
    odd_sum = (sums[0, :2] + odd_y.astype(f32)).astype(bf16)
    odd_sum, back[2] = barrier((odd_sum, back[2]))
    even_y, _ = barrier((even_y, odd_sum))
    near_sum = exchange(odd_sum, "z", 1).astype(f32)
    even_sum = sums[0, 2:] + even_y.astype(f32)
    ours, across = even_sum[0] + near_sum[0], (even_sum[1] + near_sum[1]).astype(bf16)
    across, back[3] = barrier((across, back[3]))
    layer_out = (ours + exchange(across, "z", 2).astype(f32)).astype(bf16)

    weight_grad = grad_half(0) + jnp.concatenate(over_x).astype(f32)
    back, weight_grad, _ = barrier((back, weight_grad, across))
    gate_grad, up_grad = call_kernel(
        functools.partial(grads_kernel, nz, units), place, (gate_pre, up_pre, *back),
        [wide] * 2 + [whole((units, group_rows))] * nz,
        [struct((group_rows, local_hidden), bf16)] * 2, [wide] * 2, (steps,), act_scratch[::-1],
        (12 * act_bytes, 5 * act_bytes, act_bytes // 2),
    )
    return layer_out, gate_grad, up_grad, weight_grad


def column_span(width):
    return max((s for s in range(128, 641, 128) if width % s == 0), default=0)


def body(gate_pre, up_pre, down_codes, down_scales, cotangent):
    group_rows, local_hidden = gate_pre.shape
    owned, width = down_codes.shape
    nz, nx, ny, nc = (lax.axis_size(name) for name in ("z", "x", "y", "c"))
    rows = cotangent.shape[0]
    units = nx * owned
    total_tokens = group_rows * nz * nx

    gate_value = gate_pre.astype(jnp.float32)
    up_value = up_pre.astype(jnp.float32)
    sigmoid_gate = jax.nn.sigmoid(gate_value)
    activated = gate_value * sigmoid_gate
    hidden = (activated * up_value).astype(jnp.bfloat16)

    sent = hidden.T.reshape(nz, units, group_rows)
    columns = lax.all_to_all(sent, "z", 0, 0, tiled=True) if nz > 1 else sent

    line = lax.all_gather(cotangent, ("z", "y"), axis=0)
    both = gather_pair(line, "c")
    received = jnp.moveaxis(both, 0, 1).reshape(nz, group_rows, width)

    weight = gather_pair(dequantize(down_codes, down_scales), "x").reshape(units, width)

    partial_out = lax.dot_general(
        columns, weight, (((1,), (0,)), ((), ())), preferred_element_type=jnp.float32
    ).astype(jnp.bfloat16)
    partial_out = partial_out.reshape(nz, ny, nc, rows, width)
    over_c = scatter_sum(jnp.moveaxis(partial_out, 2, 0), "c")
    over_y = scatter_sum(jnp.moveaxis(over_c.astype(jnp.bfloat16), 1, 0), "y")
    layer_out = scatter_sum(over_y.astype(jnp.bfloat16), "z").astype(jnp.bfloat16)

    dcolumns = lax.dot_general(
        weight, received, (((1,), (2,)), ((), ())), preferred_element_type=jnp.float32
    ).astype(jnp.bfloat16)
    dcolumns = jnp.moveaxis(dcolumns, 1, 0)
    back = lax.all_to_all(dcolumns, "z", 0, 0, tiled=True) if nz > 1 else dcolumns
    dhidden = back.reshape(local_hidden, group_rows).T.astype(jnp.float32)
    gate_grad = (
        dhidden * up_value * sigmoid_gate * (1.0 + gate_value * (1.0 - sigmoid_gate))
    ).astype(jnp.bfloat16)
    up_grad = (dhidden * activated).astype(jnp.bfloat16)

    partial_grad = lax.dot_general(
        columns, received, (((0, 2), (0, 1)), ((), ())), preferred_element_type=jnp.float32
    )
    weight_grad = scatter_sum(partial_grad.reshape(nx, owned, width), "x") * float(total_tokens) ** (-0.5)
    return layer_out, gate_grad, up_grad, weight_grad


def outer_split(mesh, tokens, hidden, width):
    dp, tensor = mesh.shape["dp"], mesh.shape["tensor"]

    def rows_sent(nz):
        moved = 2 * (tokens // dp) * (hidden // tensor) / width if nz > 1 else 0
        return 2 * hidden // (tensor * nz) + 2 * tokens * nz // dp + moved

    return min((nz for nz in range(1, dp + 1) if dp % nz == 0), key=rows_sent)


def solution(mesh):
    def call(gate_pre, up_pre, down_codes, down_scales, cotangent):
        tokens, hidden = gate_pre.shape
        nz = outer_split(mesh, tokens, hidden, cotangent.shape[1])
        dp, tensor = mesh.shape["dp"], mesh.shape["tensor"]
        fine = Mesh(mesh.devices.reshape(nz, dp // nz, tensor // 2, 2), ("z", "x", "y", "c"))
        act = P(("z", "x"), ("y", "c"))
        weight = P(("y", "c", "z", "x"), None)
        layer = P(("z", "x", "y", "c"), None)
        owned = hidden // (dp * tensor)
        rows = tokens // (dp * tensor)
        pairs = fine.shape["x"] == 2 and fine.shape["y"] == 2 and nz == 4
        aligned = owned % 16 == 0 and rows % 16 == 0 and column_span(hidden // tensor)
        nblocks = down_scales.shape[1]
        blocks = nblocks > 2 and cotangent.shape[1] // nblocks % 128 == 0
        return jax.shard_map(
            paired_body if pairs and aligned and blocks else body,
            mesh=fine,
            in_specs=(act, act, weight, weight, layer),
            out_specs=(layer, act, act, weight),
            check_vma=False,
        )(gate_pre, up_pre, down_codes, down_scales, cotangent)

    return call
```

```python
import functools

import jax
import jax.numpy as jnp
from jax import lax
from jax.experimental import pallas as pl
from jax.experimental.pallas import tpu as pltpu
from jax.sharding import Mesh, PartitionSpec as P

VMEM_BYTES = 32 * 2**20


def dequantize(codes, scales):
    rows, width = codes.shape
    nblocks = scales.shape[1]
    blocks = codes.astype(jnp.float32).reshape(rows, nblocks, width // nblocks) * scales[:, :, None]
    return blocks.reshape(rows, width).astype(jnp.bfloat16)


def swap(value, axis):
    return lax.ppermute(value, axis, [(0, 1), (1, 0)])


def gather_pair(value, axis):
    if lax.axis_size(axis) != 2:
        return lax.all_gather(value, axis, axis=0)
    other = swap(value, axis)
    first = lax.axis_index(axis) == 0
    return jnp.stack([jnp.where(first, value, other), jnp.where(first, other, value)])


def scatter_sum(parts, axis):
    size = lax.axis_size(axis)
    if size == 1:
        return parts[0].astype(jnp.float32)
    if size != 2:
        received = lax.all_to_all(parts.astype(jnp.bfloat16), axis, 0, 0, tiled=True)
        return jnp.sum(received.astype(jnp.float32), axis=0)
    me = lax.axis_index(axis)
    theirs = lax.dynamic_index_in_dim(parts, 1 - me, 0, keepdims=False).astype(jnp.bfloat16)
    mine = lax.dynamic_index_in_dim(parts, me, 0, keepdims=False)
    return mine.astype(jnp.float32) + swap(theirs, axis).astype(jnp.float32)


def exchange(value, axis, offset):
    size = lax.axis_size(axis)
    return lax.ppermute(value, axis, [(i, i ^ offset) for i in range(size)])


def call_kernel(kernel, place, inputs, in_specs, out_shapes, out_specs, grid, scratch, cost):
    flops, nbytes, transcendentals = cost
    return pl.pallas_call(
        kernel,
        out_shape=out_shapes,
        grid_spec=pltpu.PrefetchScalarGridSpec(
            num_scalar_prefetch=1,
            grid=grid,
            in_specs=in_specs,
            out_specs=out_specs,
            scratch_shapes=scratch,
        ),
        compiler_params=pltpu.CompilerParams(vmem_limit_bytes=VMEM_BYTES),
        cost_estimate=pl.CostEstimate(
            flops=flops, bytes_accessed=nbytes, transcendentals=transcendentals
        ),
    )(place, *inputs)


def whole(shape):
    return pl.BlockSpec(shape, lambda i, place: (0,) * len(shape))


def token_start(place, block, rows):
    return pl.multiple_of(((place[2] ^ (block % 2)) * 2 + (place[3] ^ (block // 2))) * rows, 16)


def hidden_kernel(parts, units, place, gate, up, *refs):
    outs, (natural, columns) = refs[: len(parts)], refs[len(parts) :]
    step = pl.program_id(0)
    group, span = gate.shape
    rows = group // 4
    value = gate[...].astype(jnp.float32)
    hidden = value * jax.nn.sigmoid(value) * up[...].astype(jnp.float32)
    natural[...] = hidden.astype(jnp.bfloat16)
    ordered = [natural[pl.ds(token_start(place, b, rows), rows), :] for b in range(4)]
    columns[pl.ds(pl.multiple_of(step * span, 128), span), :] = jnp.concatenate(ordered, axis=0).T

    @pl.when(step == pl.num_programs(0) - 1)
    def _():
        half = units // 2
        for out, (k, first, count) in zip(outs, parts):
            for r in range(count):
                start = (place[0] ^ k) * units + (place[1] ^ (first + r)) * half
                out[r * half : (r + 1) * half, :] = columns[
                    pl.ds(pl.multiple_of(start, 16), half), :
                ]


def weight_kernel(place, codes, scales, *halves):
    span = codes.shape[1] // scales.shape[1]
    for block in range(scales.shape[1]):
        value = codes[:, block * span : (block + 1) * span].astype(jnp.float32)
        value = (value * scales[:, block : block + 1]).astype(jnp.bfloat16)
        at = block * span
        half, at = (0, at) if at < halves[0].shape[1] else (1, at - halves[0].shape[1])
        halves[half][:, at : at + span] = value


def join_kernel(place, own_a, own_b, other_a, other_b, weight):
    half, middle = own_a.shape
    weight[:half, :middle] = own_a[...]
    weight[:half, middle:] = own_b[...]
    weight[half:, :middle] = other_a[...]
    weight[half:, middle:] = other_b[...]


def tokens_kernel(picks, place, *refs):
    tokens = refs[-1]
    rows = refs[0].shape[-2]
    for at, (array, block) in enumerate(picks):
        source = refs[array]
        tokens[at * rows : (at + 1) * rows, :] = source[block] if len(source.shape) == 3 else source[...]


def columns_kernel(parts, by_rows, by_lanes, place, *refs):
    pieces, (keep, send, *rest) = refs[: len(parts)], refs[len(parts) :]
    half, group = rest[0].shape[0], pieces[0].shape[1]
    rows = group // 4
    for piece, (k, first, count) in zip(pieces, parts):
        turned = piece[...].T
        row, lane = by_rows.index(k), by_lanes.index(k)
        lanes = slice(lane % 2 * group, (lane % 2 + 1) * group)
        for b in range(4):
            target = send if b >= 2 else keep
            start = ((b % 2) * len(by_rows) + row) * rows
            target[start : start + rows, first * half : (first + count) * half] = turned[
                b * rows : (b + 1) * rows, :
            ]
        for r in range(count):
            rest[lane // 2 * 2 + first + r][:, lanes] = piece[r * half : (r + 1) * half, :]


def grads_kernel(nz, units, place, gate, up, *refs):
    pieces, (gate_grad, up_grad, columns, natural) = refs[:nz], refs[nz:]
    step = pl.program_id(0)
    group, span = gate.shape
    rows = group // 4

    @pl.when(step == 0)
    def _():
        half = units // 2
        for k in range(nz):
            for r in range(2):
                start = (place[0] ^ k) * units + (place[1] ^ r) * half
                columns[pl.ds(pl.multiple_of(start, 16), half), :] = pieces[k][
                    r * half : (r + 1) * half, :
                ]

    ordered = columns[pl.ds(pl.multiple_of(step * span, 128), span), :].T
    for b in range(4):
        natural[pl.ds(token_start(place, b, rows), rows), :] = ordered[b * rows : (b + 1) * rows]
    dhidden = natural[...].astype(jnp.float32)
    value = gate[...].astype(jnp.float32)
    up_value = up[...].astype(jnp.float32)
    sigmoid_gate = jax.nn.sigmoid(value)
    gate_grad[...] = (
        dhidden * up_value * sigmoid_gate * (1.0 + value * (1.0 - sigmoid_gate))
    ).astype(jnp.bfloat16)
    up_grad[...] = (dhidden * (value * sigmoid_gate)).astype(jnp.bfloat16)


def matmul(lhs, rhs, lhs_dim=1, rhs_dim=0, dtype=jnp.float32):
    dims = (((lhs_dim,), (rhs_dim,)), ((), ()))
    return lax.dot_general(lhs, rhs, dims, preferred_element_type=jnp.float32).astype(dtype)


def paired_body(gate_pre, up_pre, down_codes, down_scales, cotangent):
    group_rows, local_hidden = gate_pre.shape
    owned, width = down_codes.shape
    rows = cotangent.shape[0]
    nz, units, nblocks = 4, 2 * owned, down_scales.shape[1]
    middle = 3 * nblocks // 5 * (width // nblocks)
    total_tokens = group_rows * nz * 2
    bf16, f32 = jnp.bfloat16, jnp.float32
    place = jnp.stack([lax.axis_index(name) for name in ("z", "x", "y", "c")]).astype(jnp.int32)
    struct = jax.ShapeDtypeStruct
    barrier = lax.optimization_barrier

    far, near = exchange(cotangent, "z", 2), exchange(cotangent, "z", 1)
    own_y, own_c = exchange(cotangent, "y", 1), exchange(cotangent, "c", 1)

    sides = ((owned, middle), (owned, width - middle))
    own_a, own_b = call_kernel(
        weight_kernel, place, (down_codes, down_scales),
        [whole(down_codes.shape), whole(down_scales.shape)],
        [struct(shape, bf16) for shape in sides], [whole(shape) for shape in sides], (1,), [],
        (2 * owned * width, 4 * owned * width, 0),
    )
    other_a = exchange(own_a, "x", 1)

    parts = tuple((k, 0, 2) for k in (0, 2, 3, 1))
    pieces = [struct((count * owned, group_rows), bf16) for _, _, count in parts]
    piece_specs = [whole(piece.shape) for piece in pieces]
    span = column_span(local_hidden)
    steps = local_hidden // span
    wide = pl.BlockSpec((group_rows, span), lambda i, place: (0, i))
    act_bytes = group_rows * local_hidden * 2
    act_scratch = [pltpu.VMEM((group_rows, span), bf16), pltpu.VMEM((local_hidden, group_rows), bf16)]
    sent = call_kernel(
        functools.partial(hidden_kernel, parts, units), place, (gate_pre, up_pre), [wide] * 2,
        pieces, piece_specs, (steps,), act_scratch,
        (4 * act_bytes, 3 * act_bytes, act_bytes // 2),
    )

    far, near, own_y, own_c, sent = barrier((far, near, own_y, own_c, sent))
    last = exchange(far, "z", 1)
    other_y = exchange(jnp.stack([far, near]), "y", 1)
    other_b = exchange(own_b, "x", 1)
    columns = [sent[0], exchange(sent[1], "z", 2)]
    first_c = exchange(jnp.stack([own_y, far, near]), "c", 1)
    last, other_y, columns, other_a, sent, first_c = barrier(
        (last, other_y, columns, other_a, sent, first_c)
    )

    last_y = exchange(last, "y", 1)
    columns += [exchange(sent[i], "z", parts[i][0]) for i in range(2, len(parts))]
    other_c = exchange(jnp.stack([other_y[0], other_y[1], last]), "c", 1)
    last_y, columns, other_b = barrier((last_y, columns, other_b))
    last_c = exchange(last_y, "c", 1)

    weight = call_kernel(
        join_kernel, place, (own_a, own_b, other_a, other_b),
        [whole(shape) for shape in sides] * 2,
        struct((units, width), bf16), whole((units, width)), (1,), [],
        (0, 4 * units * width, 0),
    )

    half_tokens = nz * group_rows // 2
    by_rows, by_lanes = (1, 3, 0, 2), (0, 2, 1, 3)
    keep, send, *by_units = call_kernel(
        functools.partial(columns_kernel, parts, by_rows, by_lanes), place, columns, piece_specs,
        [struct((half_tokens, units), bf16)] * 2 + [struct((owned, half_tokens), bf16)] * 4,
        [whole((half_tokens, units))] * 2 + [whole((owned, half_tokens))] * 4, (1,), [],
        (0, 12 * units * half_tokens, 0),
    )

    def gather_tokens(arrays, picks):
        return call_kernel(
            functools.partial(tokens_kernel, picks), place, arrays,
            [whole(array.shape) for array in arrays], struct((half_tokens, width), bf16),
            whole((half_tokens, width)), (1,), [], (0, 4 * half_tokens * width, 0),
        )

    even = gather_tokens(
        (cotangent, own_y, own_c, far, other_y, first_c, other_c),
        ((0, 0), (1, 0), (2, 0), (5, 0), (3, 0), (4, 0), (5, 1), (6, 0)),
    )
    odd = gather_tokens(
        (near, last, last_y, other_y, first_c, other_c, last_c),
        ((0, 0), (3, 1), (4, 2), (5, 1), (1, 0), (2, 0), (5, 2), (6, 0)),
    )
    factor = float(total_tokens) ** (-0.5)


    def grad_half(r, low=0, high=owned):
        first, second = by_units[r][low:high], by_units[2 + r][low:high]
        return (matmul(first, flat[0]) + matmul(second, flat[1])) * factor

    def back_of(k):
        rows_of_k = flat[k % 2][k // 2 * group_rows : (k // 2 + 1) * group_rows]
        return matmul(weight, rows_of_k, 1, 1, bf16)

    over_c = exchange(matmul(send, weight, dtype=bf16), "c", 1)
    kept = matmul(keep, weight, dtype=bf16)
    kept, flat = barrier((kept, [even, odd]))
    far_back = back_of(2)
    kept, far_back = barrier((kept, far_back))
    sums = (kept.astype(f32) + over_c.astype(f32)).reshape(2, nz, rows, width)
    sums, flat = barrier((sums, flat))
    odd_y = exchange(sums[1, :2].astype(bf16), "y", 1)
    even_y = exchange(sums[1, 2:].astype(bf16), "y", 1)
    over_x = exchange(grad_half(1).astype(bf16), "x", 1)
    near_back = exchange(back_of(1), "z", 1)
    odd_y, flat = barrier((odd_y, flat))
    back = [back_of(0), near_back, exchange(far_back, "z", 2), exchange(back_of(3), "z", 3)]
    odd_sum = (sums[0, :2] + odd_y.astype(f32)).astype(bf16)
    odd_sum, back[2] = barrier((odd_sum, back[2]))
    near_sum, even_y = barrier((exchange(odd_sum, "z", 1), even_y))
    near_sum = near_sum.astype(f32)
    even_sum = sums[0, 2:] + even_y.astype(f32)
    ours, across = even_sum[0] + near_sum[0], (even_sum[1] + near_sum[1]).astype(bf16)
    across, back[3] = barrier((across, back[3]))
    far_sum = exchange(across, "z", 2)

    back, flat, _ = barrier((back, flat, across))
    own_grad = grad_half(0)
    gate_grad, up_grad = call_kernel(
        functools.partial(grads_kernel, nz, units), place, (gate_pre, up_pre, *back),
        [wide] * 2 + [whole((units, group_rows))] * nz,
        [struct((group_rows, local_hidden), bf16)] * 2, [wide] * 2, (steps,), act_scratch[::-1],
        (12 * act_bytes, 5 * act_bytes, act_bytes // 2),
    )
    over_x, _ = barrier((over_x, gate_grad))
    weight_grad = own_grad + over_x.astype(f32)
    far_sum, weight_grad = barrier((far_sum, weight_grad))
    layer_out = (ours + far_sum.astype(f32)).astype(bf16)
    return layer_out, gate_grad, up_grad, weight_grad


def column_span(width):
    return max((s for s in range(128, 641, 128) if width % s == 0), default=0)


def body(gate_pre, up_pre, down_codes, down_scales, cotangent):
    group_rows, local_hidden = gate_pre.shape
    owned, width = down_codes.shape
    nz, nx, ny, nc = (lax.axis_size(name) for name in ("z", "x", "y", "c"))
    rows = cotangent.shape[0]
    units = nx * owned
    total_tokens = group_rows * nz * nx

    gate_value = gate_pre.astype(jnp.float32)
    up_value = up_pre.astype(jnp.float32)
    sigmoid_gate = jax.nn.sigmoid(gate_value)
    activated = gate_value * sigmoid_gate
    hidden = (activated * up_value).astype(jnp.bfloat16)

    sent = hidden.T.reshape(nz, units, group_rows)
    columns = lax.all_to_all(sent, "z", 0, 0, tiled=True) if nz > 1 else sent

    line = lax.all_gather(cotangent, ("z", "y"), axis=0)
    both = gather_pair(line, "c")
    received = jnp.moveaxis(both, 0, 1).reshape(nz, group_rows, width)

    weight = gather_pair(dequantize(down_codes, down_scales), "x").reshape(units, width)

    partial_out = lax.dot_general(
        columns, weight, (((1,), (0,)), ((), ())), preferred_element_type=jnp.float32
    ).astype(jnp.bfloat16)
    partial_out = partial_out.reshape(nz, ny, nc, rows, width)
    over_c = scatter_sum(jnp.moveaxis(partial_out, 2, 0), "c")
    over_y = scatter_sum(jnp.moveaxis(over_c.astype(jnp.bfloat16), 1, 0), "y")
    layer_out = scatter_sum(over_y.astype(jnp.bfloat16), "z").astype(jnp.bfloat16)

    dcolumns = lax.dot_general(
        weight, received, (((1,), (2,)), ((), ())), preferred_element_type=jnp.float32
    ).astype(jnp.bfloat16)
    dcolumns = jnp.moveaxis(dcolumns, 1, 0)
    back = lax.all_to_all(dcolumns, "z", 0, 0, tiled=True) if nz > 1 else dcolumns
    dhidden = back.reshape(local_hidden, group_rows).T.astype(jnp.float32)
    gate_grad = (
        dhidden * up_value * sigmoid_gate * (1.0 + gate_value * (1.0 - sigmoid_gate))
    ).astype(jnp.bfloat16)
    up_grad = (dhidden * activated).astype(jnp.bfloat16)

    partial_grad = lax.dot_general(
        columns, received, (((0, 2), (0, 1)), ((), ())), preferred_element_type=jnp.float32
    )
    weight_grad = scatter_sum(partial_grad.reshape(nx, owned, width), "x") * float(total_tokens) ** (-0.5)
    return layer_out, gate_grad, up_grad, weight_grad


def outer_split(mesh, tokens, hidden, width):
    dp, tensor = mesh.shape["dp"], mesh.shape["tensor"]

    def rows_sent(nz):
        moved = 2 * (tokens // dp) * (hidden // tensor) / width if nz > 1 else 0
        return 2 * hidden // (tensor * nz) + 2 * tokens * nz // dp + moved

    return min((nz for nz in range(1, dp + 1) if dp % nz == 0), key=rows_sent)


def solution(mesh):
    def call(gate_pre, up_pre, down_codes, down_scales, cotangent):
        tokens, hidden = gate_pre.shape
        nz = outer_split(mesh, tokens, hidden, cotangent.shape[1])
        dp, tensor = mesh.shape["dp"], mesh.shape["tensor"]
        fine = Mesh(mesh.devices.reshape(nz, dp // nz, tensor // 2, 2), ("z", "x", "y", "c"))
        act = P(("z", "x"), ("y", "c"))
        weight = P(("y", "c", "z", "x"), None)
        layer = P(("z", "x", "y", "c"), None)
        owned = hidden // (dp * tensor)
        rows = tokens // (dp * tensor)
        pairs = fine.shape["x"] == 2 and fine.shape["y"] == 2 and nz == 4
        aligned = owned % 16 == 0 and rows % 16 == 0 and column_span(hidden // tensor)
        nblocks = down_scales.shape[1]
        blocks = nblocks > 2 and cotangent.shape[1] // nblocks % 128 == 0
        return jax.shard_map(
            paired_body if pairs and aligned and blocks else body,
            mesh=fine,
            in_specs=(act, act, weight, weight, layer),
            out_specs=(layer, act, act, weight),
            check_vma=False,
        )(gate_pre, up_pre, down_codes, down_scales, cotangent)

    return call
```

```python
import functools

import jax
import jax.numpy as jnp
from jax import lax
from jax.experimental import pallas as pl
from jax.experimental.pallas import tpu as pltpu
from jax.sharding import Mesh, PartitionSpec as P

VMEM_BYTES = 32 * 2**20


def dequantize(codes, scales):
    rows, width = codes.shape
    nblocks = scales.shape[1]
    blocks = codes.astype(jnp.float32).reshape(rows, nblocks, width // nblocks) * scales[:, :, None]
    return blocks.reshape(rows, width).astype(jnp.bfloat16)


def swap(value, axis):
    return lax.ppermute(value, axis, [(0, 1), (1, 0)])


def gather_pair(value, axis):
    if lax.axis_size(axis) != 2:
        return lax.all_gather(value, axis, axis=0)
    other = swap(value, axis)
    first = lax.axis_index(axis) == 0
    return jnp.stack([jnp.where(first, value, other), jnp.where(first, other, value)])


def scatter_sum(parts, axis):
    size = lax.axis_size(axis)
    if size == 1:
        return parts[0].astype(jnp.float32)
    if size != 2:
        received = lax.all_to_all(parts.astype(jnp.bfloat16), axis, 0, 0, tiled=True)
        return jnp.sum(received.astype(jnp.float32), axis=0)
    me = lax.axis_index(axis)
    theirs = lax.dynamic_index_in_dim(parts, 1 - me, 0, keepdims=False).astype(jnp.bfloat16)
    mine = lax.dynamic_index_in_dim(parts, me, 0, keepdims=False)
    return mine.astype(jnp.float32) + swap(theirs, axis).astype(jnp.float32)


def exchange(value, axis, offset):
    size = lax.axis_size(axis)
    return lax.ppermute(value, axis, [(i, i ^ offset) for i in range(size)])


def call_kernel(kernel, place, inputs, in_specs, out_shapes, out_specs, grid, scratch, cost):
    flops, nbytes, transcendentals = cost
    return pl.pallas_call(
        kernel,
        out_shape=out_shapes,
        grid_spec=pltpu.PrefetchScalarGridSpec(
            num_scalar_prefetch=1,
            grid=grid,
            in_specs=in_specs,
            out_specs=out_specs,
            scratch_shapes=scratch,
        ),
        compiler_params=pltpu.CompilerParams(vmem_limit_bytes=VMEM_BYTES),
        cost_estimate=pl.CostEstimate(
            flops=flops, bytes_accessed=nbytes, transcendentals=transcendentals
        ),
    )(place, *inputs)


def whole(shape):
    return pl.BlockSpec(shape, lambda i, place: (0,) * len(shape))


def token_start(place, block, rows):
    return pl.multiple_of(((place[2] ^ (block % 2)) * 2 + (place[3] ^ (block // 2))) * rows, 16)


def hidden_kernel(parts, units, place, gate, up, *refs):
    outs, (natural, columns) = refs[: len(parts)], refs[len(parts) :]
    step = pl.program_id(0)
    group, span = gate.shape
    rows = group // 4
    value = gate[...].astype(jnp.float32)
    hidden = value * jax.nn.sigmoid(value) * up[...].astype(jnp.float32)
    natural[...] = hidden.astype(jnp.bfloat16)
    ordered = [natural[pl.ds(token_start(place, b, rows), rows), :] for b in range(4)]
    columns[pl.ds(pl.multiple_of(step * span, 128), span), :] = jnp.concatenate(ordered, axis=0).T

    @pl.when(step == pl.num_programs(0) - 1)
    def _():
        half = units // 2
        for out, (k, first, count) in zip(outs, parts):
            for r in range(count):
                start = (place[0] ^ k) * units + (place[1] ^ (first + r)) * half
                out[r * half : (r + 1) * half, :] = columns[
                    pl.ds(pl.multiple_of(start, 16), half), :
                ]


def weight_kernel(place, codes, scales, *halves):
    span = codes.shape[1] // scales.shape[1]
    for block in range(scales.shape[1]):
        value = codes[:, block * span : (block + 1) * span].astype(jnp.float32)
        value = (value * scales[:, block : block + 1]).astype(jnp.bfloat16)
        at = block * span
        half, at = (0, at) if at < halves[0].shape[1] else (1, at - halves[0].shape[1])
        halves[half][:, at : at + span] = value


def join_kernel(place, own_a, own_b, other_a, other_b, weight):
    half, middle = own_a.shape
    weight[:half, :middle] = own_a[...]
    weight[:half, middle:] = own_b[...]
    weight[half:, :middle] = other_a[...]
    weight[half:, middle:] = other_b[...]


def tokens_kernel(picks, place, *refs):
    tokens = refs[-1]
    rows = refs[0].shape[-2]
    for at, (array, block) in enumerate(picks):
        source = refs[array]
        tokens[at * rows : (at + 1) * rows, :] = source[block] if len(source.shape) == 3 else source[...]


def columns_kernel(parts, by_rows, by_lanes, place, *refs):
    pieces, (keep, send, *rest) = refs[: len(parts)], refs[len(parts) :]
    half, group = rest[0].shape[0], pieces[0].shape[1]
    rows = group // 4
    for piece, (k, first, count) in zip(pieces, parts):
        turned = piece[...].T
        row, lane = by_rows.index(k), by_lanes.index(k)
        lanes = slice(lane % 2 * group, (lane % 2 + 1) * group)
        for b in range(4):
            target = send if b >= 2 else keep
            start = ((b % 2) * len(by_rows) + row) * rows
            target[start : start + rows, first * half : (first + count) * half] = turned[
                b * rows : (b + 1) * rows, :
            ]
        for r in range(count):
            rest[lane // 2 * 2 + first + r][:, lanes] = piece[r * half : (r + 1) * half, :]


def grads_kernel(nz, units, place, gate, up, *refs):
    pieces, (gate_grad, up_grad, columns, natural) = refs[:nz], refs[nz:]
    step = pl.program_id(0)
    group, span = gate.shape
    rows = group // 4

    @pl.when(step == 0)
    def _():
        half = units // 2
        for k in range(nz):
            for r in range(2):
                start = (place[0] ^ k) * units + (place[1] ^ r) * half
                columns[pl.ds(pl.multiple_of(start, 16), half), :] = pieces[k][
                    r * half : (r + 1) * half, :
                ]

    ordered = columns[pl.ds(pl.multiple_of(step * span, 128), span), :].T
    for b in range(4):
        natural[pl.ds(token_start(place, b, rows), rows), :] = ordered[b * rows : (b + 1) * rows]
    dhidden = natural[...].astype(jnp.float32)
    value = gate[...].astype(jnp.float32)
    up_value = up[...].astype(jnp.float32)
    sigmoid_gate = jax.nn.sigmoid(value)
    gate_grad[...] = (
        dhidden * up_value * sigmoid_gate * (1.0 + value * (1.0 - sigmoid_gate))
    ).astype(jnp.bfloat16)
    up_grad[...] = (dhidden * (value * sigmoid_gate)).astype(jnp.bfloat16)


def matmul(lhs, rhs, lhs_dim=1, rhs_dim=0, dtype=jnp.float32):
    dims = (((lhs_dim,), (rhs_dim,)), ((), ()))
    return lax.dot_general(lhs, rhs, dims, preferred_element_type=jnp.float32).astype(dtype)


def paired_body(gate_pre, up_pre, down_codes, down_scales, cotangent):
    group_rows, local_hidden = gate_pre.shape
    owned, width = down_codes.shape
    rows = cotangent.shape[0]
    nz, units, nblocks = 4, 2 * owned, down_scales.shape[1]
    middle = 3 * nblocks // 5 * (width // nblocks)
    total_tokens = group_rows * nz * 2
    bf16, f32 = jnp.bfloat16, jnp.float32
    place = jnp.stack([lax.axis_index(name) for name in ("z", "x", "y", "c")]).astype(jnp.int32)
    struct = jax.ShapeDtypeStruct
    barrier = lax.optimization_barrier

    far, near = exchange(cotangent, "z", 2), exchange(cotangent, "z", 1)
    own_y, own_c = exchange(cotangent, "y", 1), exchange(cotangent, "c", 1)

    sides = ((owned, middle), (owned, width - middle))
    own_a, own_b = call_kernel(
        weight_kernel, place, (down_codes, down_scales),
        [whole(down_codes.shape), whole(down_scales.shape)],
        [struct(shape, bf16) for shape in sides], [whole(shape) for shape in sides], (1,), [],
        (2 * owned * width, 4 * owned * width, 0),
    )
    other_a = exchange(own_a, "x", 1)

    parts = tuple((k, 0, 2) for k in (0, 2, 3, 1))
    pieces = [struct((count * owned, group_rows), bf16) for _, _, count in parts]
    piece_specs = [whole(piece.shape) for piece in pieces]
    span = column_span(local_hidden)
    steps = local_hidden // span
    wide = pl.BlockSpec((group_rows, span), lambda i, place: (0, i))
    act_bytes = group_rows * local_hidden * 2
    act_scratch = [pltpu.VMEM((group_rows, span), bf16), pltpu.VMEM((local_hidden, group_rows), bf16)]
    sent = call_kernel(
        functools.partial(hidden_kernel, parts, units), place, (gate_pre, up_pre), [wide] * 2,
        pieces, piece_specs, (steps,), act_scratch,
        (4 * act_bytes, 3 * act_bytes, act_bytes // 2),
    )

    far, near, own_y, own_c, sent = barrier((far, near, own_y, own_c, sent))
    last = exchange(far, "z", 1)
    other_y = exchange(jnp.stack([far, near]), "y", 1)
    other_b = exchange(own_b, "x", 1)
    columns = [sent[0], exchange(sent[1], "z", 2)]
    first_c = exchange(jnp.stack([own_y, far, near]), "c", 1)
    last, other_y, columns, other_a, sent, first_c = barrier(
        (last, other_y, columns, other_a, sent, first_c)
    )

    last_y = exchange(last, "y", 1)
    columns += [exchange(sent[i], "z", parts[i][0]) for i in range(2, len(parts))]
    other_c = exchange(jnp.stack([other_y[0], other_y[1], last]), "c", 1)
    last_y, columns, other_b = barrier((last_y, columns, other_b))
    last_c = exchange(last_y, "c", 1)

    weight = call_kernel(
        join_kernel, place, (own_a, own_b, other_a, other_b),
        [whole(shape) for shape in sides] * 2,
        struct((units, width), bf16), whole((units, width)), (1,), [],
        (0, 4 * units * width, 0),
    )

    half_tokens = nz * group_rows // 2
    by_rows, by_lanes = (1, 3, 0, 2), (0, 2, 1, 3)
    keep, send, *by_units = call_kernel(
        functools.partial(columns_kernel, parts, by_rows, by_lanes), place, columns, piece_specs,
        [struct((half_tokens, units), bf16)] * 2 + [struct((owned, half_tokens), bf16)] * 4,
        [whole((half_tokens, units))] * 2 + [whole((owned, half_tokens))] * 4, (1,), [],
        (0, 12 * units * half_tokens, 0),
    )

    def gather_tokens(arrays, picks):
        return call_kernel(
            functools.partial(tokens_kernel, picks), place, arrays,
            [whole(array.shape) for array in arrays], struct((half_tokens, width), bf16),
            whole((half_tokens, width)), (1,), [], (0, 4 * half_tokens * width, 0),
        )

    even = gather_tokens(
        (cotangent, own_y, own_c, far, other_y, first_c, other_c),
        ((0, 0), (1, 0), (2, 0), (5, 0), (3, 0), (4, 0), (5, 1), (6, 0)),
    )
    odd = gather_tokens(
        (near, last, last_y, other_y, first_c, other_c, last_c),
        ((0, 0), (3, 1), (4, 2), (5, 1), (1, 0), (2, 0), (5, 2), (6, 0)),
    )
    factor = float(total_tokens) ** (-0.5)


    def grad_half(r, low=0, high=owned):
        first, second = by_units[r][low:high], by_units[2 + r][low:high]
        return (matmul(first, flat[0]) + matmul(second, flat[1])) * factor

    def back_of(k):
        rows_of_k = flat[k % 2][k // 2 * group_rows : (k // 2 + 1) * group_rows]
        return matmul(weight, rows_of_k, 1, 1, bf16)

    flat = [even, odd]
    far_back = back_of(2)
    far_back, send = barrier((far_back, send))
    given = matmul(send, weight, dtype=bf16)
    given, flat = barrier((given, flat))
    over_c = exchange(given, "c", 1)
    theirs = grad_half(1).astype(bf16)
    theirs, keep, flat = barrier((theirs, keep, flat))
    over_x = exchange(theirs, "x", 1)
    kept = matmul(keep, weight, dtype=bf16)
    sums = (kept.astype(f32) + over_c.astype(f32)).reshape(2, nz, rows, width)
    sums, flat = barrier((sums, flat))
    odd_y = exchange(sums[1, :2].astype(bf16), "y", 1)
    even_y = exchange(sums[1, 2:].astype(bf16), "y", 1)
    near_back, last_back = exchange(back_of(1), "z", 1), exchange(back_of(3), "z", 3)
    odd_y, flat = barrier((odd_y, flat))
    back = [back_of(0), near_back, exchange(far_back, "z", 2), last_back]
    own_grad = grad_half(0)
    odd_sum = (sums[0, :2] + odd_y.astype(f32)).astype(bf16)
    odd_sum, back[2] = barrier((odd_sum, back[2]))
    near_sum = exchange(odd_sum, "z", 1)
    gate_grad, up_grad = call_kernel(
        functools.partial(grads_kernel, nz, units), place, (gate_pre, up_pre, *back),
        [wide] * 2 + [whole((units, group_rows))] * nz,
        [struct((group_rows, local_hidden), bf16)] * 2, [wide] * 2, (steps,), act_scratch[::-1],
        (12 * act_bytes, 5 * act_bytes, act_bytes // 2),
    )
    near_sum, even_y, gate_grad, own_grad = barrier((near_sum, even_y, gate_grad, own_grad))
    near_sum = near_sum.astype(f32)
    even_sum = sums[0, 2:] + even_y.astype(f32)
    ours, across = even_sum[0] + near_sum[0], (even_sum[1] + near_sum[1]).astype(bf16)
    far_sum = exchange(across, "z", 2)
    weight_grad = own_grad + over_x.astype(f32)
    far_sum, weight_grad = barrier((far_sum, weight_grad))
    layer_out = (ours + far_sum.astype(f32)).astype(bf16)
    return layer_out, gate_grad, up_grad, weight_grad


def column_span(width):
    return max((s for s in range(128, 641, 128) if width % s == 0), default=0)


def body(gate_pre, up_pre, down_codes, down_scales, cotangent):
    group_rows, local_hidden = gate_pre.shape
    owned, width = down_codes.shape
    nz, nx, ny, nc = (lax.axis_size(name) for name in ("z", "x", "y", "c"))
    rows = cotangent.shape[0]
    units = nx * owned
    total_tokens = group_rows * nz * nx

    gate_value = gate_pre.astype(jnp.float32)
    up_value = up_pre.astype(jnp.float32)
    sigmoid_gate = jax.nn.sigmoid(gate_value)
    activated = gate_value * sigmoid_gate
    hidden = (activated * up_value).astype(jnp.bfloat16)

    sent = hidden.T.reshape(nz, units, group_rows)
    columns = lax.all_to_all(sent, "z", 0, 0, tiled=True) if nz > 1 else sent

    line = lax.all_gather(cotangent, ("z", "y"), axis=0)
    both = gather_pair(line, "c")
    received = jnp.moveaxis(both, 0, 1).reshape(nz, group_rows, width)

    weight = gather_pair(dequantize(down_codes, down_scales), "x").reshape(units, width)

    partial_out = lax.dot_general(
        columns, weight, (((1,), (0,)), ((), ())), preferred_element_type=jnp.float32
    ).astype(jnp.bfloat16)
    partial_out = partial_out.reshape(nz, ny, nc, rows, width)
    over_c = scatter_sum(jnp.moveaxis(partial_out, 2, 0), "c")
    over_y = scatter_sum(jnp.moveaxis(over_c.astype(jnp.bfloat16), 1, 0), "y")
    layer_out = scatter_sum(over_y.astype(jnp.bfloat16), "z").astype(jnp.bfloat16)

    dcolumns = lax.dot_general(
        weight, received, (((1,), (2,)), ((), ())), preferred_element_type=jnp.float32
    ).astype(jnp.bfloat16)
    dcolumns = jnp.moveaxis(dcolumns, 1, 0)
    back = lax.all_to_all(dcolumns, "z", 0, 0, tiled=True) if nz > 1 else dcolumns
    dhidden = back.reshape(local_hidden, group_rows).T.astype(jnp.float32)
    gate_grad = (
        dhidden * up_value * sigmoid_gate * (1.0 + gate_value * (1.0 - sigmoid_gate))
    ).astype(jnp.bfloat16)
    up_grad = (dhidden * activated).astype(jnp.bfloat16)

    partial_grad = lax.dot_general(
        columns, received, (((0, 2), (0, 1)), ((), ())), preferred_element_type=jnp.float32
    )
    weight_grad = scatter_sum(partial_grad.reshape(nx, owned, width), "x") * float(total_tokens) ** (-0.5)
    return layer_out, gate_grad, up_grad, weight_grad


def outer_split(mesh, tokens, hidden, width):
    dp, tensor = mesh.shape["dp"], mesh.shape["tensor"]

    def rows_sent(nz):
        moved = 2 * (tokens // dp) * (hidden // tensor) / width if nz > 1 else 0
        return 2 * hidden // (tensor * nz) + 2 * tokens * nz // dp + moved

    return min((nz for nz in range(1, dp + 1) if dp % nz == 0), key=rows_sent)


def solution(mesh):
    def call(gate_pre, up_pre, down_codes, down_scales, cotangent):
        tokens, hidden = gate_pre.shape
        nz = outer_split(mesh, tokens, hidden, cotangent.shape[1])
        dp, tensor = mesh.shape["dp"], mesh.shape["tensor"]
        fine = Mesh(mesh.devices.reshape(nz, dp // nz, tensor // 2, 2), ("z", "x", "y", "c"))
        act = P(("z", "x"), ("y", "c"))
        weight = P(("y", "c", "z", "x"), None)
        layer = P(("z", "x", "y", "c"), None)
        owned = hidden // (dp * tensor)
        rows = tokens // (dp * tensor)
        pairs = fine.shape["x"] == 2 and fine.shape["y"] == 2 and nz == 4
        aligned = owned % 16 == 0 and rows % 16 == 0 and column_span(hidden // tensor)
        nblocks = down_scales.shape[1]
        blocks = nblocks > 2 and cotangent.shape[1] // nblocks % 128 == 0
        return jax.shard_map(
            paired_body if pairs and aligned and blocks else body,
            mesh=fine,
            in_specs=(act, act, weight, weight, layer),
            out_specs=(layer, act, act, weight),
            check_vma=False,
        )(gate_pre, up_pre, down_codes, down_scales, cotangent)

    return call
```

```python
import functools

import jax
import jax.numpy as jnp
from jax import lax
from jax.experimental import pallas as pl
from jax.experimental.pallas import tpu as pltpu
from jax.sharding import Mesh, PartitionSpec as P

VMEM_BYTES = 32 * 2**20


def dequantize(codes, scales):
    rows, width = codes.shape
    nblocks = scales.shape[1]
    blocks = codes.astype(jnp.float32).reshape(rows, nblocks, width // nblocks) * scales[:, :, None]
    return blocks.reshape(rows, width).astype(jnp.bfloat16)


def swap(value, axis):
    return lax.ppermute(value, axis, [(0, 1), (1, 0)])


def gather_pair(value, axis):
    if lax.axis_size(axis) != 2:
        return lax.all_gather(value, axis, axis=0)
    other = swap(value, axis)
    first = lax.axis_index(axis) == 0
    return jnp.stack([jnp.where(first, value, other), jnp.where(first, other, value)])


def scatter_sum(parts, axis):
    size = lax.axis_size(axis)
    if size == 1:
        return parts[0].astype(jnp.float32)
    if size != 2:
        received = lax.all_to_all(parts.astype(jnp.bfloat16), axis, 0, 0, tiled=True)
        return jnp.sum(received.astype(jnp.float32), axis=0)
    me = lax.axis_index(axis)
    theirs = lax.dynamic_index_in_dim(parts, 1 - me, 0, keepdims=False).astype(jnp.bfloat16)
    mine = lax.dynamic_index_in_dim(parts, me, 0, keepdims=False)
    return mine.astype(jnp.float32) + swap(theirs, axis).astype(jnp.float32)


def exchange(value, axis, offset):
    size = lax.axis_size(axis)
    return lax.ppermute(value, axis, [(i, i ^ offset) for i in range(size)])


def call_kernel(kernel, place, inputs, in_specs, out_shapes, out_specs, grid, scratch, cost):
    flops, nbytes, transcendentals = cost
    return pl.pallas_call(
        kernel,
        out_shape=out_shapes,
        grid_spec=pltpu.PrefetchScalarGridSpec(
            num_scalar_prefetch=1,
            grid=grid,
            in_specs=in_specs,
            out_specs=out_specs,
            scratch_shapes=scratch,
        ),
        compiler_params=pltpu.CompilerParams(vmem_limit_bytes=VMEM_BYTES),
        cost_estimate=pl.CostEstimate(
            flops=flops, bytes_accessed=nbytes, transcendentals=transcendentals
        ),
    )(place, *inputs)


def whole(shape):
    return pl.BlockSpec(shape, lambda i, place: (0,) * len(shape))


def token_start(place, block, rows):
    return pl.multiple_of(((place[2] ^ (block % 2)) * 2 + (place[3] ^ (block // 2))) * rows, 16)


def hidden_kernel(parts, units, place, gate, up, *refs):
    outs, (natural, columns) = refs[: len(parts)], refs[len(parts) :]
    step = pl.program_id(0)
    group, span = gate.shape
    rows = group // 4
    value = gate[...].astype(jnp.float32)
    hidden = value * jax.nn.sigmoid(value) * up[...].astype(jnp.float32)
    natural[...] = hidden.astype(jnp.bfloat16)
    ordered = [natural[pl.ds(token_start(place, b, rows), rows), :] for b in range(4)]
    columns[pl.ds(pl.multiple_of(step * span, 128), span), :] = jnp.concatenate(ordered, axis=0).T

    @pl.when(step == pl.num_programs(0) - 1)
    def _():
        half = units // 2
        for out, (k, first, count) in zip(outs, parts):
            for r in range(count):
                start = (place[0] ^ k) * units + (place[1] ^ (first + r)) * half
                out[r * half : (r + 1) * half, :] = columns[
                    pl.ds(pl.multiple_of(start, 16), half), :
                ]


def weight_kernel(place, codes, scales, *halves):
    span = codes.shape[1] // scales.shape[1]
    for block in range(scales.shape[1]):
        value = codes[:, block * span : (block + 1) * span].astype(jnp.float32)
        value = (value * scales[:, block : block + 1]).astype(jnp.bfloat16)
        at = block * span
        half, at = (0, at) if at < halves[0].shape[1] else (1, at - halves[0].shape[1])
        halves[half][:, at : at + span] = value


def join_kernel(place, own_a, own_b, other_a, other_b, weight):
    half, middle = own_a.shape
    weight[:half, :middle] = own_a[...]
    weight[:half, middle:] = own_b[...]
    weight[half:, :middle] = other_a[...]
    weight[half:, middle:] = other_b[...]


def tokens_kernel(picks, place, *refs):
    tokens = refs[-1]
    rows = refs[0].shape[-2]
    for at, (array, block) in enumerate(picks):
        source = refs[array]
        tokens[at * rows : (at + 1) * rows, :] = source[block] if len(source.shape) == 3 else source[...]


def columns_kernel(parts, by_rows, by_lanes, place, *refs):
    pieces, (keep, send, *rest) = refs[: len(parts)], refs[len(parts) :]
    half, group = rest[0].shape[0], pieces[0].shape[1]
    rows = group // 4
    for piece, (k, first, count) in zip(pieces, parts):
        turned = piece[...].T
        row, lane = by_rows.index(k), by_lanes.index(k)
        lanes = slice(lane % 2 * group, (lane % 2 + 1) * group)
        for b in range(4):
            target = send if b >= 2 else keep
            start = ((b % 2) * len(by_rows) + row) * rows
            target[start : start + rows, first * half : (first + count) * half] = turned[
                b * rows : (b + 1) * rows, :
            ]
        for r in range(count):
            rest[lane // 2 * 2 + first + r][:, lanes] = piece[r * half : (r + 1) * half, :]


def grads_kernel(parts, units, place, gate, up, *refs):
    pieces, (gate_grad, up_grad, columns, natural) = refs[: len(parts)], refs[len(parts) :]
    step = pl.program_id(0)
    group, span = gate.shape
    rows = group // 4

    @pl.when(step == 0)
    def _():
        half = units // 2
        for piece, (k, first, count) in zip(pieces, parts):
            for r in range(count):
                start = (place[0] ^ k) * units + (place[1] ^ (first + r)) * half
                columns[pl.ds(pl.multiple_of(start, 16), half), :] = piece[
                    r * half : (r + 1) * half, :
                ]

    ordered = columns[pl.ds(pl.multiple_of(step * span, 128), span), :].T
    for b in range(4):
        natural[pl.ds(token_start(place, b, rows), rows), :] = ordered[b * rows : (b + 1) * rows]
    dhidden = natural[...].astype(jnp.float32)
    value = gate[...].astype(jnp.float32)
    up_value = up[...].astype(jnp.float32)
    sigmoid_gate = jax.nn.sigmoid(value)
    gate_grad[...] = (
        dhidden * up_value * sigmoid_gate * (1.0 + value * (1.0 - sigmoid_gate))
    ).astype(jnp.bfloat16)
    up_grad[...] = (dhidden * (value * sigmoid_gate)).astype(jnp.bfloat16)


def matmul(lhs, rhs, lhs_dim=1, rhs_dim=0, dtype=jnp.float32):
    dims = (((lhs_dim,), (rhs_dim,)), ((), ()))
    return lax.dot_general(lhs, rhs, dims, preferred_element_type=jnp.float32).astype(dtype)


def paired_body(gate_pre, up_pre, down_codes, down_scales, cotangent):
    group_rows, local_hidden = gate_pre.shape
    owned, width = down_codes.shape
    rows = cotangent.shape[0]
    nz, units, nblocks = 4, 2 * owned, down_scales.shape[1]
    middle = 3 * nblocks // 5 * (width // nblocks)
    total_tokens = group_rows * nz * 2
    bf16, f32 = jnp.bfloat16, jnp.float32
    place = jnp.stack([lax.axis_index(name) for name in ("z", "x", "y", "c")]).astype(jnp.int32)
    struct = jax.ShapeDtypeStruct
    barrier = lax.optimization_barrier

    far, near = exchange(cotangent, "z", 2), exchange(cotangent, "z", 1)
    own_y, own_c = exchange(cotangent, "y", 1), exchange(cotangent, "c", 1)

    sides = ((owned, middle), (owned, width - middle))
    own_a, own_b = call_kernel(
        weight_kernel, place, (down_codes, down_scales),
        [whole(down_codes.shape), whole(down_scales.shape)],
        [struct(shape, bf16) for shape in sides], [whole(shape) for shape in sides], (1,), [],
        (2 * owned * width, 4 * owned * width, 0),
    )
    other_a = exchange(own_a, "x", 1)

    parts = tuple((k, 0, 2) for k in (0, 2, 3, 1))
    pieces = [struct((count * owned, group_rows), bf16) for _, _, count in parts]
    piece_specs = [whole(piece.shape) for piece in pieces]
    span = column_span(local_hidden)
    steps = local_hidden // span
    wide = pl.BlockSpec((group_rows, span), lambda i, place: (0, i))
    act_bytes = group_rows * local_hidden * 2
    act_scratch = [pltpu.VMEM((group_rows, span), bf16), pltpu.VMEM((local_hidden, group_rows), bf16)]
    sent = call_kernel(
        functools.partial(hidden_kernel, parts, units), place, (gate_pre, up_pre), [wide] * 2,
        pieces, piece_specs, (steps,), act_scratch,
        (4 * act_bytes, 3 * act_bytes, act_bytes // 2),
    )

    far, near, own_y, own_c, sent = barrier((far, near, own_y, own_c, sent))
    last = exchange(far, "z", 1)
    other_y = exchange(jnp.stack([far, near]), "y", 1)
    other_b = exchange(own_b, "x", 1)
    columns = [sent[0], exchange(sent[1], "z", 2)]
    first_c = exchange(jnp.stack([own_y, far, near]), "c", 1)
    last, other_y, columns, other_a, sent, first_c = barrier(
        (last, other_y, columns, other_a, sent, first_c)
    )

    last_y = exchange(last, "y", 1)
    columns += [exchange(sent[i], "z", parts[i][0]) for i in range(2, len(parts))]
    other_c = exchange(jnp.stack([other_y[0], other_y[1], last]), "c", 1)
    last_y, columns, other_b = barrier((last_y, columns, other_b))
    last_c = exchange(last_y, "c", 1)

    weight = call_kernel(
        join_kernel, place, (own_a, own_b, other_a, other_b),
        [whole(shape) for shape in sides] * 2,
        struct((units, width), bf16), whole((units, width)), (1,), [],
        (0, 4 * units * width, 0),
    )

    half_tokens = nz * group_rows // 2
    by_rows, by_lanes = (1, 3, 0, 2), (0, 2, 1, 3)
    keep, send, *by_units = call_kernel(
        functools.partial(columns_kernel, parts, by_rows, by_lanes), place, columns, piece_specs,
        [struct((half_tokens, units), bf16)] * 2 + [struct((owned, half_tokens), bf16)] * 4,
        [whole((half_tokens, units))] * 2 + [whole((owned, half_tokens))] * 4, (1,), [],
        (0, 12 * units * half_tokens, 0),
    )

    def gather_tokens(arrays, picks):
        return call_kernel(
            functools.partial(tokens_kernel, picks), place, arrays,
            [whole(array.shape) for array in arrays], struct((half_tokens, width), bf16),
            whole((half_tokens, width)), (1,), [], (0, 4 * half_tokens * width, 0),
        )

    send, last_c = barrier((send, last_c))
    even = gather_tokens(
        (cotangent, own_y, own_c, far, other_y, first_c, other_c),
        ((0, 0), (1, 0), (2, 0), (5, 0), (3, 0), (4, 0), (5, 1), (6, 0)),
    )
    odd = gather_tokens(
        (near, last, last_y, other_y, first_c, other_c, last_c),
        ((0, 0), (3, 1), (4, 2), (5, 1), (1, 0), (2, 0), (5, 2), (6, 0)),
    )
    factor = float(total_tokens) ** (-0.5)


    def grad_half(r, low=0, high=owned):
        first, second = by_units[r][low:high], by_units[2 + r][low:high]
        return (matmul(first, flat[0]) + matmul(second, flat[1])) * factor

    def back_of(k, low=0, high=units):
        rows_of_k = flat[k % 2][k // 2 * group_rows : (k // 2 + 1) * group_rows]
        return matmul(weight[low:high], rows_of_k, 1, 1, bf16)

    given = matmul(send, weight, dtype=bf16)
    given, even = barrier((given, even))
    flat = [even, odd]
    far_back = back_of(2)
    far_back, flat = barrier((far_back, flat))
    over_c = exchange(given, "c", 1)
    theirs = grad_half(1).astype(bf16)
    theirs, keep, flat = barrier((theirs, keep, flat))
    over_x = exchange(theirs, "x", 1)
    kept = matmul(keep, weight, dtype=bf16)
    sums = (kept.astype(f32) + over_c.astype(f32)).reshape(2, nz, rows, width)
    sums, flat = barrier((sums, flat))
    odd_y = exchange(sums[1, :2].astype(bf16), "y", 1)
    even_y = exchange(sums[1, 2:].astype(bf16), "y", 1)
    far_back = exchange(far_back, "z", 2)
    near_back = exchange(back_of(1), "z", 1)
    last_back, far_back = barrier((back_of(3, 0, owned), far_back))
    last_back = exchange(last_back, "z", 3)
    odd_y, flat = barrier((odd_y, flat))
    odd_sum = (sums[0, :2] + odd_y.astype(f32)).astype(bf16)
    odd_sum, far_back, last_back = barrier((odd_sum, far_back, last_back))
    near_sum, even_y = barrier((exchange(odd_sum, "z", 1), even_y))
    back = [back_of(0), near_back, far_back, last_back, exchange(back_of(3, owned, units), "z", 3)]
    near_sum = near_sum.astype(f32)
    even_sum = sums[0, 2:] + even_y.astype(f32)
    ours, across = even_sum[0] + near_sum[0], (even_sum[1] + near_sum[1]).astype(bf16)
    far_sum = exchange(across, "z", 2)
    back, flat, _ = barrier((back, flat, across))
    back_parts = tuple((k, 0, 2) for k in range(3)) + ((3, 0, 1), (3, 1, 1))
    gate_grad, up_grad = call_kernel(
        functools.partial(grads_kernel, back_parts, units), place, (gate_pre, up_pre, *back),
        [wide] * 2 + [whole(value.shape) for value in back],
        [struct((group_rows, local_hidden), bf16)] * 2, [wide] * 2, (steps,), act_scratch[::-1],
        (12 * act_bytes, 5 * act_bytes, act_bytes // 2),
    )
    over_x, _ = barrier((over_x, gate_grad))
    weight_grad = grad_half(0) + over_x.astype(f32)
    far_sum, weight_grad = barrier((far_sum, weight_grad))
    layer_out = (ours + far_sum.astype(f32)).astype(bf16)
    return layer_out, gate_grad, up_grad, weight_grad


def column_span(width):
    return max((s for s in range(128, 641, 128) if width % s == 0), default=0)


def body(gate_pre, up_pre, down_codes, down_scales, cotangent):
    group_rows, local_hidden = gate_pre.shape
    owned, width = down_codes.shape
    nz, nx, ny, nc = (lax.axis_size(name) for name in ("z", "x", "y", "c"))
    rows = cotangent.shape[0]
    units = nx * owned
    total_tokens = group_rows * nz * nx

    gate_value = gate_pre.astype(jnp.float32)
    up_value = up_pre.astype(jnp.float32)
    sigmoid_gate = jax.nn.sigmoid(gate_value)
    activated = gate_value * sigmoid_gate
    hidden = (activated * up_value).astype(jnp.bfloat16)

    sent = hidden.T.reshape(nz, units, group_rows)
    columns = lax.all_to_all(sent, "z", 0, 0, tiled=True) if nz > 1 else sent

    line = lax.all_gather(cotangent, ("z", "y"), axis=0)
    both = gather_pair(line, "c")
    received = jnp.moveaxis(both, 0, 1).reshape(nz, group_rows, width)

    weight = gather_pair(dequantize(down_codes, down_scales), "x").reshape(units, width)

    partial_out = lax.dot_general(
        columns, weight, (((1,), (0,)), ((), ())), preferred_element_type=jnp.float32
    ).astype(jnp.bfloat16)
    partial_out = partial_out.reshape(nz, ny, nc, rows, width)
    over_c = scatter_sum(jnp.moveaxis(partial_out, 2, 0), "c")
    over_y = scatter_sum(jnp.moveaxis(over_c.astype(jnp.bfloat16), 1, 0), "y")
    layer_out = scatter_sum(over_y.astype(jnp.bfloat16), "z").astype(jnp.bfloat16)

    dcolumns = lax.dot_general(
        weight, received, (((1,), (2,)), ((), ())), preferred_element_type=jnp.float32
    ).astype(jnp.bfloat16)
    dcolumns = jnp.moveaxis(dcolumns, 1, 0)
    back = lax.all_to_all(dcolumns, "z", 0, 0, tiled=True) if nz > 1 else dcolumns
    dhidden = back.reshape(local_hidden, group_rows).T.astype(jnp.float32)
    gate_grad = (
        dhidden * up_value * sigmoid_gate * (1.0 + gate_value * (1.0 - sigmoid_gate))
    ).astype(jnp.bfloat16)
    up_grad = (dhidden * activated).astype(jnp.bfloat16)

    partial_grad = lax.dot_general(
        columns, received, (((0, 2), (0, 1)), ((), ())), preferred_element_type=jnp.float32
    )
    weight_grad = scatter_sum(partial_grad.reshape(nx, owned, width), "x") * float(total_tokens) ** (-0.5)
    return layer_out, gate_grad, up_grad, weight_grad


def outer_split(mesh, tokens, hidden, width):
    dp, tensor = mesh.shape["dp"], mesh.shape["tensor"]

    def rows_sent(nz):
        moved = 2 * (tokens // dp) * (hidden // tensor) / width if nz > 1 else 0
        return 2 * hidden // (tensor * nz) + 2 * tokens * nz // dp + moved

    return min((nz for nz in range(1, dp + 1) if dp % nz == 0), key=rows_sent)


def solution(mesh):
    def call(gate_pre, up_pre, down_codes, down_scales, cotangent):
        tokens, hidden = gate_pre.shape
        nz = outer_split(mesh, tokens, hidden, cotangent.shape[1])
        dp, tensor = mesh.shape["dp"], mesh.shape["tensor"]
        fine = Mesh(mesh.devices.reshape(nz, dp // nz, tensor // 2, 2), ("z", "x", "y", "c"))
        act = P(("z", "x"), ("y", "c"))
        weight = P(("y", "c", "z", "x"), None)
        layer = P(("z", "x", "y", "c"), None)
        owned = hidden // (dp * tensor)
        rows = tokens // (dp * tensor)
        pairs = fine.shape["x"] == 2 and fine.shape["y"] == 2 and nz == 4
        aligned = owned % 16 == 0 and rows % 16 == 0 and column_span(hidden // tensor)
        nblocks = down_scales.shape[1]
        blocks = nblocks > 2 and cotangent.shape[1] // nblocks % 128 == 0
        return jax.shard_map(
            paired_body if pairs and aligned and blocks else body,
            mesh=fine,
            in_specs=(act, act, weight, weight, layer),
            out_specs=(layer, act, act, weight),
            check_vma=False,
        )(gate_pre, up_pre, down_codes, down_scales, cotangent)

    return call
```

```python
import functools

import jax
import jax.numpy as jnp
from jax import lax
from jax.experimental import pallas as pl
from jax.experimental.pallas import tpu as pltpu
from jax.sharding import Mesh, PartitionSpec as P

VMEM_BYTES = 32 * 2**20


def dequantize(codes, scales):
    rows, width = codes.shape
    nblocks = scales.shape[1]
    blocks = codes.astype(jnp.float32).reshape(rows, nblocks, width // nblocks) * scales[:, :, None]
    return blocks.reshape(rows, width).astype(jnp.bfloat16)


def swap(value, axis):
    return lax.ppermute(value, axis, [(0, 1), (1, 0)])


def gather_pair(value, axis):
    if lax.axis_size(axis) != 2:
        return lax.all_gather(value, axis, axis=0)
    other = swap(value, axis)
    first = lax.axis_index(axis) == 0
    return jnp.stack([jnp.where(first, value, other), jnp.where(first, other, value)])


def scatter_sum(parts, axis):
    size = lax.axis_size(axis)
    if size == 1:
        return parts[0].astype(jnp.float32)
    if size != 2:
        received = lax.all_to_all(parts.astype(jnp.bfloat16), axis, 0, 0, tiled=True)
        return jnp.sum(received.astype(jnp.float32), axis=0)
    me = lax.axis_index(axis)
    theirs = lax.dynamic_index_in_dim(parts, 1 - me, 0, keepdims=False).astype(jnp.bfloat16)
    mine = lax.dynamic_index_in_dim(parts, me, 0, keepdims=False)
    return mine.astype(jnp.float32) + swap(theirs, axis).astype(jnp.float32)


def exchange(value, axis, offset):
    size = lax.axis_size(axis)
    return lax.ppermute(value, axis, [(i, i ^ offset) for i in range(size)])


def call_kernel(kernel, place, inputs, in_specs, out_shapes, out_specs, grid, scratch, cost):
    flops, nbytes, transcendentals = cost
    return pl.pallas_call(
        kernel,
        out_shape=out_shapes,
        grid_spec=pltpu.PrefetchScalarGridSpec(
            num_scalar_prefetch=1,
            grid=grid,
            in_specs=in_specs,
            out_specs=out_specs,
            scratch_shapes=scratch,
        ),
        compiler_params=pltpu.CompilerParams(vmem_limit_bytes=VMEM_BYTES),
        cost_estimate=pl.CostEstimate(
            flops=flops, bytes_accessed=nbytes, transcendentals=transcendentals
        ),
    )(place, *inputs)


def whole(shape):
    return pl.BlockSpec(shape, lambda i, place: (0,) * len(shape))


def token_start(place, block, rows):
    return pl.multiple_of(((place[2] ^ (block % 2)) * 2 + (place[3] ^ (block // 2))) * rows, 16)


def hidden_kernel(parts, units, place, gate, up, *refs):
    outs, (natural, columns) = refs[: len(parts)], refs[len(parts) :]
    step = pl.program_id(0)
    group, span = gate.shape
    rows = group // 4
    value = gate[...].astype(jnp.float32)
    hidden = value * jax.nn.sigmoid(value) * up[...].astype(jnp.float32)
    natural[...] = hidden.astype(jnp.bfloat16)
    ordered = [natural[pl.ds(token_start(place, b, rows), rows), :] for b in range(4)]
    columns[pl.ds(pl.multiple_of(step * span, 128), span), :] = jnp.concatenate(ordered, axis=0).T

    @pl.when(step == pl.num_programs(0) - 1)
    def _():
        half = units // 2
        for out, (k, first, count) in zip(outs, parts):
            for r in range(count):
                start = (place[0] ^ k) * units + (place[1] ^ (first + r)) * half
                out[r * half : (r + 1) * half, :] = columns[
                    pl.ds(pl.multiple_of(start, 16), half), :
                ]


def weight_kernel(place, codes, scales, *halves):
    span = codes.shape[1] // scales.shape[1]
    for block in range(scales.shape[1]):
        value = codes[:, block * span : (block + 1) * span].astype(jnp.float32)
        value = (value * scales[:, block : block + 1]).astype(jnp.bfloat16)
        at = block * span
        half, at = (0, at) if at < halves[0].shape[1] else (1, at - halves[0].shape[1])
        halves[half][:, at : at + span] = value


def join_kernel(place, own_a, own_b, other_a, other_b, weight):
    half, middle = own_a.shape
    weight[:half, :middle] = own_a[...]
    weight[:half, middle:] = own_b[...]
    weight[half:, :middle] = other_a[...]
    weight[half:, middle:] = other_b[...]


def tokens_kernel(picks, place, *refs):
    tokens = refs[-1]
    rows = refs[0].shape[-2]
    for at, (array, block) in enumerate(picks):
        source = refs[array]
        tokens[at * rows : (at + 1) * rows, :] = source[block] if len(source.shape) == 3 else source[...]


def columns_kernel(parts, by_rows, by_lanes, place, *refs):
    pieces, (keep, send, *rest) = refs[: len(parts)], refs[len(parts) :]
    half, group = rest[0].shape[0], pieces[0].shape[1]
    rows = group // 4
    for piece, (k, first, count) in zip(pieces, parts):
        turned = piece[...].T
        row, lane = by_rows.index(k), by_lanes.index(k)
        lanes = slice(lane % 2 * group, (lane % 2 + 1) * group)
        for b in range(4):
            target = send if b >= 2 else keep
            start = ((b % 2) * len(by_rows) + row) * rows
            target[start : start + rows, first * half : (first + count) * half] = turned[
                b * rows : (b + 1) * rows, :
            ]
        for r in range(count):
            rest[lane // 2 * 2 + first + r][:, lanes] = piece[r * half : (r + 1) * half, :]


def grads_kernel(nz, units, place, gate, up, *refs):
    pieces, (gate_grad, up_grad, columns, natural) = refs[:nz], refs[nz:]
    step = pl.program_id(0)
    group, span = gate.shape
    rows = group // 4

    @pl.when(step == 0)
    def _():
        half = units // 2
        for k in range(nz):
            for r in range(2):
                start = (place[0] ^ k) * units + (place[1] ^ r) * half
                columns[pl.ds(pl.multiple_of(start, 16), half), :] = pieces[k][
                    r * half : (r + 1) * half, :
                ]

    ordered = columns[pl.ds(pl.multiple_of(step * span, 128), span), :].T
    for b in range(4):
        natural[pl.ds(token_start(place, b, rows), rows), :] = ordered[b * rows : (b + 1) * rows]
    dhidden = natural[...].astype(jnp.float32)
    value = gate[...].astype(jnp.float32)
    up_value = up[...].astype(jnp.float32)
    sigmoid_gate = jax.nn.sigmoid(value)
    gate_grad[...] = (
        dhidden * up_value * sigmoid_gate * (1.0 + value * (1.0 - sigmoid_gate))
    ).astype(jnp.bfloat16)
    up_grad[...] = (dhidden * (value * sigmoid_gate)).astype(jnp.bfloat16)


def matmul(lhs, rhs, lhs_dim=1, rhs_dim=0, dtype=jnp.float32):
    dims = (((lhs_dim,), (rhs_dim,)), ((), ()))
    return lax.dot_general(lhs, rhs, dims, preferred_element_type=jnp.float32).astype(dtype)


def paired_body(gate_pre, up_pre, down_codes, down_scales, cotangent):
    group_rows, local_hidden = gate_pre.shape
    owned, width = down_codes.shape
    rows = cotangent.shape[0]
    nz, units, nblocks = 4, 2 * owned, down_scales.shape[1]
    middle = 3 * nblocks // 5 * (width // nblocks)
    total_tokens = group_rows * nz * 2
    bf16, f32 = jnp.bfloat16, jnp.float32
    place = jnp.stack([lax.axis_index(name) for name in ("z", "x", "y", "c")]).astype(jnp.int32)
    struct = jax.ShapeDtypeStruct
    barrier = lax.optimization_barrier

    far, near = exchange(cotangent, "z", 2), exchange(cotangent, "z", 1)
    own_y, own_c = exchange(cotangent, "y", 1), exchange(cotangent, "c", 1)

    sides = ((owned, middle), (owned, width - middle))
    own_a, own_b = call_kernel(
        weight_kernel, place, (down_codes, down_scales),
        [whole(down_codes.shape), whole(down_scales.shape)],
        [struct(shape, bf16) for shape in sides], [whole(shape) for shape in sides], (1,), [],
        (2 * owned * width, 4 * owned * width, 0),
    )
    other_a = exchange(own_a, "x", 1)

    parts = tuple((k, 0, 2) for k in (0, 2, 3, 1))
    pieces = [struct((count * owned, group_rows), bf16) for _, _, count in parts]
    piece_specs = [whole(piece.shape) for piece in pieces]
    span = column_span(local_hidden)
    steps = local_hidden // span
    wide = pl.BlockSpec((group_rows, span), lambda i, place: (0, i))
    act_bytes = group_rows * local_hidden * 2
    act_scratch = [pltpu.VMEM((group_rows, span), bf16), pltpu.VMEM((local_hidden, group_rows), bf16)]
    sent = call_kernel(
        functools.partial(hidden_kernel, parts, units), place, (gate_pre, up_pre), [wide] * 2,
        pieces, piece_specs, (steps,), act_scratch,
        (4 * act_bytes, 3 * act_bytes, act_bytes // 2),
    )

    far, near, own_y, own_c, sent = barrier((far, near, own_y, own_c, sent))
    last = exchange(far, "z", 1)
    other_y = exchange(jnp.stack([far, near]), "y", 1)
    other_b = exchange(own_b, "x", 1)
    columns = [sent[0], exchange(sent[1], "z", 2)]
    first_c = exchange(jnp.stack([own_y, far, near]), "c", 1)
    last, other_y, columns, other_a, sent, first_c = barrier(
        (last, other_y, columns, other_a, sent, first_c)
    )

    last_y = exchange(last, "y", 1)
    columns += [exchange(sent[i], "z", parts[i][0]) for i in range(2, len(parts))]
    other_c = exchange(jnp.stack([other_y[0], other_y[1], last]), "c", 1)
    weight = call_kernel(
        join_kernel, place, (own_a, own_b, other_a, other_b),
        [whole(shape) for shape in sides] * 2,
        struct((units, width), bf16), whole((units, width)), (1,), [],
        (0, 4 * units * width, 0),
    )

    half_tokens = nz * group_rows // 2

    def gather_tokens(arrays, picks):
        return call_kernel(
            functools.partial(tokens_kernel, picks), place, arrays,
            [whole(array.shape) for array in arrays], struct((half_tokens, width), bf16),
            whole((half_tokens, width)), (1,), [], (0, 4 * half_tokens * width, 0),
        )

    even = gather_tokens(
        (cotangent, own_y, own_c, far, other_y, first_c, other_c),
        ((0, 0), (1, 0), (2, 0), (5, 0), (3, 0), (4, 0), (5, 1), (6, 0)),
    )
    far_back = matmul(weight, even[group_rows:], 1, 1, bf16)
    last_y, columns, far_back, even = barrier((last_y, columns, far_back, even))
    last_c = exchange(last_y, "c", 1)
    by_rows, by_lanes = (1, 3, 0, 2), (0, 2, 1, 3)
    keep, send, *by_units = call_kernel(
        functools.partial(columns_kernel, parts, by_rows, by_lanes), place, columns, piece_specs,
        [struct((half_tokens, units), bf16)] * 2 + [struct((owned, half_tokens), bf16)] * 4,
        [whole((half_tokens, units))] * 2 + [whole((owned, half_tokens))] * 4, (1,), [],
        (0, 12 * units * half_tokens, 0),
    )

    send, keep, last_c = barrier((send, keep, last_c))
    odd = gather_tokens(
        (near, last, last_y, other_y, first_c, other_c, last_c),
        ((0, 0), (3, 1), (4, 2), (5, 1), (1, 0), (2, 0), (5, 2), (6, 0)),
    )
    flat = [even, odd]

    factor = float(total_tokens) ** (-0.5)

    def grad_half(r):
        return (matmul(by_units[r], flat[0]) + matmul(by_units[2 + r], flat[1])) * factor

    def back_of(k):
        rows_of_k = flat[k % 2][k // 2 * group_rows : (k // 2 + 1) * group_rows]
        return matmul(weight, rows_of_k, 1, 1, bf16)

    given = matmul(send, weight, dtype=bf16)
    given, flat = barrier((given, flat))
    over_c = exchange(given, "c", 1)
    theirs = grad_half(1).astype(bf16)
    near_back, far_back = barrier((back_of(1), far_back))
    theirs, keep, flat, near_back = barrier((theirs, keep, flat, near_back))
    over_x = exchange(theirs, "x", 1)
    kept = matmul(keep, weight, dtype=bf16)
    near_back, far_back = exchange(near_back, "z", 1), exchange(far_back, "z", 2)
    sums = (kept.astype(f32) + over_c.astype(f32)).reshape(2, nz, rows, width)
    odd_y = exchange(sums[1, :2].astype(bf16), "y", 1)
    even_y = exchange(sums[1, 2:].astype(bf16), "y", 1)
    odd_y, flat, near_back = barrier((odd_y, flat, near_back))
    odd_sum = (sums[0, :2] + odd_y.astype(f32)).astype(bf16)
    odd_sum, far_back = barrier((odd_sum, far_back))
    own_grad = grad_half(0)
    near_sum, even_y, own_grad = barrier((exchange(odd_sum, "z", 1), even_y, own_grad))
    back = [near_back, far_back, exchange(back_of(3), "z", 3)]
    near_sum = near_sum.astype(f32)
    even_sum = sums[0, 2:] + even_y.astype(f32)
    ours, across = even_sum[0] + near_sum[0], (even_sum[1] + near_sum[1]).astype(bf16)
    far_sum = exchange(across, "z", 2)

    back, flat, _ = barrier((back, flat, across))
    back = [back_of(0)] + back
    gate_grad, up_grad = call_kernel(
        functools.partial(grads_kernel, nz, units), place, (gate_pre, up_pre, *back),
        [wide] * 2 + [whole((units, group_rows))] * nz,
        [struct((group_rows, local_hidden), bf16)] * 2, [wide] * 2, (steps,), act_scratch[::-1],
        (12 * act_bytes, 5 * act_bytes, act_bytes // 2),
    )
    over_x, _ = barrier((over_x, gate_grad))
    weight_grad = own_grad + over_x.astype(f32)
    far_sum, weight_grad = barrier((far_sum, weight_grad))
    layer_out = (ours + far_sum.astype(f32)).astype(bf16)
    return layer_out, gate_grad, up_grad, weight_grad


def column_span(width):
    return max((s for s in range(128, 641, 128) if width % s == 0), default=0)


def body(gate_pre, up_pre, down_codes, down_scales, cotangent):
    group_rows, local_hidden = gate_pre.shape
    owned, width = down_codes.shape
    nz, nx, ny, nc = (lax.axis_size(name) for name in ("z", "x", "y", "c"))
    rows = cotangent.shape[0]
    units = nx * owned
    total_tokens = group_rows * nz * nx

    gate_value = gate_pre.astype(jnp.float32)
    up_value = up_pre.astype(jnp.float32)
    sigmoid_gate = jax.nn.sigmoid(gate_value)
    activated = gate_value * sigmoid_gate
    hidden = (activated * up_value).astype(jnp.bfloat16)

    sent = hidden.T.reshape(nz, units, group_rows)
    columns = lax.all_to_all(sent, "z", 0, 0, tiled=True) if nz > 1 else sent

    line = lax.all_gather(cotangent, ("z", "y"), axis=0)
    both = gather_pair(line, "c")
    received = jnp.moveaxis(both, 0, 1).reshape(nz, group_rows, width)

    weight = gather_pair(dequantize(down_codes, down_scales), "x").reshape(units, width)

    partial_out = lax.dot_general(
        columns, weight, (((1,), (0,)), ((), ())), preferred_element_type=jnp.float32
    ).astype(jnp.bfloat16)
    partial_out = partial_out.reshape(nz, ny, nc, rows, width)
    over_c = scatter_sum(jnp.moveaxis(partial_out, 2, 0), "c")
    over_y = scatter_sum(jnp.moveaxis(over_c.astype(jnp.bfloat16), 1, 0), "y")
    layer_out = scatter_sum(over_y.astype(jnp.bfloat16), "z").astype(jnp.bfloat16)

    dcolumns = lax.dot_general(
        weight, received, (((1,), (2,)), ((), ())), preferred_element_type=jnp.float32
    ).astype(jnp.bfloat16)
    dcolumns = jnp.moveaxis(dcolumns, 1, 0)
    back = lax.all_to_all(dcolumns, "z", 0, 0, tiled=True) if nz > 1 else dcolumns
    dhidden = back.reshape(local_hidden, group_rows).T.astype(jnp.float32)
    gate_grad = (
        dhidden * up_value * sigmoid_gate * (1.0 + gate_value * (1.0 - sigmoid_gate))
    ).astype(jnp.bfloat16)
    up_grad = (dhidden * activated).astype(jnp.bfloat16)

    partial_grad = lax.dot_general(
        columns, received, (((0, 2), (0, 1)), ((), ())), preferred_element_type=jnp.float32
    )
    weight_grad = scatter_sum(partial_grad.reshape(nx, owned, width), "x") * float(total_tokens) ** (-0.5)
    return layer_out, gate_grad, up_grad, weight_grad


def outer_split(mesh, tokens, hidden, width):
    dp, tensor = mesh.shape["dp"], mesh.shape["tensor"]

    def rows_sent(nz):
        moved = 2 * (tokens // dp) * (hidden // tensor) / width if nz > 1 else 0
        return 2 * hidden // (tensor * nz) + 2 * tokens * nz // dp + moved

    return min((nz for nz in range(1, dp + 1) if dp % nz == 0), key=rows_sent)


def solution(mesh):
    def call(gate_pre, up_pre, down_codes, down_scales, cotangent):
        tokens, hidden = gate_pre.shape
        nz = outer_split(mesh, tokens, hidden, cotangent.shape[1])
        dp, tensor = mesh.shape["dp"], mesh.shape["tensor"]
        fine = Mesh(mesh.devices.reshape(nz, dp // nz, tensor // 2, 2), ("z", "x", "y", "c"))
        act = P(("z", "x"), ("y", "c"))
        weight = P(("y", "c", "z", "x"), None)
        layer = P(("z", "x", "y", "c"), None)
        owned = hidden // (dp * tensor)
        rows = tokens // (dp * tensor)
        pairs = fine.shape["x"] == 2 and fine.shape["y"] == 2 and nz == 4
        aligned = owned % 16 == 0 and rows % 16 == 0 and column_span(hidden // tensor)
        nblocks = down_scales.shape[1]
        blocks = nblocks > 2 and cotangent.shape[1] // nblocks % 128 == 0
        return jax.shard_map(
            paired_body if pairs and aligned and blocks else body,
            mesh=fine,
            in_specs=(act, act, weight, weight, layer),
            out_specs=(layer, act, act, weight),
            check_vma=False,
        )(gate_pre, up_pre, down_codes, down_scales, cotangent)

    return call
```

```python
import functools

import jax
import jax.numpy as jnp
from jax import lax
from jax.experimental import pallas as pl
from jax.experimental.pallas import tpu as pltpu
from jax.sharding import Mesh, PartitionSpec as P

VMEM_BYTES = 32 * 2**20


def dequantize(codes, scales):
    rows, width = codes.shape
    nblocks = scales.shape[1]
    blocks = codes.astype(jnp.float32).reshape(rows, nblocks, width // nblocks) * scales[:, :, None]
    return blocks.reshape(rows, width).astype(jnp.bfloat16)


def swap(value, axis):
    return lax.ppermute(value, axis, [(0, 1), (1, 0)])


def gather_pair(value, axis):
    if lax.axis_size(axis) != 2:
        return lax.all_gather(value, axis, axis=0)
    other = swap(value, axis)
    first = lax.axis_index(axis) == 0
    return jnp.stack([jnp.where(first, value, other), jnp.where(first, other, value)])


def scatter_sum(parts, axis):
    size = lax.axis_size(axis)
    if size == 1:
        return parts[0].astype(jnp.float32)
    if size != 2:
        received = lax.all_to_all(parts.astype(jnp.bfloat16), axis, 0, 0, tiled=True)
        return jnp.sum(received.astype(jnp.float32), axis=0)
    me = lax.axis_index(axis)
    theirs = lax.dynamic_index_in_dim(parts, 1 - me, 0, keepdims=False).astype(jnp.bfloat16)
    mine = lax.dynamic_index_in_dim(parts, me, 0, keepdims=False)
    return mine.astype(jnp.float32) + swap(theirs, axis).astype(jnp.float32)


def exchange(value, axis, offset):
    size = lax.axis_size(axis)
    return lax.ppermute(value, axis, [(i, i ^ offset) for i in range(size)])


def call_kernel(kernel, place, inputs, in_specs, out_shapes, out_specs, grid, scratch, cost):
    flops, nbytes, transcendentals = cost
    return pl.pallas_call(
        kernel,
        out_shape=out_shapes,
        grid_spec=pltpu.PrefetchScalarGridSpec(
            num_scalar_prefetch=1,
            grid=grid,
            in_specs=in_specs,
            out_specs=out_specs,
            scratch_shapes=scratch,
        ),
        compiler_params=pltpu.CompilerParams(vmem_limit_bytes=VMEM_BYTES),
        cost_estimate=pl.CostEstimate(
            flops=flops, bytes_accessed=nbytes, transcendentals=transcendentals
        ),
    )(place, *inputs)


def whole(shape):
    return pl.BlockSpec(shape, lambda i, place: (0,) * len(shape))


def token_start(place, block, rows):
    return pl.multiple_of(((place[2] ^ (block % 2)) * 2 + (place[3] ^ (block // 2))) * rows, 16)


def hidden_kernel(parts, units, place, gate, up, *refs):
    outs, (natural, columns) = refs[: len(parts)], refs[len(parts) :]
    step = pl.program_id(0)
    group, span = gate.shape
    rows = group // 4
    value = gate[...].astype(jnp.float32)
    hidden = value * jax.nn.sigmoid(value) * up[...].astype(jnp.float32)
    natural[...] = hidden.astype(jnp.bfloat16)
    ordered = [natural[pl.ds(token_start(place, b, rows), rows), :] for b in range(4)]
    columns[pl.ds(pl.multiple_of(step * span, 128), span), :] = jnp.concatenate(ordered, axis=0).T

    @pl.when(step == pl.num_programs(0) - 1)
    def _():
        half = units // 2
        for out, (k, first, count) in zip(outs, parts):
            for r in range(count):
                start = (place[0] ^ k) * units + (place[1] ^ (first + r)) * half
                out[r * half : (r + 1) * half, :] = columns[
                    pl.ds(pl.multiple_of(start, 16), half), :
                ]


def weight_kernel(place, codes, scales, *halves):
    span = codes.shape[1] // scales.shape[1]
    for block in range(scales.shape[1]):
        value = codes[:, block * span : (block + 1) * span].astype(jnp.float32)
        value = (value * scales[:, block : block + 1]).astype(jnp.bfloat16)
        at = block * span
        half, at = (0, at) if at < halves[0].shape[1] else (1, at - halves[0].shape[1])
        halves[half][:, at : at + span] = value


def join_kernel(place, own_a, own_b, other_a, other_b, weight):
    half, middle = own_a.shape
    weight[:half, :middle] = own_a[...]
    weight[:half, middle:] = own_b[...]
    weight[half:, :middle] = other_a[...]
    weight[half:, middle:] = other_b[...]


def tokens_kernel(picks, place, *refs):
    tokens = refs[-1]
    rows = refs[0].shape[-2]
    for at, (array, block) in enumerate(picks):
        source = refs[array]
        tokens[at * rows : (at + 1) * rows, :] = source[block] if len(source.shape) == 3 else source[...]


def columns_kernel(parts, by_rows, by_lanes, place, *refs):
    pieces, (keep, send, *rest) = refs[: len(parts)], refs[len(parts) :]
    half, group = rest[0].shape[0], pieces[0].shape[1]
    rows = group // 4
    for piece, (k, first, count) in zip(pieces, parts):
        turned = piece[...].T
        row, lane = by_rows.index(k), by_lanes.index(k)
        lanes = slice(lane % 2 * group, (lane % 2 + 1) * group)
        for b in range(4):
            target = send if b >= 2 else keep
            start = ((b % 2) * len(by_rows) + row) * rows
            target[start : start + rows, first * half : (first + count) * half] = turned[
                b * rows : (b + 1) * rows, :
            ]
        for r in range(count):
            rest[lane // 2 * 2 + first + r][:, lanes] = piece[r * half : (r + 1) * half, :]


def grads_kernel(nz, units, place, gate, up, *refs):
    pieces, (gate_grad, up_grad, columns, natural) = refs[:nz], refs[nz:]
    step = pl.program_id(0)
    group, span = gate.shape
    rows = group // 4

    @pl.when(step == 0)
    def _():
        half = units // 2
        for k in range(nz):
            for r in range(2):
                start = (place[0] ^ k) * units + (place[1] ^ r) * half
                columns[pl.ds(pl.multiple_of(start, 16), half), :] = pieces[k][
                    r * half : (r + 1) * half, :
                ]

    ordered = columns[pl.ds(pl.multiple_of(step * span, 128), span), :].T
    for b in range(4):
        natural[pl.ds(token_start(place, b, rows), rows), :] = ordered[b * rows : (b + 1) * rows]
    dhidden = natural[...].astype(jnp.float32)
    value = gate[...].astype(jnp.float32)
    up_value = up[...].astype(jnp.float32)
    sigmoid_gate = jax.nn.sigmoid(value)
    gate_grad[...] = (
        dhidden * up_value * sigmoid_gate * (1.0 + value * (1.0 - sigmoid_gate))
    ).astype(jnp.bfloat16)
    up_grad[...] = (dhidden * (value * sigmoid_gate)).astype(jnp.bfloat16)


def matmul(lhs, rhs, lhs_dim=1, rhs_dim=0, dtype=jnp.float32):
    dims = (((lhs_dim,), (rhs_dim,)), ((), ()))
    return lax.dot_general(lhs, rhs, dims, preferred_element_type=jnp.float32).astype(dtype)


def paired_body(gate_pre, up_pre, down_codes, down_scales, cotangent):
    group_rows, local_hidden = gate_pre.shape
    owned, width = down_codes.shape
    rows = cotangent.shape[0]
    nz, units, nblocks = 4, 2 * owned, down_scales.shape[1]
    middle = 3 * nblocks // 5 * (width // nblocks)
    total_tokens = group_rows * nz * 2
    bf16, f32 = jnp.bfloat16, jnp.float32
    place = jnp.stack([lax.axis_index(name) for name in ("z", "x", "y", "c")]).astype(jnp.int32)
    struct = jax.ShapeDtypeStruct
    barrier = lax.optimization_barrier

    far, near = exchange(cotangent, "z", 2), exchange(cotangent, "z", 1)
    own_y, own_c = exchange(cotangent, "y", 1), exchange(cotangent, "c", 1)

    sides = ((owned, middle), (owned, width - middle))
    own_a, own_b = call_kernel(
        weight_kernel, place, (down_codes, down_scales),
        [whole(down_codes.shape), whole(down_scales.shape)],
        [struct(shape, bf16) for shape in sides], [whole(shape) for shape in sides], (1,), [],
        (2 * owned * width, 4 * owned * width, 0),
    )
    other_a = exchange(own_a, "x", 1)

    parts = tuple((k, 0, 2) for k in (0, 2, 3, 1))
    pieces = [struct((count * owned, group_rows), bf16) for _, _, count in parts]
    piece_specs = [whole(piece.shape) for piece in pieces]
    span = column_span(local_hidden)
    steps = local_hidden // span
    wide = pl.BlockSpec((group_rows, span), lambda i, place: (0, i))
    act_bytes = group_rows * local_hidden * 2
    act_scratch = [pltpu.VMEM((group_rows, span), bf16), pltpu.VMEM((local_hidden, group_rows), bf16)]
    sent = call_kernel(
        functools.partial(hidden_kernel, parts, units), place, (gate_pre, up_pre), [wide] * 2,
        pieces, piece_specs, (steps,), act_scratch,
        (4 * act_bytes, 3 * act_bytes, act_bytes // 2),
    )

    far, near, own_y, own_c, sent = barrier((far, near, own_y, own_c, sent))
    last = exchange(far, "z", 1)
    other_y = exchange(jnp.stack([far, near]), "y", 1)
    other_b = exchange(own_b, "x", 1)
    columns = [sent[0], exchange(sent[1], "z", 2)]
    first_c = exchange(jnp.stack([own_y, far, near]), "c", 1)
    last, other_y, columns, other_a, sent, first_c = barrier(
        (last, other_y, columns, other_a, sent, first_c)
    )

    last_y = exchange(last, "y", 1)
    columns += [exchange(sent[i], "z", parts[i][0]) for i in range(2, len(parts))]
    other_c = exchange(jnp.stack([other_y[0], other_y[1], last]), "c", 1)
    weight = call_kernel(
        join_kernel, place, (own_a, own_b, other_a, other_b),
        [whole(shape) for shape in sides] * 2,
        struct((units, width), bf16), whole((units, width)), (1,), [],
        (0, 4 * units * width, 0),
    )

    half_tokens = nz * group_rows // 2

    def gather_tokens(arrays, picks):
        return call_kernel(
            functools.partial(tokens_kernel, picks), place, arrays,
            [whole(array.shape) for array in arrays], struct((half_tokens, width), bf16),
            whole((half_tokens, width)), (1,), [], (0, 4 * half_tokens * width, 0),
        )

    even = gather_tokens(
        (cotangent, own_y, own_c, far, other_y, first_c, other_c),
        ((0, 0), (1, 0), (2, 0), (5, 0), (3, 0), (4, 0), (5, 1), (6, 0)),
    )
    far_back = matmul(weight, even[group_rows:], 1, 1, bf16)
    last_y, columns, far_back, even = barrier((last_y, columns, far_back, even))
    last_c = exchange(last_y, "c", 1)
    by_rows, by_lanes = (1, 3, 0, 2), (0, 2, 1, 3)
    keep, send, *by_units = call_kernel(
        functools.partial(columns_kernel, parts, by_rows, by_lanes), place, columns, piece_specs,
        [struct((half_tokens, units), bf16)] * 2 + [struct((owned, half_tokens), bf16)] * 4,
        [whole((half_tokens, units))] * 2 + [whole((owned, half_tokens))] * 4, (1,), [],
        (0, 12 * units * half_tokens, 0),
    )

    send, keep, last_c = barrier((send, keep, last_c))
    odd = gather_tokens(
        (near, last, last_y, other_y, first_c, other_c, last_c),
        ((0, 0), (3, 1), (4, 2), (5, 1), (1, 0), (2, 0), (5, 2), (6, 0)),
    )
    flat = [even, odd]

    factor = float(total_tokens) ** (-0.5)

    def grad_half(r):
        return (matmul(by_units[r], flat[0]) + matmul(by_units[2 + r], flat[1])) * factor

    def back_of(k):
        rows_of_k = flat[k % 2][k // 2 * group_rows : (k // 2 + 1) * group_rows]
        return matmul(weight, rows_of_k, 1, 1, bf16)

    given = matmul(send, weight, dtype=bf16)
    given, flat = barrier((given, flat))
    over_c = exchange(given, "c", 1)
    theirs = grad_half(1).astype(bf16)
    theirs, keep, flat = barrier((theirs, keep, flat))
    over_x = exchange(theirs, "x", 1)
    kept = matmul(keep, weight, dtype=bf16)
    back = [None, back_of(1), far_back, back_of(3)]
    back = [None] + [exchange(back[k], "z", k) for k in range(1, nz)]
    sums = (kept.astype(f32) + over_c.astype(f32)).reshape(2, nz, rows, width)
    odd_y = exchange(sums[1, :2].astype(bf16), "y", 1)
    even_y = exchange(sums[1, 2:].astype(bf16), "y", 1)
    odd_y, flat = barrier((odd_y, flat))
    back[0] = back_of(0)
    odd_sum = (sums[0, :2] + odd_y.astype(f32)).astype(bf16)
    odd_sum, back[2] = barrier((odd_sum, back[2]))
    even_y, _ = barrier((even_y, odd_sum))
    near_sum = exchange(odd_sum, "z", 1).astype(f32)
    even_sum = sums[0, 2:] + even_y.astype(f32)
    ours, across = even_sum[0] + near_sum[0], (even_sum[1] + near_sum[1]).astype(bf16)
    across, back[3] = barrier((across, back[3]))
    layer_out = (ours + exchange(across, "z", 2).astype(f32)).astype(bf16)

    back, _ = barrier((back, across))
    gate_grad, up_grad = call_kernel(
        functools.partial(grads_kernel, nz, units), place, (gate_pre, up_pre, *back),
        [wide] * 2 + [whole((units, group_rows))] * nz,
        [struct((group_rows, local_hidden), bf16)] * 2, [wide] * 2, (steps,), act_scratch[::-1],
        (12 * act_bytes, 5 * act_bytes, act_bytes // 2),
    )
    over_x, _ = barrier((over_x, gate_grad))
    weight_grad = grad_half(0) + over_x.astype(f32)
    return layer_out, gate_grad, up_grad, weight_grad


def column_span(width):
    return max((s for s in range(128, 641, 128) if width % s == 0), default=0)


def body(gate_pre, up_pre, down_codes, down_scales, cotangent):
    group_rows, local_hidden = gate_pre.shape
    owned, width = down_codes.shape
    nz, nx, ny, nc = (lax.axis_size(name) for name in ("z", "x", "y", "c"))
    rows = cotangent.shape[0]
    units = nx * owned
    total_tokens = group_rows * nz * nx

    gate_value = gate_pre.astype(jnp.float32)
    up_value = up_pre.astype(jnp.float32)
    sigmoid_gate = jax.nn.sigmoid(gate_value)
    activated = gate_value * sigmoid_gate
    hidden = (activated * up_value).astype(jnp.bfloat16)

    sent = hidden.T.reshape(nz, units, group_rows)
    columns = lax.all_to_all(sent, "z", 0, 0, tiled=True) if nz > 1 else sent

    line = lax.all_gather(cotangent, ("z", "y"), axis=0)
    both = gather_pair(line, "c")
    received = jnp.moveaxis(both, 0, 1).reshape(nz, group_rows, width)

    weight = gather_pair(dequantize(down_codes, down_scales), "x").reshape(units, width)

    partial_out = lax.dot_general(
        columns, weight, (((1,), (0,)), ((), ())), preferred_element_type=jnp.float32
    ).astype(jnp.bfloat16)
    partial_out = partial_out.reshape(nz, ny, nc, rows, width)
    over_c = scatter_sum(jnp.moveaxis(partial_out, 2, 0), "c")
    over_y = scatter_sum(jnp.moveaxis(over_c.astype(jnp.bfloat16), 1, 0), "y")
    layer_out = scatter_sum(over_y.astype(jnp.bfloat16), "z").astype(jnp.bfloat16)

    dcolumns = lax.dot_general(
        weight, received, (((1,), (2,)), ((), ())), preferred_element_type=jnp.float32
    ).astype(jnp.bfloat16)
    dcolumns = jnp.moveaxis(dcolumns, 1, 0)
    back = lax.all_to_all(dcolumns, "z", 0, 0, tiled=True) if nz > 1 else dcolumns
    dhidden = back.reshape(local_hidden, group_rows).T.astype(jnp.float32)
    gate_grad = (
        dhidden * up_value * sigmoid_gate * (1.0 + gate_value * (1.0 - sigmoid_gate))
    ).astype(jnp.bfloat16)
    up_grad = (dhidden * activated).astype(jnp.bfloat16)

    partial_grad = lax.dot_general(
        columns, received, (((0, 2), (0, 1)), ((), ())), preferred_element_type=jnp.float32
    )
    weight_grad = scatter_sum(partial_grad.reshape(nx, owned, width), "x") * float(total_tokens) ** (-0.5)
    return layer_out, gate_grad, up_grad, weight_grad


def outer_split(mesh, tokens, hidden, width):
    dp, tensor = mesh.shape["dp"], mesh.shape["tensor"]

    def rows_sent(nz):
        moved = 2 * (tokens // dp) * (hidden // tensor) / width if nz > 1 else 0
        return 2 * hidden // (tensor * nz) + 2 * tokens * nz // dp + moved

    return min((nz for nz in range(1, dp + 1) if dp % nz == 0), key=rows_sent)


def solution(mesh):
    def call(gate_pre, up_pre, down_codes, down_scales, cotangent):
        tokens, hidden = gate_pre.shape
        nz = outer_split(mesh, tokens, hidden, cotangent.shape[1])
        dp, tensor = mesh.shape["dp"], mesh.shape["tensor"]
        fine = Mesh(mesh.devices.reshape(nz, dp // nz, tensor // 2, 2), ("z", "x", "y", "c"))
        act = P(("z", "x"), ("y", "c"))
        weight = P(("y", "c", "z", "x"), None)
        layer = P(("z", "x", "y", "c"), None)
        owned = hidden // (dp * tensor)
        rows = tokens // (dp * tensor)
        pairs = fine.shape["x"] == 2 and fine.shape["y"] == 2 and nz == 4
        aligned = owned % 16 == 0 and rows % 16 == 0 and column_span(hidden // tensor)
        nblocks = down_scales.shape[1]
        blocks = nblocks > 2 and cotangent.shape[1] // nblocks % 128 == 0
        return jax.shard_map(
            paired_body if pairs and aligned and blocks else body,
            mesh=fine,
            in_specs=(act, act, weight, weight, layer),
            out_specs=(layer, act, act, weight),
            check_vma=False,
        )(gate_pre, up_pre, down_codes, down_scales, cotangent)

    return call
```

```python
import functools

import jax
import jax.numpy as jnp
from jax import lax
from jax.experimental import pallas as pl
from jax.experimental.pallas import tpu as pltpu
from jax.sharding import Mesh, PartitionSpec as P

VMEM_BYTES = 32 * 2**20


def dequantize(codes, scales):
    rows, width = codes.shape
    nblocks = scales.shape[1]
    blocks = codes.astype(jnp.float32).reshape(rows, nblocks, width // nblocks) * scales[:, :, None]
    return blocks.reshape(rows, width).astype(jnp.bfloat16)


def swap(value, axis):
    return lax.ppermute(value, axis, [(0, 1), (1, 0)])


def gather_pair(value, axis):
    if lax.axis_size(axis) != 2:
        return lax.all_gather(value, axis, axis=0)
    other = swap(value, axis)
    first = lax.axis_index(axis) == 0
    return jnp.stack([jnp.where(first, value, other), jnp.where(first, other, value)])


def scatter_sum(parts, axis):
    size = lax.axis_size(axis)
    if size == 1:
        return parts[0].astype(jnp.float32)
    if size != 2:
        received = lax.all_to_all(parts.astype(jnp.bfloat16), axis, 0, 0, tiled=True)
        return jnp.sum(received.astype(jnp.float32), axis=0)
    me = lax.axis_index(axis)
    theirs = lax.dynamic_index_in_dim(parts, 1 - me, 0, keepdims=False).astype(jnp.bfloat16)
    mine = lax.dynamic_index_in_dim(parts, me, 0, keepdims=False)
    return mine.astype(jnp.float32) + swap(theirs, axis).astype(jnp.float32)


def exchange(value, axis, offset):
    size = lax.axis_size(axis)
    return lax.ppermute(value, axis, [(i, i ^ offset) for i in range(size)])


def call_kernel(kernel, place, inputs, in_specs, out_shapes, out_specs, grid, scratch, cost):
    flops, nbytes, transcendentals = cost
    return pl.pallas_call(
        kernel,
        out_shape=out_shapes,
        grid_spec=pltpu.PrefetchScalarGridSpec(
            num_scalar_prefetch=1,
            grid=grid,
            in_specs=in_specs,
            out_specs=out_specs,
            scratch_shapes=scratch,
        ),
        compiler_params=pltpu.CompilerParams(vmem_limit_bytes=VMEM_BYTES),
        cost_estimate=pl.CostEstimate(
            flops=flops, bytes_accessed=nbytes, transcendentals=transcendentals
        ),
    )(place, *inputs)


def whole(shape):
    return pl.BlockSpec(shape, lambda i, place: (0,) * len(shape))


def token_start(place, block, rows):
    return pl.multiple_of(((place[2] ^ (block % 2)) * 2 + (place[3] ^ (block // 2))) * rows, 16)


def hidden_kernel(parts, units, place, gate, up, *refs):
    outs, (natural, columns) = refs[: len(parts)], refs[len(parts) :]
    step = pl.program_id(0)
    group, span = gate.shape
    rows = group // 4
    value = gate[...].astype(jnp.float32)
    hidden = value * jax.nn.sigmoid(value) * up[...].astype(jnp.float32)
    natural[...] = hidden.astype(jnp.bfloat16)
    ordered = [natural[pl.ds(token_start(place, b, rows), rows), :] for b in range(4)]
    columns[pl.ds(pl.multiple_of(step * span, 128), span), :] = jnp.concatenate(ordered, axis=0).T

    @pl.when(step == pl.num_programs(0) - 1)
    def _():
        half = units // 2
        for out, (k, first, count) in zip(outs, parts):
            for r in range(count):
                start = (place[0] ^ k) * units + (place[1] ^ (first + r)) * half
                out[r * half : (r + 1) * half, :] = columns[
                    pl.ds(pl.multiple_of(start, 16), half), :
                ]


def weight_kernel(place, codes, scales, *halves):
    span = codes.shape[1] // scales.shape[1]
    for block in range(scales.shape[1]):
        value = codes[:, block * span : (block + 1) * span].astype(jnp.float32)
        value = (value * scales[:, block : block + 1]).astype(jnp.bfloat16)
        at = block * span
        half, at = (0, at) if at < halves[0].shape[1] else (1, at - halves[0].shape[1])
        halves[half][:, at : at + span] = value


def join_kernel(place, own_a, own_b, other_a, other_b, weight):
    half, middle = own_a.shape
    weight[:half, :middle] = own_a[...]
    weight[:half, middle:] = own_b[...]
    weight[half:, :middle] = other_a[...]
    weight[half:, middle:] = other_b[...]


def tokens_kernel(picks, place, *refs):
    tokens = refs[-1]
    rows = refs[0].shape[-2]
    for at, (array, block) in enumerate(picks):
        source = refs[array]
        tokens[at * rows : (at + 1) * rows, :] = source[block] if len(source.shape) == 3 else source[...]


def columns_kernel(parts, by_rows, by_lanes, place, *refs):
    pieces, (keep, send, *rest) = refs[: len(parts)], refs[len(parts) :]
    half, group = rest[0].shape[0], pieces[0].shape[1]
    rows = group // 4
    for piece, (k, first, count) in zip(pieces, parts):
        turned = piece[...].T
        row, lane = by_rows.index(k), by_lanes.index(k)
        lanes = slice(lane % 2 * group, (lane % 2 + 1) * group)
        for b in range(4):
            target = send if b >= 2 else keep
            start = ((b % 2) * len(by_rows) + row) * rows
            target[start : start + rows, first * half : (first + count) * half] = turned[
                b * rows : (b + 1) * rows, :
            ]
        for r in range(count):
            rest[lane // 2 * 2 + first + r][:, lanes] = piece[r * half : (r + 1) * half, :]


def grads_kernel(nz, units, place, gate, up, *refs):
    pieces, (gate_grad, up_grad, columns, natural) = refs[:nz], refs[nz:]
    step = pl.program_id(0)
    group, span = gate.shape
    rows = group // 4

    @pl.when(step == 0)
    def _():
        half = units // 2
        for k in range(nz):
            for r in range(2):
                start = (place[0] ^ k) * units + (place[1] ^ r) * half
                columns[pl.ds(pl.multiple_of(start, 16), half), :] = pieces[k][
                    r * half : (r + 1) * half, :
                ]

    ordered = columns[pl.ds(pl.multiple_of(step * span, 128), span), :].T
    for b in range(4):
        natural[pl.ds(token_start(place, b, rows), rows), :] = ordered[b * rows : (b + 1) * rows]
    dhidden = natural[...].astype(jnp.float32)
    value = gate[...].astype(jnp.float32)
    up_value = up[...].astype(jnp.float32)
    sigmoid_gate = jax.nn.sigmoid(value)
    gate_grad[...] = (
        dhidden * up_value * sigmoid_gate * (1.0 + value * (1.0 - sigmoid_gate))
    ).astype(jnp.bfloat16)
    up_grad[...] = (dhidden * (value * sigmoid_gate)).astype(jnp.bfloat16)


def matmul(lhs, rhs, lhs_dim=1, rhs_dim=0, dtype=jnp.float32):
    dims = (((lhs_dim,), (rhs_dim,)), ((), ()))
    return lax.dot_general(lhs, rhs, dims, preferred_element_type=jnp.float32).astype(dtype)


def paired_body(gate_pre, up_pre, down_codes, down_scales, cotangent):
    group_rows, local_hidden = gate_pre.shape
    owned, width = down_codes.shape
    rows = cotangent.shape[0]
    nz, units, nblocks = 4, 2 * owned, down_scales.shape[1]
    middle = 3 * nblocks // 5 * (width // nblocks)
    total_tokens = group_rows * nz * 2
    bf16, f32 = jnp.bfloat16, jnp.float32
    place = jnp.stack([lax.axis_index(name) for name in ("z", "x", "y", "c")]).astype(jnp.int32)
    struct = jax.ShapeDtypeStruct
    barrier = lax.optimization_barrier

    far, near = exchange(cotangent, "z", 2), exchange(cotangent, "z", 1)
    own_y, own_c = exchange(cotangent, "y", 1), exchange(cotangent, "c", 1)

    sides = ((owned, middle), (owned, width - middle))
    own_a, own_b = call_kernel(
        weight_kernel, place, (down_codes, down_scales),
        [whole(down_codes.shape), whole(down_scales.shape)],
        [struct(shape, bf16) for shape in sides], [whole(shape) for shape in sides], (1,), [],
        (2 * owned * width, 4 * owned * width, 0),
    )
    other_a = exchange(own_a, "x", 1)

    parts = tuple((k, 0, 2) for k in (0, 2, 3, 1))
    pieces = [struct((count * owned, group_rows), bf16) for _, _, count in parts]
    piece_specs = [whole(piece.shape) for piece in pieces]
    span = column_span(local_hidden)
    steps = local_hidden // span
    wide = pl.BlockSpec((group_rows, span), lambda i, place: (0, i))
    act_bytes = group_rows * local_hidden * 2
    act_scratch = [pltpu.VMEM((group_rows, span), bf16), pltpu.VMEM((local_hidden, group_rows), bf16)]
    sent = call_kernel(
        functools.partial(hidden_kernel, parts, units), place, (gate_pre, up_pre), [wide] * 2,
        pieces, piece_specs, (steps,), act_scratch,
        (4 * act_bytes, 3 * act_bytes, act_bytes // 2),
    )

    far, near, own_y, own_c, sent = barrier((far, near, own_y, own_c, sent))
    last = exchange(far, "z", 1)
    other_y = exchange(jnp.stack([far, near]), "y", 1)
    other_b = exchange(own_b, "x", 1)
    columns = [sent[0], exchange(sent[1], "z", 2)]
    first_c = exchange(jnp.stack([own_y, far, near]), "c", 1)
    last, other_y, columns, other_a, sent, first_c = barrier(
        (last, other_y, columns, other_a, sent, first_c)
    )

    last_y = exchange(last, "y", 1)
    columns += [exchange(sent[i], "z", parts[i][0]) for i in range(2, len(parts))]
    other_c = exchange(jnp.stack([other_y[0], other_y[1], last]), "c", 1)
    weight = call_kernel(
        join_kernel, place, (own_a, own_b, other_a, other_b),
        [whole(shape) for shape in sides] * 2,
        struct((units, width), bf16), whole((units, width)), (1,), [],
        (0, 4 * units * width, 0),
    )

    half_tokens = nz * group_rows // 2

    def gather_tokens(arrays, picks):
        return call_kernel(
            functools.partial(tokens_kernel, picks), place, arrays,
            [whole(array.shape) for array in arrays], struct((half_tokens, width), bf16),
            whole((half_tokens, width)), (1,), [], (0, 4 * half_tokens * width, 0),
        )

    even = gather_tokens(
        (cotangent, own_y, own_c, far, other_y, first_c, other_c),
        ((0, 0), (1, 0), (2, 0), (5, 0), (3, 0), (4, 0), (5, 1), (6, 0)),
    )
    far_back = matmul(weight, even[group_rows:], 1, 1, bf16)
    last_y, columns, far_back, even = barrier((last_y, columns, far_back, even))
    last_c = exchange(last_y, "c", 1)

    by_rows, by_lanes = (1, 3, 0, 2), (0, 2, 1, 3)
    keep, send, *by_units = call_kernel(
        functools.partial(columns_kernel, parts, by_rows, by_lanes), place, columns, piece_specs,
        [struct((half_tokens, units), bf16)] * 2 + [struct((owned, half_tokens), bf16)] * 4,
        [whole((half_tokens, units))] * 2 + [whole((owned, half_tokens))] * 4, (1,), [],
        (0, 12 * units * half_tokens, 0),
    )

    odd = gather_tokens(
        (near, last, last_y, other_y, first_c, other_c, last_c),
        ((0, 0), (3, 1), (4, 2), (5, 1), (1, 0), (2, 0), (5, 2), (6, 0)),
    )
    even, odd, send, keep = barrier((even, odd, send, keep))
    flat = [even, odd]

    factor = float(total_tokens) ** (-0.5)


    def grad_half(r):
        return (matmul(by_units[r], flat[0]) + matmul(by_units[2 + r], flat[1])) * factor

    def back_of(k):
        rows_of_k = flat[k % 2][k // 2 * group_rows : (k // 2 + 1) * group_rows]
        return matmul(weight, rows_of_k, 1, 1, bf16)

    over_c = exchange(matmul(send, weight, dtype=bf16), "c", 1)
    theirs = grad_half(1).astype(bf16)
    theirs, keep, flat = barrier((theirs, keep, flat))
    over_x = exchange(theirs, "x", 1)
    kept = matmul(keep, weight, dtype=bf16)
    back = [back_of(0), back_of(1), far_back, back_of(3)]
    back = [back[0]] + [exchange(back[k], "z", k) for k in range(1, nz)]
    sums = (kept.astype(f32) + over_c.astype(f32)).reshape(2, nz, rows, width)
    odd_y = exchange(sums[1, :2].astype(bf16), "y", 1)
    even_y = exchange(sums[1, 2:].astype(bf16), "y", 1)
    odd_sum = (sums[0, :2] + odd_y.astype(f32)).astype(bf16)
    odd_sum, back[2] = barrier((odd_sum, back[2]))
    even_y, _ = barrier((even_y, odd_sum))
    near_sum = exchange(odd_sum, "z", 1).astype(f32)
    even_sum = sums[0, 2:] + even_y.astype(f32)
    ours, across = even_sum[0] + near_sum[0], (even_sum[1] + near_sum[1]).astype(bf16)
    across, back[3] = barrier((across, back[3]))
    layer_out = (ours + exchange(across, "z", 2).astype(f32)).astype(bf16)

    back, _ = barrier((back, across))
    gate_grad, up_grad = call_kernel(
        functools.partial(grads_kernel, nz, units), place, (gate_pre, up_pre, *back),
        [wide] * 2 + [whole((units, group_rows))] * nz,
        [struct((group_rows, local_hidden), bf16)] * 2, [wide] * 2, (steps,), act_scratch[::-1],
        (12 * act_bytes, 5 * act_bytes, act_bytes // 2),
    )
    over_x, _ = barrier((over_x, gate_grad))
    weight_grad = grad_half(0) + over_x.astype(f32)
    return layer_out, gate_grad, up_grad, weight_grad


def column_span(width):
    return max((s for s in range(128, 641, 128) if width % s == 0), default=0)


def body(gate_pre, up_pre, down_codes, down_scales, cotangent):
    group_rows, local_hidden = gate_pre.shape
    owned, width = down_codes.shape
    nz, nx, ny, nc = (lax.axis_size(name) for name in ("z", "x", "y", "c"))
    rows = cotangent.shape[0]
    units = nx * owned
    total_tokens = group_rows * nz * nx

    gate_value = gate_pre.astype(jnp.float32)
    up_value = up_pre.astype(jnp.float32)
    sigmoid_gate = jax.nn.sigmoid(gate_value)
    activated = gate_value * sigmoid_gate
    hidden = (activated * up_value).astype(jnp.bfloat16)

    sent = hidden.T.reshape(nz, units, group_rows)
    columns = lax.all_to_all(sent, "z", 0, 0, tiled=True) if nz > 1 else sent

    line = lax.all_gather(cotangent, ("z", "y"), axis=0)
    both = gather_pair(line, "c")
    received = jnp.moveaxis(both, 0, 1).reshape(nz, group_rows, width)

    weight = gather_pair(dequantize(down_codes, down_scales), "x").reshape(units, width)

    partial_out = lax.dot_general(
        columns, weight, (((1,), (0,)), ((), ())), preferred_element_type=jnp.float32
    ).astype(jnp.bfloat16)
    partial_out = partial_out.reshape(nz, ny, nc, rows, width)
    over_c = scatter_sum(jnp.moveaxis(partial_out, 2, 0), "c")
    over_y = scatter_sum(jnp.moveaxis(over_c.astype(jnp.bfloat16), 1, 0), "y")
    layer_out = scatter_sum(over_y.astype(jnp.bfloat16), "z").astype(jnp.bfloat16)

    dcolumns = lax.dot_general(
        weight, received, (((1,), (2,)), ((), ())), preferred_element_type=jnp.float32
    ).astype(jnp.bfloat16)
    dcolumns = jnp.moveaxis(dcolumns, 1, 0)
    back = lax.all_to_all(dcolumns, "z", 0, 0, tiled=True) if nz > 1 else dcolumns
    dhidden = back.reshape(local_hidden, group_rows).T.astype(jnp.float32)
    gate_grad = (
        dhidden * up_value * sigmoid_gate * (1.0 + gate_value * (1.0 - sigmoid_gate))
    ).astype(jnp.bfloat16)
    up_grad = (dhidden * activated).astype(jnp.bfloat16)

    partial_grad = lax.dot_general(
        columns, received, (((0, 2), (0, 1)), ((), ())), preferred_element_type=jnp.float32
    )
    weight_grad = scatter_sum(partial_grad.reshape(nx, owned, width), "x") * float(total_tokens) ** (-0.5)
    return layer_out, gate_grad, up_grad, weight_grad


def outer_split(mesh, tokens, hidden, width):
    dp, tensor = mesh.shape["dp"], mesh.shape["tensor"]

    def rows_sent(nz):
        moved = 2 * (tokens // dp) * (hidden // tensor) / width if nz > 1 else 0
        return 2 * hidden // (tensor * nz) + 2 * tokens * nz // dp + moved

    return min((nz for nz in range(1, dp + 1) if dp % nz == 0), key=rows_sent)


def solution(mesh):
    def call(gate_pre, up_pre, down_codes, down_scales, cotangent):
        tokens, hidden = gate_pre.shape
        nz = outer_split(mesh, tokens, hidden, cotangent.shape[1])
        dp, tensor = mesh.shape["dp"], mesh.shape["tensor"]
        fine = Mesh(mesh.devices.reshape(nz, dp // nz, tensor // 2, 2), ("z", "x", "y", "c"))
        act = P(("z", "x"), ("y", "c"))
        weight = P(("y", "c", "z", "x"), None)
        layer = P(("z", "x", "y", "c"), None)
        owned = hidden // (dp * tensor)
        rows = tokens // (dp * tensor)
        pairs = fine.shape["x"] == 2 and fine.shape["y"] == 2 and nz == 4
        aligned = owned % 16 == 0 and rows % 16 == 0 and column_span(hidden // tensor)
        nblocks = down_scales.shape[1]
        blocks = nblocks > 2 and cotangent.shape[1] // nblocks % 128 == 0
        return jax.shard_map(
            paired_body if pairs and aligned and blocks else body,
            mesh=fine,
            in_specs=(act, act, weight, weight, layer),
            out_specs=(layer, act, act, weight),
            check_vma=False,
        )(gate_pre, up_pre, down_codes, down_scales, cotangent)

    return call
```

```python
import functools

import jax
import jax.numpy as jnp
from jax import lax
from jax.experimental import pallas as pl
from jax.experimental.pallas import tpu as pltpu
from jax.sharding import Mesh, PartitionSpec as P

VMEM_BYTES = 32 * 2**20


def dequantize(codes, scales):
    rows, width = codes.shape
    nblocks = scales.shape[1]
    blocks = codes.astype(jnp.float32).reshape(rows, nblocks, width // nblocks) * scales[:, :, None]
    return blocks.reshape(rows, width).astype(jnp.bfloat16)


def swap(value, axis):
    return lax.ppermute(value, axis, [(0, 1), (1, 0)])


def gather_pair(value, axis):
    if lax.axis_size(axis) != 2:
        return lax.all_gather(value, axis, axis=0)
    other = swap(value, axis)
    first = lax.axis_index(axis) == 0
    return jnp.stack([jnp.where(first, value, other), jnp.where(first, other, value)])


def scatter_sum(parts, axis):
    size = lax.axis_size(axis)
    if size == 1:
        return parts[0].astype(jnp.float32)
    if size != 2:
        received = lax.all_to_all(parts.astype(jnp.bfloat16), axis, 0, 0, tiled=True)
        return jnp.sum(received.astype(jnp.float32), axis=0)
    me = lax.axis_index(axis)
    theirs = lax.dynamic_index_in_dim(parts, 1 - me, 0, keepdims=False).astype(jnp.bfloat16)
    mine = lax.dynamic_index_in_dim(parts, me, 0, keepdims=False)
    return mine.astype(jnp.float32) + swap(theirs, axis).astype(jnp.float32)


def exchange(value, axis, offset):
    size = lax.axis_size(axis)
    return lax.ppermute(value, axis, [(i, i ^ offset) for i in range(size)])


def call_kernel(kernel, place, inputs, in_specs, out_shapes, out_specs, grid, scratch, cost):
    flops, nbytes, transcendentals = cost
    return pl.pallas_call(
        kernel,
        out_shape=out_shapes,
        grid_spec=pltpu.PrefetchScalarGridSpec(
            num_scalar_prefetch=1,
            grid=grid,
            in_specs=in_specs,
            out_specs=out_specs,
            scratch_shapes=scratch,
        ),
        compiler_params=pltpu.CompilerParams(vmem_limit_bytes=VMEM_BYTES),
        cost_estimate=pl.CostEstimate(
            flops=flops, bytes_accessed=nbytes, transcendentals=transcendentals
        ),
    )(place, *inputs)


def whole(shape):
    return pl.BlockSpec(shape, lambda i, place: (0,) * len(shape))


def token_start(place, block, rows):
    return pl.multiple_of(((place[2] ^ (block % 2)) * 2 + (place[3] ^ (block // 2))) * rows, 16)


def hidden_kernel(parts, units, place, gate, up, *refs):
    outs, (natural, columns) = refs[: len(parts)], refs[len(parts) :]
    step = pl.program_id(0)
    group, span = gate.shape
    rows = group // 4
    value = gate[...].astype(jnp.float32)
    hidden = value * jax.nn.sigmoid(value) * up[...].astype(jnp.float32)
    natural[...] = hidden.astype(jnp.bfloat16)
    ordered = [natural[pl.ds(token_start(place, b, rows), rows), :] for b in range(4)]
    columns[pl.ds(pl.multiple_of(step * span, 128), span), :] = jnp.concatenate(ordered, axis=0).T

    @pl.when(step == pl.num_programs(0) - 1)
    def _():
        half = units // 2
        for out, (k, first, count) in zip(outs, parts):
            for r in range(count):
                start = (place[0] ^ k) * units + (place[1] ^ (first + r)) * half
                out[r * half : (r + 1) * half, :] = columns[
                    pl.ds(pl.multiple_of(start, 16), half), :
                ]


def weight_kernel(place, codes, scales, *halves):
    span = codes.shape[1] // scales.shape[1]
    for block in range(scales.shape[1]):
        value = codes[:, block * span : (block + 1) * span].astype(jnp.float32)
        value = (value * scales[:, block : block + 1]).astype(jnp.bfloat16)
        at = block * span
        half, at = (0, at) if at < halves[0].shape[1] else (1, at - halves[0].shape[1])
        halves[half][:, at : at + span] = value


def join_kernel(place, own_a, own_b, other_a, other_b, weight):
    half, middle = own_a.shape
    weight[:half, :middle] = own_a[...]
    weight[:half, middle:] = own_b[...]
    weight[half:, :middle] = other_a[...]
    weight[half:, middle:] = other_b[...]


def tokens_kernel(picks, place, *refs):
    tokens = refs[-1]
    rows = refs[0].shape[-2]
    for at, (array, block) in enumerate(picks):
        source = refs[array]
        tokens[at * rows : (at + 1) * rows, :] = source[block] if len(source.shape) == 3 else source[...]


def columns_kernel(parts, by_rows, by_lanes, place, *refs):
    pieces, (keep, send, *rest) = refs[: len(parts)], refs[len(parts) :]
    half, group = rest[0].shape[0], pieces[0].shape[1]
    rows = group // 4
    for piece, (k, first, count) in zip(pieces, parts):
        turned = piece[...].T
        row, lane = by_rows.index(k), by_lanes.index(k)
        lanes = slice(lane % 2 * group, (lane % 2 + 1) * group)
        for b in range(4):
            target = send if b >= 2 else keep
            start = ((b % 2) * len(by_rows) + row) * rows
            target[start : start + rows, first * half : (first + count) * half] = turned[
                b * rows : (b + 1) * rows, :
            ]
        for r in range(count):
            rest[lane // 2 * 2 + first + r][:, lanes] = piece[r * half : (r + 1) * half, :]


def grads_kernel(nz, units, place, gate, up, *refs):
    pieces, (gate_grad, up_grad, columns, natural) = refs[:nz], refs[nz:]
    step = pl.program_id(0)
    group, span = gate.shape
    rows = group // 4

    @pl.when(step == 0)
    def _():
        half = units // 2
        for k in range(nz):
            for r in range(2):
                start = (place[0] ^ k) * units + (place[1] ^ r) * half
                columns[pl.ds(pl.multiple_of(start, 16), half), :] = pieces[k][
                    r * half : (r + 1) * half, :
                ]

    ordered = columns[pl.ds(pl.multiple_of(step * span, 128), span), :].T
    for b in range(4):
        natural[pl.ds(token_start(place, b, rows), rows), :] = ordered[b * rows : (b + 1) * rows]
    dhidden = natural[...].astype(jnp.float32)
    value = gate[...].astype(jnp.float32)
    up_value = up[...].astype(jnp.float32)
    sigmoid_gate = jax.nn.sigmoid(value)
    gate_grad[...] = (
        dhidden * up_value * sigmoid_gate * (1.0 + value * (1.0 - sigmoid_gate))
    ).astype(jnp.bfloat16)
    up_grad[...] = (dhidden * (value * sigmoid_gate)).astype(jnp.bfloat16)


def matmul(lhs, rhs, lhs_dim=1, rhs_dim=0, dtype=jnp.float32):
    dims = (((lhs_dim,), (rhs_dim,)), ((), ()))
    return lax.dot_general(lhs, rhs, dims, preferred_element_type=jnp.float32).astype(dtype)


def paired_body(gate_pre, up_pre, down_codes, down_scales, cotangent):
    group_rows, local_hidden = gate_pre.shape
    owned, width = down_codes.shape
    rows = cotangent.shape[0]
    nz, units, nblocks = 4, 2 * owned, down_scales.shape[1]
    middle = 3 * nblocks // 5 * (width // nblocks)
    total_tokens = group_rows * nz * 2
    bf16, f32 = jnp.bfloat16, jnp.float32
    place = jnp.stack([lax.axis_index(name) for name in ("z", "x", "y", "c")]).astype(jnp.int32)
    struct = jax.ShapeDtypeStruct
    barrier = lax.optimization_barrier

    far, near = exchange(cotangent, "z", 2), exchange(cotangent, "z", 1)
    own_y, own_c = exchange(cotangent, "y", 1), exchange(cotangent, "c", 1)

    sides = ((owned, middle), (owned, width - middle))
    own_a, own_b = call_kernel(
        weight_kernel, place, (down_codes, down_scales),
        [whole(down_codes.shape), whole(down_scales.shape)],
        [struct(shape, bf16) for shape in sides], [whole(shape) for shape in sides], (1,), [],
        (2 * owned * width, 4 * owned * width, 0),
    )
    other_a = exchange(own_a, "x", 1)

    parts = tuple((k, 0, 2) for k in (0, 2, 3, 1))
    pieces = [struct((count * owned, group_rows), bf16) for _, _, count in parts]
    piece_specs = [whole(piece.shape) for piece in pieces]
    span = column_span(local_hidden)
    steps = local_hidden // span
    wide = pl.BlockSpec((group_rows, span), lambda i, place: (0, i))
    act_bytes = group_rows * local_hidden * 2
    act_scratch = [pltpu.VMEM((group_rows, span), bf16), pltpu.VMEM((local_hidden, group_rows), bf16)]
    sent = call_kernel(
        functools.partial(hidden_kernel, parts, units), place, (gate_pre, up_pre), [wide] * 2,
        pieces, piece_specs, (steps,), act_scratch,
        (4 * act_bytes, 3 * act_bytes, act_bytes // 2),
    )

    far, near, own_y, own_c, sent = barrier((far, near, own_y, own_c, sent))
    last = exchange(far, "z", 1)
    other_y = exchange(jnp.stack([far, near]), "y", 1)
    other_b = exchange(own_b, "x", 1)
    columns = [sent[0], exchange(sent[1], "z", 2)]
    first_c = exchange(jnp.stack([own_y, far, near]), "c", 1)
    last, other_y, columns, other_a, sent, first_c = barrier(
        (last, other_y, columns, other_a, sent, first_c)
    )

    last_y = exchange(last, "y", 1)
    columns += [exchange(sent[i], "z", parts[i][0]) for i in range(2, len(parts))]
    other_c = exchange(jnp.stack([other_y[0], other_y[1], last]), "c", 1)
    weight = call_kernel(
        join_kernel, place, (own_a, own_b, other_a, other_b),
        [whole(shape) for shape in sides] * 2,
        struct((units, width), bf16), whole((units, width)), (1,), [],
        (0, 4 * units * width, 0),
    )

    half_tokens = nz * group_rows // 2

    def gather_tokens(arrays, picks):
        return call_kernel(
            functools.partial(tokens_kernel, picks), place, arrays,
            [whole(array.shape) for array in arrays], struct((half_tokens, width), bf16),
            whole((half_tokens, width)), (1,), [], (0, 4 * half_tokens * width, 0),
        )

    even = gather_tokens(
        (cotangent, own_y, own_c, far, other_y, first_c, other_c),
        ((0, 0), (1, 0), (2, 0), (5, 0), (3, 0), (4, 0), (5, 1), (6, 0)),
    )
    far_back = matmul(weight, even[group_rows:], 1, 1, bf16)
    last_y, columns, far_back, even = barrier((last_y, columns, far_back, even))
    last_c = exchange(last_y, "c", 1)

    by_rows, by_lanes = (1, 3, 0, 2), (0, 2, 1, 3)
    keep, send, *by_units = call_kernel(
        functools.partial(columns_kernel, parts, by_rows, by_lanes), place, columns, piece_specs,
        [struct((half_tokens, units), bf16)] * 2 + [struct((owned, half_tokens), bf16)] * 4,
        [whole((half_tokens, units))] * 2 + [whole((owned, half_tokens))] * 4, (1,), [],
        (0, 12 * units * half_tokens, 0),
    )

    odd = gather_tokens(
        (near, last, last_y, other_y, first_c, other_c, last_c),
        ((0, 0), (3, 1), (4, 2), (5, 1), (1, 0), (2, 0), (5, 2), (6, 0)),
    )
    even, odd, send, keep = barrier((even, odd, send, keep))
    flat = [even, odd]

    factor = float(total_tokens) ** (-0.5)


    def grad_half(r):
        return (matmul(by_units[r], flat[0]) + matmul(by_units[2 + r], flat[1])) * factor

    def back_of(k):
        rows_of_k = flat[k % 2][k // 2 * group_rows : (k // 2 + 1) * group_rows]
        return matmul(weight, rows_of_k, 1, 1, bf16)

    over_c = exchange(matmul(send, weight, dtype=bf16), "c", 1)
    theirs = grad_half(1).astype(bf16)
    theirs, keep, flat = barrier((theirs, keep, flat))
    over_x = exchange(theirs, "x", 1)
    kept = matmul(keep, weight, dtype=bf16)
    back = [back_of(0), back_of(1), far_back, back_of(3)]
    back = [back[0]] + [exchange(back[k], "z", k) for k in range(1, nz)]
    sums = (kept.astype(f32) + over_c.astype(f32)).reshape(2, nz, rows, width)
    odd_y = exchange(sums[1, :2].astype(bf16), "y", 1)
    even_y = exchange(sums[1, 2:].astype(bf16), "y", 1)
    odd_y, flat = barrier((odd_y, flat))
    odd_sum = (sums[0, :2] + odd_y.astype(f32)).astype(bf16)
    odd_sum, back[2] = barrier((odd_sum, back[2]))
    even_y, _ = barrier((even_y, odd_sum))
    near_sum = exchange(odd_sum, "z", 1).astype(f32)
    even_sum = sums[0, 2:] + even_y.astype(f32)
    ours, across = even_sum[0] + near_sum[0], (even_sum[1] + near_sum[1]).astype(bf16)
    across, back[3] = barrier((across, back[3]))
    layer_out = (ours + exchange(across, "z", 2).astype(f32)).astype(bf16)

    back, _ = barrier((back, across))
    gate_grad, up_grad = call_kernel(
        functools.partial(grads_kernel, nz, units), place, (gate_pre, up_pre, *back),
        [wide] * 2 + [whole((units, group_rows))] * nz,
        [struct((group_rows, local_hidden), bf16)] * 2, [wide] * 2, (steps,), act_scratch[::-1],
        (12 * act_bytes, 5 * act_bytes, act_bytes // 2),
    )
    over_x, _ = barrier((over_x, gate_grad))
    weight_grad = grad_half(0) + over_x.astype(f32)
    return layer_out, gate_grad, up_grad, weight_grad


def column_span(width):
    return max((s for s in range(128, 641, 128) if width % s == 0), default=0)


def body(gate_pre, up_pre, down_codes, down_scales, cotangent):
    group_rows, local_hidden = gate_pre.shape
    owned, width = down_codes.shape
    nz, nx, ny, nc = (lax.axis_size(name) for name in ("z", "x", "y", "c"))
    rows = cotangent.shape[0]
    units = nx * owned
    total_tokens = group_rows * nz * nx

    gate_value = gate_pre.astype(jnp.float32)
    up_value = up_pre.astype(jnp.float32)
    sigmoid_gate = jax.nn.sigmoid(gate_value)
    activated = gate_value * sigmoid_gate
    hidden = (activated * up_value).astype(jnp.bfloat16)

    sent = hidden.T.reshape(nz, units, group_rows)
    columns = lax.all_to_all(sent, "z", 0, 0, tiled=True) if nz > 1 else sent

    line = lax.all_gather(cotangent, ("z", "y"), axis=0)
    both = gather_pair(line, "c")
    received = jnp.moveaxis(both, 0, 1).reshape(nz, group_rows, width)

    weight = gather_pair(dequantize(down_codes, down_scales), "x").reshape(units, width)

    partial_out = lax.dot_general(
        columns, weight, (((1,), (0,)), ((), ())), preferred_element_type=jnp.float32
    ).astype(jnp.bfloat16)
    partial_out = partial_out.reshape(nz, ny, nc, rows, width)
    over_c = scatter_sum(jnp.moveaxis(partial_out, 2, 0), "c")
    over_y = scatter_sum(jnp.moveaxis(over_c.astype(jnp.bfloat16), 1, 0), "y")
    layer_out = scatter_sum(over_y.astype(jnp.bfloat16), "z").astype(jnp.bfloat16)

    dcolumns = lax.dot_general(
        weight, received, (((1,), (2,)), ((), ())), preferred_element_type=jnp.float32
    ).astype(jnp.bfloat16)
    dcolumns = jnp.moveaxis(dcolumns, 1, 0)
    back = lax.all_to_all(dcolumns, "z", 0, 0, tiled=True) if nz > 1 else dcolumns
    dhidden = back.reshape(local_hidden, group_rows).T.astype(jnp.float32)
    gate_grad = (
        dhidden * up_value * sigmoid_gate * (1.0 + gate_value * (1.0 - sigmoid_gate))
    ).astype(jnp.bfloat16)
    up_grad = (dhidden * activated).astype(jnp.bfloat16)

    partial_grad = lax.dot_general(
        columns, received, (((0, 2), (0, 1)), ((), ())), preferred_element_type=jnp.float32
    )
    weight_grad = scatter_sum(partial_grad.reshape(nx, owned, width), "x") * float(total_tokens) ** (-0.5)
    return layer_out, gate_grad, up_grad, weight_grad


def outer_split(mesh, tokens, hidden, width):
    dp, tensor = mesh.shape["dp"], mesh.shape["tensor"]

    def rows_sent(nz):
        moved = 2 * (tokens // dp) * (hidden // tensor) / width if nz > 1 else 0
        return 2 * hidden // (tensor * nz) + 2 * tokens * nz // dp + moved

    return min((nz for nz in range(1, dp + 1) if dp % nz == 0), key=rows_sent)


def solution(mesh):
    def call(gate_pre, up_pre, down_codes, down_scales, cotangent):
        tokens, hidden = gate_pre.shape
        nz = outer_split(mesh, tokens, hidden, cotangent.shape[1])
        dp, tensor = mesh.shape["dp"], mesh.shape["tensor"]
        fine = Mesh(mesh.devices.reshape(nz, dp // nz, tensor // 2, 2), ("z", "x", "y", "c"))
        act = P(("z", "x"), ("y", "c"))
        weight = P(("y", "c", "z", "x"), None)
        layer = P(("z", "x", "y", "c"), None)
        owned = hidden // (dp * tensor)
        rows = tokens // (dp * tensor)
        pairs = fine.shape["x"] == 2 and fine.shape["y"] == 2 and nz == 4
        aligned = owned % 16 == 0 and rows % 16 == 0 and column_span(hidden // tensor)
        nblocks = down_scales.shape[1]
        blocks = nblocks > 2 and cotangent.shape[1] // nblocks % 128 == 0
        return jax.shard_map(
            paired_body if pairs and aligned and blocks else body,
            mesh=fine,
            in_specs=(act, act, weight, weight, layer),
            out_specs=(layer, act, act, weight),
            check_vma=False,
        )(gate_pre, up_pre, down_codes, down_scales, cotangent)

    return call
```
